32 devices in a mesh: batch: 4 (over x, core), seq: 8 (over z, y).
Axes of the slice: x: 2, y: 2, z: 4, core: 2. Of those that a mesh axis runs over, the one named last changes fastest.
Arguments:
- tokens: bfloat16 [16, 2048, 1024], P('batch', 'seq'), may hold values from -6 to 6
- segments: int32 [16, 2048], P('batch', 'seq'), may hold values from 0 to 40, as said below
- cotangent: bfloat16 [16, 2048, 1024], P('batch', 'seq'), may hold values from -6 to 6
- first_gain: bfloat16 [1024], P(('batch', 'seq')), may hold values from 0.5 to 1.5
- query_weight: bfloat16 [1024, 1024], P(('batch', 'seq')), may hold values from -0.1875 to 0.1875
- key_weight: bfloat16 [1024, 128], P(('batch', 'seq')), may hold values from -0.1875 to 0.1875
- value_weight: bfloat16 [1024, 128], P(('batch', 'seq')), may hold values from -0.1875 to 0.1875
- out_weight: bfloat16 [1024, 1024], P(None, ('batch', 'seq')), may hold values from -1 to 1
- second_gain: bfloat16 [1024], P(('batch', 'seq')), may hold values from 0.5 to 1.5
- gate_weight: bfloat16 [1024, 3072], P(('batch', 'seq')), may hold values from -0.1875 to 0.1875
- up_weight: bfloat16 [1024, 3072], P(('batch', 'seq')), may hold values from -0.1875 to 0.1875
- down_weight: bfloat16 [3072, 1024], P(None, ('batch', 'seq')), may hold values from -0.109375 to 0.109375
Outputs:
- output: bfloat16 [16, 2048, 1024], P('batch', 'seq')
- grad_input: bfloat16 [16, 2048, 1024], P('batch', 'seq')
- grad_first_gain: float32 [1024], P(('batch', 'seq'))
- grad_query_weight: float32 [1024, 1024], P(('batch', 'seq'))
- grad_key_weight: float32 [1024, 128], P(('batch', 'seq'))
- grad_value_weight: float32 [1024, 128], P(('batch', 'seq'))
- grad_out_weight: float32 [1024, 1024], P(None, ('batch', 'seq'))
- grad_second_gain: float32 [1024], P(('batch', 'seq'))
- grad_gate_weight: float32 [1024, 3072], P(('batch', 'seq'))
- grad_up_weight: float32 [1024, 3072], P(('batch', 'seq'))
- grad_down_weight: float32 [3072, 1024], P(None, ('batch', 'seq'))
The draws below stay inside these ranges and needn't reach their ends.
Inputs may be any that keep to these rules, and one draw needn't show every extreme that they name: `segments`: each row is 0 at its first position and rises by 0 or 1 from one position to the next; among the 4 rows of each index of batch, one row is 0 throughout, and some other row reaches the largest value.
All inputs are finite; a program needn't handle non-finite values.
Results may differ from the reference program's by a relative error of at most 0.014.
Values may be sent and summed in bfloat16 or wider, within the bound.
A program may use at most 256 MiB of HBM per device.

```python
import jax
import jax.numpy as jnp
from jax import lax

D = 1024
HEADS = 8
HEAD_DIM = 128
FF = 3072
WINDOW = 1024
BLOCK = 256
SEQS = 4
LENGTH = 2048
SEQUENCES = 16


def draw_segments(key, part):
    key_level = jax.random.fold_in(key, 11)
    key_bits = jax.random.fold_in(key, 23)
    key_pick = jax.random.fold_in(key, 37)
    top_value = LENGTH // 64 + LENGTH // BLOCK
    level = jax.random.randint(key_level, (SEQUENCES, LENGTH // 64, 1), 3, 12)
    noise_bits = jax.random.randint(key_bits, (SEQUENCES, LENGTH // 64, 64), 0, 4096)
    marks = noise_bits % jnp.left_shift(1, level) == 0
    marks = marks.reshape(SEQUENCES, LENGTH)
    places = jnp.arange(LENGTH)
    marks = marks & (places > 0)[None, :]
    chosen = jax.random.randint(key_pick, (SEQUENCES // SEQS,), 0, SEQS)
    local_row = jnp.arange(SEQUENCES) % SEQS
    single = local_row == jnp.repeat(chosen, SEQS)
    busiest = local_row == jnp.repeat((chosen + 1) % SEQS, SEQS)
    forced = (places % 64 == 3) | (places % BLOCK == BLOCK // 2 + 1)
    marks = jnp.where(busiest[:, None], forced[None, :], marks & jnp.logical_not(single)[:, None])
    counted = jnp.cumsum(marks.astype(jnp.int32), axis=1)
    return jnp.minimum(counted, top_value).astype(jnp.int32)


def with_spikes(entries, own_key, source, target, shards_of, factor):
    owner, partner = [(jnp.arange(entries.shape[axis_at]) // (entries.shape[axis_at] // shards_of)).reshape([-1 if axis == axis_at else 1 for axis in range(entries.ndim)]) for axis_at in (source, target)]
    chosen = jax.random.permutation(own_key, shards_of)[partner]
    strong = (owner == chosen) | (owner == (partner + shards_of // 2) % shards_of)
    return jnp.where(strong, factor * entries, entries)


def shard_levels(rng, extent, shards, smallest, high):
    loudness, own = 1.0, jax.random.fold_in(rng, 6)
    for position, parts in shards:
        steps = jnp.exp(jax.random.uniform(jax.random.fold_in(own, position), (parts,), jnp.float32, smallest / len(shards), high / len(shards)))
        loudness = loudness * jnp.repeat(steps, extent[position] // parts).reshape([-1 if axis == position else 1 for axis in range(len(extent))])
    return loudness


def bell_draw(stream_key, extent, width, bound, shards=(), held_as=jnp.bfloat16):
    entries = jax.random.normal(stream_key, extent, jnp.float32) * width
    if len(shards) > 0:
        entries = shard_levels(stream_key, extent, shards, -0.22, 0.18) * entries
    return jnp.clip(entries, min=-bound, max=bound).astype(held_as)


def bell_draw_with(own_key, extent, spread, limit, pieces, heavy, held_as=jnp.bfloat16):
    values = spread * jax.random.normal(own_key, extent, jnp.float32)
    if pieces:
        values = values * shard_levels(own_key, extent, pieces, -0.22, 0.18)
    return jnp.clip(with_spikes(values, jax.random.fold_in(own_key, 3), *heavy), -limit, limit).astype(held_as)


def setup_inputs(seed: int = 0) -> dict:
    streams_of = jax.random.split(jax.random.key(seed), 13)
    tokens = bell_draw(streams_of[0], (SEQUENCES, LENGTH, D), 1.0, 6.0, ((0, 4), (1, 8)))
    segments = draw_segments(jax.random.fold_in(streams_of[12], 71), 0)
    cotangent = bell_draw_with(streams_of[2], (SEQUENCES, LENGTH, D), 1.0, 6.0, ((0, 4), (1, 8)), (1, 2, 8, 2.0))
    first_gain = jnp.clip(1.0 + 0.1 * jax.random.normal(streams_of[3], (D,), jnp.float32), 0.5, 1.5).astype(jnp.bfloat16)
    query_weight = bell_draw(streams_of[4], (D, HEADS * HEAD_DIM), D ** -0.5, 0.1875, ((0, 32),))
    key_weight = bell_draw(streams_of[5], (D, HEAD_DIM), D ** -0.5, 0.1875, ((0, 32),))
    value_weight = bell_draw(streams_of[6], (D, HEAD_DIM), D ** -0.5, 0.1875, ((0, 32),))
    out_weight = bell_draw(streams_of[7], (HEADS * HEAD_DIM, D), (HEADS * HEAD_DIM // 32) ** -0.5, 1.0, ((1, 32),))
    second_gain = jnp.clip(1.0 + 0.1 * jax.random.normal(streams_of[8], (D,), jnp.float32), 0.5, 1.5).astype(jnp.bfloat16)
    gate_weight = bell_draw(streams_of[9], (D, FF), D ** -0.5, 0.1875, ((0, 32),))
    up_weight = bell_draw(streams_of[10], (D, FF), D ** -0.5, 0.1875, ((0, 32),))
    down_weight = bell_draw(streams_of[11], (FF, D), FF ** -0.5, 0.109375, ((1, 32),))
    return {"tokens": tokens, "segments": segments, "cotangent": cotangent, "first_gain": first_gain, "query_weight": query_weight, "key_weight": key_weight, "value_weight": value_weight, "out_weight": out_weight, "second_gain": second_gain, "gate_weight": gate_weight, "up_weight": up_weight, "down_weight": down_weight}


@jax.custom_vjp
def low(v):
    return lax.optimization_barrier(v.astype(jnp.bfloat16)).astype(jnp.float32)

@jax.custom_vjp
def low_back(v):
    return v

def low_keep(v):
    return (low(v), None)

def low_pass(kept, grad):
    return (grad,)

def back_keep(v):
    return (v, None)

def back_low(kept, grad):
    return (low(grad),)
low.defvjp(low_keep, low_pass)
low_back.defvjp(back_keep, back_low)

def matmul(left, right):
    return jnp.dot(left, right, precision=lax.Precision.HIGHEST)

def rms_scale(values, gain):
    return values * lax.rsqrt(lax.optimization_barrier(jnp.mean(values * values, axis=-1, keepdims=True)) + 1e-06) * gain

def rotate(values, cosine, sine):
    half_width = values.shape[-1] // 2
    turned = jnp.concatenate([-values[..., half_width:], values[..., :half_width]], axis=-1)
    return values * cosine + turned * sine

def tables(positions, head_dim):
    inverse = 10000.0 ** (-2.0 * jnp.arange(head_dim // 2, dtype=jnp.float32) / head_dim)
    inverse = jnp.concatenate([inverse, inverse])
    angle = positions.astype(jnp.float32)[:, None] * inverse[None, :]
    return (jnp.cos(angle), jnp.sin(angle))

def attend(queries, keys, values, starts):
    span = min(512, LENGTH)
    blocks = LENGTH // span
    scale = HEAD_DIM ** (-0.5)
    padding = jnp.zeros((WINDOW, keys.shape[-1]), keys.dtype)
    key_rows = jnp.concatenate([padding, keys], axis=0)
    value_rows = jnp.concatenate([padding, values], axis=0)

    def one_block(block_index):
        first = (block_index * span).astype(jnp.int32)
        query_part = lax.dynamic_slice_in_dim(queries, first, span, 0)
        key_part = lax.dynamic_slice_in_dim(key_rows, first, span + WINDOW, 0)
        value_part = lax.dynamic_slice_in_dim(value_rows, first, span + WINDOW, 0)
        start_part = lax.dynamic_slice_in_dim(starts, first, span, 0)
        query_place = first + jnp.arange(span, dtype=jnp.int32)
        key_place = first - WINDOW + jnp.arange(span + WINDOW, dtype=jnp.int32)
        allowed = (key_place[None, :] <= query_place[:, None]) & (query_place[:, None] - key_place[None, :] < WINDOW) & (key_place[None, :] >= start_part[:, None])
        score = low_back(jnp.einsum('qhd,kd->hqk', query_part, key_part, precision=lax.Precision.HIGHEST) * scale)
        score = jnp.where(allowed[None], score, -1e+30)
        weights = low(jax.nn.softmax(score, axis=-1))
        return jnp.einsum('hqk,kd->qhd', weights, value_part, precision=lax.Precision.HIGHEST)
    result = lax.map(jax.checkpoint(one_block), jnp.arange(blocks, dtype=jnp.int32))
    return result.reshape(LENGTH, HEADS * HEAD_DIM)

def forward(inputs, cosine, sine, starts, first_gain, query_weight, key_weight, value_weight, out_weight, second_gain, gate_weight, up_weight, down_weight):
    length = inputs.shape[0]
    normed_one = low(rms_scale(inputs, first_gain))
    query = low_back(matmul(normed_one, query_weight)).reshape(length, HEADS, HEAD_DIM)
    query = low(rotate(query, cosine[:, None, :], sine[:, None, :]))
    keys = low_back(matmul(normed_one, key_weight))
    keys = low(rotate(keys, cosine, sine))
    values = low_back(low(matmul(normed_one, value_weight)))
    attended = low_back(low(attend(query, keys, values, starts)))
    mixed = inputs + low_back(matmul(attended, out_weight))
    normed_two = low(rms_scale(mixed, second_gain))
    gate = low_back(matmul(normed_two, gate_weight))
    up_part = low_back(matmul(normed_two, up_weight))
    hidden = low(jax.nn.gelu(gate, approximate=True) * up_part)
    return mixed + low_back(matmul(hidden, down_weight))

def reference(tokens, segments, cotangent, first_gain, query_weight, key_weight, value_weight, out_weight, second_gain, gate_weight, up_weight, down_weight):
    params = (first_gain.astype(jnp.float32), query_weight.astype(jnp.float32), key_weight.astype(jnp.float32), value_weight.astype(jnp.float32), out_weight.astype(jnp.float32), second_gain.astype(jnp.float32), gate_weight.astype(jnp.float32), up_weight.astype(jnp.float32), down_weight.astype(jnp.float32))

    def one_sequence(totals, item):
        inputs, doc_ids, grad_output = item
        places = jnp.arange(doc_ids.shape[0], dtype=jnp.int32)
        fresh = jnp.concatenate([jnp.ones((1,), dtype=bool), doc_ids[1:] != doc_ids[:-1]])
        starts = lax.cummax(jnp.where(fresh, places, 0).astype(jnp.int32), axis=0)
        cosine, sine = tables(places - starts, HEAD_DIM)

        def run(inputs_f, gain_a, query_w, key_w, value_w, out_w, gain_b, gate_w, up_w, down_w):
            return forward(inputs_f, cosine, sine, starts, gain_a, query_w, key_w, value_w, out_w, gain_b, gate_w, up_w, down_w)
        result, pull = jax.vjp(run, inputs.astype(jnp.float32), params[0], params[1], params[2], params[3], params[4], params[5], params[6], params[7], params[8])
        grads = pull(grad_output.astype(jnp.float32))
        totals = tuple((older + newer for older, newer in zip(totals, grads[1:])))
        return (totals, (result.astype(jnp.bfloat16), grads[0].astype(jnp.bfloat16)))
    initial = tuple((jnp.zeros(param.shape, jnp.float32) for param in params))
    totals, (output, grad_input) = lax.scan(one_sequence, initial, (tokens, segments, cotangent))
    return (output, grad_input, totals[0], totals[1], totals[2], totals[3], totals[4], totals[5], totals[6], totals[7], totals[8])
```

```python
import functools

import jax
import jax.numpy as jnp
from jax import lax
from jax.experimental import pallas as pl
from jax.experimental.pallas import tpu as pltpu
from jax.sharding import PartitionSpec as P

WINDOW = 1024
FF_CHUNKS = 6
MESH_ID = pl.DeviceIdType.MESH
MIB = 1 << 20


def rotate(values, cosine, sine):
    half_width = values.shape[-1] // 2
    turned = jnp.concatenate([-values[..., half_width:], values[..., :half_width]], axis=-1)
    return values * cosine + turned * sine


def tables(positions, head_dim):
    inverse = 10000.0 ** (-2.0 * jnp.arange(head_dim // 2, dtype=jnp.float32) / head_dim)
    angle = positions.astype(jnp.float32)[:, None] * inverse[None, :]
    cosine, sine = jnp.cos(angle), jnp.sin(angle)
    return (
        jnp.concatenate([cosine, cosine], axis=-1),
        jnp.concatenate([sine, sine], axis=-1),
    )


def rms_scale(values, gain):
    return values * lax.rsqrt(jnp.mean(values * values, axis=-1, keepdims=True) + 1e-06) * gain


def gated(gate, up_part):
    return jax.nn.gelu(gate, approximate=True) * up_part


def matmul(left, right):
    return jnp.dot(left, right, preferred_element_type=jnp.float32)


def left_times(left, right):
    return lax.dot_general(
        left, right, (((0,), (0,)), ((), ())), preferred_element_type=jnp.float32
    )


def right_times(left, right):
    return lax.dot_general(
        left, right, (((1,), (1,)), ((), ())), preferred_element_type=jnp.float32
    )


def place():
    batch, seq = lax.axis_index("batch"), lax.axis_index("seq")
    return batch // 2, lax.rem(batch, 2), seq // 2, lax.rem(seq, 2)


def device(x, c, z, y):
    return (x * 2 + c, z * 2 + y)


def greet(partners):
    barrier = pltpu.get_barrier_semaphore()
    for partner in partners:
        pl.semaphore_signal(barrier, inc=1, device_id=partner, device_id_type=MESH_ID)
    pl.semaphore_wait(barrier, len(partners))


def neighbours():
    x, c, z, y = place()
    return [
        device(x, c, lax.rem(z + 1, 4), y),
        device(x, c, lax.rem(z + 2, 4), y),
        device(x, c, lax.rem(z + 3, 4), y),
        device(1 - x, c, z, y),
        device(x, c, z, 1 - y),
        device(x, 1 - c, z, y),
    ]


def send(source, target, send_sem, recv_sem, partner):
    copy = pltpu.make_async_remote_copy(
        src_ref=source,
        dst_ref=target,
        send_sem=send_sem,
        recv_sem=recv_sem,
        device_id=partner,
        device_id_type=MESH_ID,
    )
    copy.start()
    return copy


class Gather:
    STEPS = 4
    SEMS = 8

    def __init__(self, shard, full, sems, local_sem, chunks):
        self.shard, self.full, self.sems, self.local_sem = shard, full, sems, local_sem
        self.chunks = chunks
        self.copies = {}

    def go(self, chunk, slot, source, partner):
        self.copies[chunk, slot] = send(
            source, source, self.sems.at[0, chunk, slot], self.sems.at[1, chunk, slot], partner
        )

    def arrived(self, chunk, slot):
        self.copies[chunk, slot].wait_recv()

    def step(self, number, chunk):
        x, c, z, y = place()
        start, middle, end = self.chunks[chunk]
        full = self.full
        whole = pl.ds(start, end - start)
        first, second = pl.ds(start, middle - start), pl.ds(middle, end - middle)
        if number == 0:
            mine = full.at[x, c, z, y, :, whole]
            keep = pltpu.make_async_copy(
                self.shard.at[:, whole], mine, self.local_sem.at[chunk]
            )
            keep.start()
            self.copies[chunk, "keep"] = keep
            for hop in (1, 2, 3):
                self.copies[chunk, hop - 1] = send(
                    self.shard.at[:, whole],
                    mine,
                    self.sems.at[0, chunk, hop - 1],
                    self.sems.at[1, chunk, hop - 1],
                    device(x, c, lax.rem(z + hop, 4), y),
                )
        elif number == 1:
            self.copies[chunk, "keep"].wait()
            for slot in (0, 1, 2):
                self.arrived(chunk, slot)
            self.go(chunk, 3, full.at[x, c, :, y, :, first], device(x, c, z, 1 - y))
            self.go(chunk, 4, full.at[x, c, :, y, :, second], device(1 - x, c, z, y))
        elif number == 2:
            self.arrived(chunk, 3)
            self.go(chunk, 5, full.at[x, c, :, :, :, first], device(1 - x, c, z, y))
            self.arrived(chunk, 4)
            self.go(chunk, 6, full.at[:, c, :, y, :, second], device(x, c, z, 1 - y))
        elif number == 3:
            self.arrived(chunk, 5)
            self.arrived(chunk, 6)
            self.go(chunk, 7, full.at[:, c, :, :, :, whole], device(x, 1 - c, z, y))
        else:
            self.arrived(chunk, 7)

    def drain(self):
        for (_, slot), copy in self.copies.items():
            if slot != "keep":
                copy.wait_send()


def gather_kernel(chunks, shard_ref, full_ref, sems, local_sem):
    greet(neighbours())
    gather = Gather(shard_ref, full_ref, sems, local_sem, chunks)
    for tick in range(len(chunks) + Gather.STEPS):
        for number in range(Gather.STEPS + 1):
            chunk = tick - number
            if 0 <= chunk < len(chunks):
                gather.step(number, chunk)
    gather.drain()


def gather_all(shard, chunks):
    rows, columns = shard.shape
    count = len(chunks)
    full = pl.pallas_call(
        functools.partial(gather_kernel, chunks),
        out_shape=jax.ShapeDtypeStruct((2, 2, 4, 2, rows, columns), shard.dtype),
        in_specs=[pl.BlockSpec(memory_space=pl.ANY)],
        out_specs=pl.BlockSpec(memory_space=pl.ANY),
        scratch_shapes=[
            pltpu.SemaphoreType.DMA((2, count, Gather.SEMS)),
            pltpu.SemaphoreType.DMA((count,)),
        ],
        compiler_params=pltpu.CompilerParams(collective_id=0, has_side_effects=True),
        name="gather_weights",
    )(shard)
    return full.reshape(32 * rows, columns)


class Scatter:
    STEPS = 4
    SEMS = 8

    def __init__(self, own, first, second_a, second_b, third_a, third_b, last, sems):
        self.own = own
        self.first = first
        self.second_a, self.second_b = second_a, second_b
        self.third_a, self.third_b = third_a, third_b
        self.last = last
        self.sems = sems
        self.copies = {}


def add_rows(target, other):
    target[...] = (target[...].astype(jnp.float32) + other[...].astype(jnp.float32)).astype(
        target.dtype
    )


def scatter_kernel(chunks, own_ref, out_ref, *scratch):
    greet(neighbours())
    x, c, z, y = place()
    count = len(chunks)
    sems, local_sems, out_sem = scratch[:3]
    buffers = scratch[3:]
    copies = {}

    def go(chunk, slot, source, target, partner):
        copies[chunk, slot] = send(
            source, target, sems.at[0, chunk, slot], sems.at[1, chunk, slot], partner
        )

    for tick in range(count + 5):
        for number in range(6):
            chunk = tick - number
            if not 0 <= chunk < count:
                continue
            start, middle, end = chunks[chunk]
            width, half = end - start, middle - start
            one, two_a, two_b, three_a, three_b, last, mine, result = buffers[
                8 * chunk : 8 * chunk + 8
            ]
            whole = pl.ds(start, width)
            if number == 0:
                go(chunk, 0, own_ref.at[:, 1 - c, :, :, :, whole], one, device(x, 1 - c, z, y))
                keep = pltpu.make_async_copy(
                    own_ref.at[:, c, :, :, :, whole], mine, local_sems.at[chunk]
                )
                keep.start()
                copies[chunk, "keep"] = keep
            elif number == 1:
                copies[chunk, "keep"].wait()
                copies[chunk, 0].wait_recv()
                for i in range(2):
                    for j in range(4):

                        @pl.loop(0, 2)
                        def _(k):
                            add_rows(one.at[i, j, k], mine.at[i, j, k])

                go(chunk, 1, one.at[1 - x, :, :, :, :half], two_a, device(1 - x, c, z, y))
                go(chunk, 2, one.at[:, :, 1 - y, :, half:], two_b, device(x, c, z, 1 - y))
            elif number == 2:
                copies[chunk, 1].wait_recv()
                for j in range(4):

                    @pl.loop(0, 2)
                    def _(k):
                        add_rows(two_a.at[j, k], one.at[x, j, k, :, :half])

                go(chunk, 3, two_a.at[:, 1 - y], three_a, device(x, c, z, 1 - y))
                copies[chunk, 2].wait_recv()
                for j in range(2):

                    @pl.loop(0, 4)
                    def _(k):
                        add_rows(two_b.at[j, k], one.at[j, k, y, :, half:])

                go(chunk, 4, two_b.at[1 - x], three_b, device(1 - x, c, z, y))
            elif number == 3:
                copies[chunk, 3].wait_recv()

                @pl.loop(0, 4)
                def _(k):
                    mine[0, k, 0, :, :half] = (
                        three_a[k].astype(jnp.float32) + two_a[k, y].astype(jnp.float32)
                    ).astype(mine.dtype)

                copies[chunk, 4].wait_recv()

                @pl.loop(0, 4)
                def _(k):
                    mine[0, k, 0, :, half:] = (
                        three_b[k].astype(jnp.float32) + two_b[x, k].astype(jnp.float32)
                    ).astype(mine.dtype)

                for hop in (1, 2, 3):
                    go(
                        chunk,
                        4 + hop,
                        mine.at[0, lax.rem(z + hop, 4), 0],
                        last.at[hop - 1],
                        device(x, c, lax.rem(z + hop, 4), y),
                    )
            elif number == 4:
                total = mine[0, z, 0].astype(jnp.float32)
                for hop in (1, 2, 3):
                    copies[chunk, 4 + hop].wait_recv()
                    total += last[hop - 1].astype(jnp.float32)
                result[...] = total
                done = pltpu.make_async_copy(result, out_ref.at[:, whole], out_sem.at[chunk])
                done.start()
                copies[chunk, "done"] = done
            else:
                for slot in range(8):
                    copies[chunk, slot].wait_send()
                copies[chunk, "done"].wait()


def scatter_all(own, rows, chunks):
    columns = own.shape[1]
    count = len(chunks)
    scratch = [
        pltpu.SemaphoreType.DMA((2, count, Scatter.SEMS)),
        pltpu.SemaphoreType.DMA((count,)),
        pltpu.SemaphoreType.DMA((count,)),
    ]
    for start, middle, end in chunks:
        n, h = end - start, middle - start
        scratch += [
            pltpu.VMEM((2, 4, 2, rows, n), own.dtype),
            pltpu.VMEM((4, 2, rows, h), own.dtype),
            pltpu.VMEM((2, 4, rows, n - h), own.dtype),
            pltpu.VMEM((4, rows, h), own.dtype),
            pltpu.VMEM((4, rows, n - h), own.dtype),
            pltpu.VMEM((3, rows, n), own.dtype),
            pltpu.VMEM((2, 4, 2, rows, n), own.dtype),
            pltpu.VMEM((rows, n), jnp.float32),
        ]
    return pl.pallas_call(
        functools.partial(scatter_kernel, chunks),
        out_shape=jax.ShapeDtypeStruct((rows, columns), jnp.float32),
        in_specs=[pl.BlockSpec(memory_space=pl.ANY)],
        out_specs=pl.BlockSpec(memory_space=pl.ANY),
        scratch_shapes=scratch,
        compiler_params=pltpu.CompilerParams(
            collective_id=1, has_side_effects=True, vmem_limit_bytes=56 * MIB
        ),
        name="scatter_grads",
    )(own.reshape(2, 2, 4, 2, rows, columns))


def columns_of(width, head_dim, heads, hidden):
    attention = width + 2 * head_dim + 128
    chunks = [(0, 640, attention), (attention, attention + width // 2, attention + width)]
    start = attention + width
    step = 3 * hidden // FF_CHUNKS
    for _ in range(FF_CHUNKS):
        chunks.append((start, start + step // 2, start + step))
        start += step
    return chunks


def stack_ff(gate, up_part, down_t):
    rows, hidden = gate.shape
    parts = [p.reshape(rows, FF_CHUNKS, hidden // FF_CHUNKS) for p in (gate, up_part, down_t)]
    return jnp.stack(parts, axis=2).reshape(rows, 3 * hidden)


def unstack_ff(stacked):
    rows, hidden = stacked.shape[0], stacked.shape[1] // 3
    parts = stacked.reshape(rows, FF_CHUNKS, 3, hidden // FF_CHUNKS)
    return [parts[:, :, i].reshape(rows, hidden) for i in range(3)]


def allowed_pairs(query_place, key_place, starts):
    later = key_place[None, :] <= query_place[:, None]
    inside = query_place[:, None] - key_place[None, :] < WINDOW
    same_doc = key_place[None, :] >= starts[:, None]
    return later & inside & same_doc


def attend_one(query, pairs, starts, query_place, key_place, scale, head_dim):
    keys = pairs[:, :head_dim]
    values = pairs[:, head_dim:]
    allowed = allowed_pairs(query_place, key_place, starts)
    score = jnp.einsum("qhd,kd->hqk", query, keys, preferred_element_type=jnp.float32) * scale
    score = jnp.where(allowed[None], score, -1e30)
    peak = jnp.max(score, axis=-1, keepdims=True)
    log_total = peak + jnp.log(jnp.sum(jnp.exp(score - peak), axis=-1, keepdims=True))
    weights_low = jnp.exp(score - log_total).astype(jnp.bfloat16)
    result = jnp.einsum("hqk,kd->qhd", weights_low, values, preferred_element_type=jnp.float32)
    return (result, log_total[..., 0])


def attend_back(query, pairs, starts, log_total, grad_out, query_place, key_place, scale, head_dim):
    keys = pairs[:, :head_dim]
    values = pairs[:, head_dim:]
    allowed = allowed_pairs(query_place, key_place, starts)
    score = jnp.einsum("qhd,kd->hqk", query, keys, preferred_element_type=jnp.float32) * scale
    score = jnp.where(allowed[None], score, -1e30)
    weights = jnp.exp(score - log_total[..., None])
    weights_low = weights.astype(jnp.bfloat16)
    grad_weights = jnp.einsum("qhd,kd->hqk", grad_out, values, preferred_element_type=jnp.float32)
    grad_values = jnp.einsum(
        "hqk,qhd->kd", weights_low, grad_out, preferred_element_type=jnp.float32
    )
    grad_score = (
        weights * (grad_weights - jnp.sum(weights * grad_weights, axis=-1, keepdims=True))
    ).astype(jnp.bfloat16)
    grad_query = (
        jnp.einsum("hqk,kd->qhd", grad_score, keys, preferred_element_type=jnp.float32) * scale
    )
    grad_keys = (
        jnp.einsum("hqk,qhd->kd", grad_score, query, preferred_element_type=jnp.float32) * scale
    )
    return (grad_query, jnp.concatenate([grad_keys, grad_values], axis=-1))


def shifted(value, axis, steps):
    count = lax.axis_size(axis)
    initial, last = (max(0, -steps), min(count, count - steps))
    return lax.ppermute(value, axis, [(source, source + steps) for source in range(initial, last)])


def on_device(
    own_links,
    tokens,
    segments,
    cotangent,
    first_gain,
    query_weight,
    key_weight,
    value_weight,
    out_weight,
    second_gain,
    gate_weight,
    up_weight,
    down_weight,
):
    seqs, block_len, width = tokens.shape
    head_dim = key_weight.shape[1]
    heads = query_weight.shape[1] // head_dim
    hidden_width = gate_weight.shape[1]
    shard_rows = first_gain.shape[0]
    reach = (WINDOW - 1 + block_len - 1) // block_len
    span = (reach + 1) * block_len
    scale = head_dim ** (-0.5)
    rows = seqs * block_len
    chunks = columns_of(width, head_dim, heads, hidden_width)

    gains = jnp.zeros((shard_rows, 128), first_gain.dtype)
    gains = gains.at[:, 0].set(first_gain).at[:, 1].set(second_gain)
    shard = jnp.concatenate(
        [
            query_weight,
            key_weight,
            value_weight,
            gains,
            out_weight.T,
            stack_ff(gate_weight, up_weight, down_weight.T),
        ],
        axis=1,
    )
    if own_links:
        full = gather_all(shard, chunks)
    else:
        full = lax.all_gather(shard, ("batch", "seq"), axis=0, tiled=True)
    all_segments = lax.all_gather(segments, "seq", axis=1, tiled=True)
    query_full = full[:, :width]
    key_full = full[:, width : width + head_dim]
    value_full = full[:, width + head_dim : width + 2 * head_dim]
    gains_full = full[:, width + 2 * head_dim : chunks[0][2]].astype(jnp.float32)
    gain_one, gain_two = gains_full[:, 0], gains_full[:, 1]
    out_t = full[:, chunks[1][0] : chunks[1][2]]
    gate_full, up_full, down_t = unstack_ff(full[:, chunks[2][0] :])

    starts = jnp.sum(all_segments[:, None, :] < segments[:, :, None], axis=-1, dtype=jnp.int32)
    query_place = jnp.arange(block_len, dtype=jnp.int32) + lax.axis_index("seq") * block_len
    key_place = query_place[0] - reach * block_len + jnp.arange(span, dtype=jnp.int32)
    cosine, sine = tables((query_place[None, :] - starts).reshape(-1), head_dim)

    def forward_item(item):
        return attend_one(item[0], item[1], item[2], query_place, key_place, scale, head_dim)

    def backward_item(item):
        return attend_back(
            item[0], item[1], item[2], item[3], item[4], query_place, key_place, scale, head_dim
        )

    inputs = tokens.reshape(rows, width).astype(jnp.float32)
    normed_one = rms_scale(inputs, gain_one).astype(jnp.bfloat16)
    query = rotate(
        matmul(normed_one, query_full).reshape(rows, heads, head_dim),
        cosine[:, None, :],
        sine[:, None, :],
    ).astype(jnp.bfloat16)
    key_rot = rotate(matmul(normed_one, key_full), cosine, sine).astype(jnp.bfloat16)
    value_low = matmul(normed_one, value_full).astype(jnp.bfloat16)
    own_pairs = jnp.concatenate([key_rot, value_low], axis=-1).reshape(
        seqs, block_len, 2 * head_dim
    )
    pieces = [shifted(own_pairs, "seq", distance) for distance in range(reach, 0, -1)]
    window_pairs = jnp.concatenate(pieces + [own_pairs], axis=1)
    query_seq = query.reshape(seqs, block_len, heads, head_dim)
    attended, log_total = lax.map(forward_item, (query_seq, window_pairs, starts))
    attended_low = attended.reshape(rows, heads * head_dim).astype(jnp.bfloat16)
    mixed = inputs + right_times(attended_low, out_t)
    normed_two = rms_scale(mixed, gain_two).astype(jnp.bfloat16)
    gate = matmul(normed_two, gate_full)
    up_part = matmul(normed_two, up_full)
    hidden = gated(gate, up_part).astype(jnp.bfloat16)
    output = (mixed + right_times(hidden, down_t)).astype(jnp.bfloat16)

    grad_rows = cotangent.reshape(rows, width)
    grad_down_t = left_times(grad_rows, hidden)
    grad_hidden = matmul(grad_rows, down_t)
    _, pull_gated = jax.vjp(gated, gate, up_part)
    grad_gate, grad_up = pull_gated(grad_hidden)
    grad_gate = grad_gate.astype(jnp.bfloat16)
    grad_up = grad_up.astype(jnp.bfloat16)
    grad_gate_w = left_times(normed_two, grad_gate)
    grad_up_w = left_times(normed_two, grad_up)
    grad_normed_two = right_times(grad_gate, gate_full) + right_times(grad_up, up_full)
    _, pull_second = jax.vjp(rms_scale, mixed, gain_two)
    grad_mixed, grad_gain_two = pull_second(grad_normed_two)
    grad_mixed = grad_mixed + grad_rows.astype(jnp.float32)
    grad_branch = grad_mixed.astype(jnp.bfloat16)
    grad_out_t = left_times(grad_branch, attended_low)
    grad_attended = matmul(grad_branch, out_t).astype(jnp.bfloat16)
    grad_query, grad_pairs = lax.map(
        backward_item,
        (
            query_seq,
            window_pairs,
            starts,
            log_total,
            grad_attended.reshape(seqs, block_len, heads, head_dim),
        ),
    )
    own_grad = grad_pairs[:, reach * block_len :]
    for distance in range(1, reach + 1):
        piece = grad_pairs[:, (reach - distance) * block_len : (reach - distance + 1) * block_len]
        own_grad = own_grad + shifted(piece.astype(jnp.bfloat16), "seq", -distance).astype(
            piece.dtype
        )
    grad_key_rot = own_grad[..., :head_dim].reshape(rows, head_dim)
    grad_value = own_grad[..., head_dim:].reshape(rows, head_dim).astype(jnp.bfloat16)
    grad_q = rotate(
        grad_query.reshape(rows, heads, head_dim), cosine[:, None, :], -sine[:, None, :]
    )
    grad_q = grad_q.reshape(rows, heads * head_dim).astype(jnp.bfloat16)
    grad_k = rotate(grad_key_rot, cosine, -sine).astype(jnp.bfloat16)
    grad_qkv = jnp.concatenate([grad_q, grad_k, grad_value], axis=1)
    grad_qkv_w = left_times(normed_one, grad_qkv)
    grad_normed_one = right_times(grad_qkv, full[:, : width + 2 * head_dim])
    _, pull_first = jax.vjp(rms_scale, inputs, gain_one)
    grad_x, grad_gain_one = pull_first(grad_normed_one)
    grad_input = (grad_x + grad_mixed).astype(jnp.bfloat16)

    grad_gains = jnp.zeros((width, 128), jnp.float32)
    grad_gains = grad_gains.at[:, 0].set(grad_gain_one).at[:, 1].set(grad_gain_two)
    grads = jnp.concatenate(
        [
            grad_qkv_w,
            grad_gains,
            grad_out_t,
            stack_ff(grad_gate_w, grad_up_w, grad_down_t),
        ],
        axis=1,
    ).astype(jnp.bfloat16)
    if own_links:
        share = scatter_all(grads, shard_rows, chunks)
    else:
        share = lax.psum_scatter(grads, ("batch", "seq"), scatter_dimension=0, tiled=True)
        share = share.astype(jnp.float32)
    share_gate, share_up, share_down_t = unstack_ff(share[:, chunks[2][0] :])
    return (
        output.reshape(tokens.shape),
        grad_input.reshape(tokens.shape),
        share[:, width + 2 * head_dim],
        share[:, :width],
        share[:, width : width + head_dim],
        share[:, width + head_dim : width + 2 * head_dim],
        share[:, chunks[1][0] : chunks[1][2]].T,
        share[:, width + 2 * head_dim + 1],
        share_gate,
        share_up,
        share_down_t.T,
    )


def solution(mesh):
    both = ("batch", "seq")
    rows_split, columns_split = P(both, None), P(None, both)
    tokens_split, gain_split = P("batch", "seq", None), P(both)
    weights = (
        gain_split,
        rows_split,
        rows_split,
        rows_split,
        columns_split,
        gain_split,
        rows_split,
        rows_split,
        columns_split,
    )
    in_specs = (tokens_split, P("batch", "seq"), tokens_split) + weights
    out_specs = (tokens_split, tokens_split) + weights
    own_links = (mesh.shape["batch"], mesh.shape["seq"]) == (4, 8)
    return jax.shard_map(
        functools.partial(on_device, own_links),
        mesh=mesh,
        in_specs=in_specs,
        out_specs=out_specs,
        check_vma=False,
    )
```

```python
import functools

import jax
import jax.numpy as jnp
from jax import lax
from jax.experimental import pallas as pl
from jax.experimental.pallas import tpu as pltpu
from jax.sharding import PartitionSpec as P

WINDOW = 1024
FF_CHUNKS = 6
MESH_ID = pl.DeviceIdType.MESH
MIB = 1 << 20


def tables(positions, head_dim):
    inverse = 10000.0 ** (-2.0 * jnp.arange(head_dim // 2, dtype=jnp.float32) / head_dim)
    angle = positions.astype(jnp.float32)[:, None] * inverse[None, :]
    cosine, sine = jnp.cos(angle), jnp.sin(angle)
    return (
        jnp.concatenate([cosine, cosine], axis=-1),
        jnp.concatenate([-sine, sine], axis=-1),
    )


def matmul(left, right):
    return jnp.dot(left, right, preferred_element_type=jnp.float32)


def right_times(left, right):
    return lax.dot_general(
        left, right, (((1,), (1,)), ((), ())), preferred_element_type=jnp.float32
    )


def place():
    batch, seq = lax.axis_index("batch"), lax.axis_index("seq")
    return batch // 2, lax.rem(batch, 2), seq // 2, lax.rem(seq, 2)


def device(x, c, z, y):
    return (x * 2 + c, z * 2 + y)


def greet(partners):
    barrier = pltpu.get_barrier_semaphore()
    for partner in partners:
        pl.semaphore_signal(barrier, inc=1, device_id=partner, device_id_type=MESH_ID)
    pl.semaphore_wait(barrier, len(partners))


def neighbours():
    x, c, z, y = place()
    return [
        device(x, c, lax.rem(z + 1, 4), y),
        device(x, c, lax.rem(z + 2, 4), y),
        device(x, c, lax.rem(z + 3, 4), y),
        device(1 - x, c, z, y),
        device(x, c, z, 1 - y),
        device(x, 1 - c, z, y),
    ]


def send(source, target, send_sem, recv_sem, partner):
    copy = pltpu.make_async_remote_copy(
        src_ref=source,
        dst_ref=target,
        send_sem=send_sem,
        recv_sem=recv_sem,
        device_id=partner,
        device_id_type=MESH_ID,
    )
    copy.start()
    return copy


class Gather:
    STEPS = 4
    SEMS = 8

    def __init__(self, shard, full, sems, local_sem, chunks):
        self.shard, self.full, self.sems, self.local_sem = shard, full, sems, local_sem
        self.chunks = chunks
        self.copies = {}

    def go(self, chunk, slot, source, partner):
        self.copies[chunk, slot] = send(
            source, source, self.sems.at[0, chunk, slot], self.sems.at[1, chunk, slot], partner
        )

    def arrived(self, chunk, slot):
        self.copies[chunk, slot].wait_recv()

    def step(self, number, chunk):
        x, c, z, y = place()
        start, middle, end = self.chunks[chunk]
        full = self.full
        whole = pl.ds(start, end - start)
        first, second = pl.ds(start, middle - start), pl.ds(middle, end - middle)
        if number == 0:
            mine = full.at[x, c, z, y, :, whole]
            keep = pltpu.make_async_copy(
                self.shard.at[:, whole], mine, self.local_sem.at[chunk]
            )
            keep.start()
            self.copies[chunk, "keep"] = keep
            for hop in (1, 2, 3):
                self.copies[chunk, hop - 1] = send(
                    self.shard.at[:, whole],
                    mine,
                    self.sems.at[0, chunk, hop - 1],
                    self.sems.at[1, chunk, hop - 1],
                    device(x, c, lax.rem(z + hop, 4), y),
                )
        elif number == 1:
            self.copies[chunk, "keep"].wait()
            for slot in (0, 1, 2):
                self.arrived(chunk, slot)
            self.go(chunk, 3, full.at[x, c, :, y, :, first], device(x, c, z, 1 - y))
            self.go(chunk, 4, full.at[x, c, :, y, :, second], device(1 - x, c, z, y))
        elif number == 2:
            self.arrived(chunk, 3)
            self.go(chunk, 5, full.at[x, c, :, :, :, first], device(1 - x, c, z, y))
            self.arrived(chunk, 4)
            self.go(chunk, 6, full.at[:, c, :, y, :, second], device(x, c, z, 1 - y))
        elif number == 3:
            self.arrived(chunk, 5)
            self.arrived(chunk, 6)
            self.go(chunk, 7, full.at[:, c, :, :, :, whole], device(x, 1 - c, z, y))
        else:
            self.arrived(chunk, 7)

    def drain(self):
        for (_, slot), copy in self.copies.items():
            if slot != "keep":
                copy.wait_send()


def gather_kernel(chunks, shard_ref, full_ref, sems, local_sem):
    greet(neighbours())
    gather = Gather(shard_ref, full_ref, sems, local_sem, chunks)
    for tick in range(len(chunks) + Gather.STEPS):
        for number in range(Gather.STEPS + 1):
            chunk = tick - number
            if 0 <= chunk < len(chunks):
                gather.step(number, chunk)
    gather.drain()


def gather_all(shard, chunks):
    rows, columns = shard.shape
    count = len(chunks)
    full = pl.pallas_call(
        functools.partial(gather_kernel, chunks),
        out_shape=jax.ShapeDtypeStruct((2, 2, 4, 2, rows, columns), shard.dtype),
        in_specs=[pl.BlockSpec(memory_space=pl.ANY)],
        out_specs=pl.BlockSpec(memory_space=pl.ANY),
        scratch_shapes=[
            pltpu.SemaphoreType.DMA((2, count, Gather.SEMS)),
            pltpu.SemaphoreType.DMA((count,)),
        ],
        compiler_params=pltpu.CompilerParams(collective_id=0, has_side_effects=True),
        name="gather_weights",
    )(shard)
    return full.reshape(32 * rows, columns)


class Scatter:
    STEPS = 4
    SEMS = 8

    def __init__(self, own, first, second_a, second_b, third_a, third_b, last, sems):
        self.own = own
        self.first = first
        self.second_a, self.second_b = second_a, second_b
        self.third_a, self.third_b = third_a, third_b
        self.last = last
        self.sems = sems
        self.copies = {}


def add_rows(target, other):
    target[...] = (target[...].astype(jnp.float32) + other[...].astype(jnp.float32)).astype(
        target.dtype
    )


def scatter_kernel(chunks, own_ref, out_ref, *scratch):
    greet(neighbours())
    x, c, z, y = place()
    count = len(chunks)
    sems, local_sems, out_sem = scratch[:3]
    buffers = scratch[3:]
    copies = {}

    def go(chunk, slot, source, target, partner):
        copies[chunk, slot] = send(
            source, target, sems.at[0, chunk, slot], sems.at[1, chunk, slot], partner
        )

    for tick in range(count + 5):
        for number in range(6):
            chunk = tick - number
            if not 0 <= chunk < count:
                continue
            start, middle, end = chunks[chunk]
            width, half = end - start, middle - start
            one, two_a, two_b, three_a, three_b, last, mine, result = buffers[
                8 * chunk : 8 * chunk + 8
            ]
            whole = pl.ds(start, width)
            if number == 0:
                go(chunk, 0, own_ref.at[:, 1 - c, :, :, :, whole], one, device(x, 1 - c, z, y))
                keep = pltpu.make_async_copy(
                    own_ref.at[:, c, :, :, :, whole], mine, local_sems.at[chunk]
                )
                keep.start()
                copies[chunk, "keep"] = keep
            elif number == 1:
                copies[chunk, "keep"].wait()
                copies[chunk, 0].wait_recv()
                for i in range(2):
                    for j in range(4):

                        @pl.loop(0, 2)
                        def _(k):
                            add_rows(one.at[i, j, k], mine.at[i, j, k])

                go(chunk, 1, one.at[1 - x, :, :, :, :half], two_a, device(1 - x, c, z, y))
                go(chunk, 2, one.at[:, :, 1 - y, :, half:], two_b, device(x, c, z, 1 - y))
            elif number == 2:
                copies[chunk, 1].wait_recv()
                for j in range(4):

                    @pl.loop(0, 2)
                    def _(k):
                        add_rows(two_a.at[j, k], one.at[x, j, k, :, :half])

                go(chunk, 3, two_a.at[:, 1 - y], three_a, device(x, c, z, 1 - y))
                copies[chunk, 2].wait_recv()
                for j in range(2):

                    @pl.loop(0, 4)
                    def _(k):
                        add_rows(two_b.at[j, k], one.at[j, k, y, :, half:])

                go(chunk, 4, two_b.at[1 - x], three_b, device(1 - x, c, z, y))
            elif number == 3:
                copies[chunk, 3].wait_recv()

                @pl.loop(0, 4)
                def _(k):
                    mine[0, k, 0, :, :half] = (
                        three_a[k].astype(jnp.float32) + two_a[k, y].astype(jnp.float32)
                    ).astype(mine.dtype)

                copies[chunk, 4].wait_recv()

                @pl.loop(0, 4)
                def _(k):
                    mine[0, k, 0, :, half:] = (
                        three_b[k].astype(jnp.float32) + two_b[x, k].astype(jnp.float32)
                    ).astype(mine.dtype)

                for hop in (1, 2, 3):
                    go(
                        chunk,
                        4 + hop,
                        mine.at[0, lax.rem(z + hop, 4), 0],
                        last.at[hop - 1],
                        device(x, c, lax.rem(z + hop, 4), y),
                    )
            elif number == 4:
                total = mine[0, z, 0].astype(jnp.float32)
                for hop in (1, 2, 3):
                    copies[chunk, 4 + hop].wait_recv()
                    total += last[hop - 1].astype(jnp.float32)
                result[...] = total
                done = pltpu.make_async_copy(result, out_ref.at[:, whole], out_sem.at[chunk])
                done.start()
                copies[chunk, "done"] = done
            else:
                for slot in range(8):
                    copies[chunk, slot].wait_send()
                copies[chunk, "done"].wait()


def scatter_all(own, rows, chunks):
    columns = own.shape[1]
    count = len(chunks)
    scratch = [
        pltpu.SemaphoreType.DMA((2, count, Scatter.SEMS)),
        pltpu.SemaphoreType.DMA((count,)),
        pltpu.SemaphoreType.DMA((count,)),
    ]
    for start, middle, end in chunks:
        n, h = end - start, middle - start
        scratch += [
            pltpu.VMEM((2, 4, 2, rows, n), own.dtype),
            pltpu.VMEM((4, 2, rows, h), own.dtype),
            pltpu.VMEM((2, 4, rows, n - h), own.dtype),
            pltpu.VMEM((4, rows, h), own.dtype),
            pltpu.VMEM((4, rows, n - h), own.dtype),
            pltpu.VMEM((3, rows, n), own.dtype),
            pltpu.VMEM((2, 4, 2, rows, n), own.dtype),
            pltpu.VMEM((rows, n), jnp.float32),
        ]
    return pl.pallas_call(
        functools.partial(scatter_kernel, chunks),
        out_shape=jax.ShapeDtypeStruct((rows, columns), jnp.float32),
        in_specs=[pl.BlockSpec(memory_space=pl.ANY)],
        out_specs=pl.BlockSpec(memory_space=pl.ANY),
        scratch_shapes=scratch,
        compiler_params=pltpu.CompilerParams(
            collective_id=1, has_side_effects=True, vmem_limit_bytes=56 * MIB
        ),
        name="scatter_grads",
    )(own.reshape(2, 2, 4, 2, rows, columns))


ROW_TILE = 256
LOG2E = 1.4426950408889634
NEG = -1e30


def row(block, index):
    return pl.BlockSpec(block, index)


def vmem():
    return pl.BlockSpec(memory_space=pltpu.VMEM)


def hbm():
    return pl.BlockSpec(memory_space=pl.ANY)


def params(**more):
    return pltpu.CompilerParams(vmem_limit_bytes=58 * MIB, **more)


def inverse_rms(values):
    return lax.rsqrt(jnp.mean(values * values, axis=-1, keepdims=True) + 1e-06)


def rms_back(values, scale, gain, grad):
    inner = jnp.mean(values * gain * grad, axis=-1, keepdims=True)
    return scale * gain * grad - values * (scale * scale * scale * inner)


def project_kernel(x_ref, cos_ref, sin_ref, w_ref, h_ref, q_ref, kv_ref, gains_ref):
    heads, head_dim = q_ref.shape[1], q_ref.shape[3]
    width = heads * head_dim
    gains = w_ref[:, width + 2 * head_dim :].astype(jnp.float32).T[:8]

    @pl.when(pl.program_id(0) == 0)
    def _():
        gains_ref[...] = gains

    x = x_ref[...].astype(jnp.float32)
    normed = (x * inverse_rms(x) * gains[0:1]).astype(jnp.bfloat16)
    h_ref[...] = normed
    cosine, sine = cos_ref[...], sin_ref[...]

    def turn(u):
        return (u * cosine + pltpu.roll(u, head_dim // 2, 1) * sine).astype(jnp.bfloat16)

    for pair in range(heads // 2):
        both = matmul(normed, w_ref[:, 2 * pair * head_dim : (2 * pair + 2) * head_dim])
        q_ref[0, 2 * pair] = turn(both[:, :head_dim])
        q_ref[0, 2 * pair + 1] = turn(both[:, head_dim:])
    both = matmul(normed, w_ref[:, width : width + 2 * head_dim])
    kv_ref[0, :, :head_dim] = turn(both[:, :head_dim])
    kv_ref[0, :, head_dim:] = both[:, head_dim:].astype(jnp.bfloat16)


def project(x, cosine, sine, weights, seqs, heads, head_dim):
    rows, width = x.shape
    block = rows // seqs
    return pl.pallas_call(
        project_kernel,
        grid=(seqs,),
        in_specs=[
            row((block, width), lambda b: (b, 0)),
            row((block, head_dim), lambda b: (b, 0)),
            row((block, head_dim), lambda b: (b, 0)),
            row(weights.shape, lambda b: (0, 0)),
        ],
        out_specs=[
            row((block, width), lambda b: (b, 0)),
            row((1, heads, block, head_dim), lambda b: (b, 0, 0, 0)),
            row((1, block, 2 * head_dim), lambda b: (b, 0, 0)),
            row((8, width), lambda b: (0, 0)),
        ],
        out_shape=[
            jax.ShapeDtypeStruct((rows, width), jnp.bfloat16),
            jax.ShapeDtypeStruct((seqs, heads, block, head_dim), jnp.bfloat16),
            jax.ShapeDtypeStruct((seqs, block, 2 * head_dim), jnp.bfloat16),
            jax.ShapeDtypeStruct((8, width), jnp.float32),
        ],
        compiler_params=params(),
        name="project",
    )(x, cosine, sine, weights)


HALF = 128
GROUP = 4


def attend_kernel(scale, q_ref, kv_ref, low_ref, o_ref, lse_ref):
    heads, block, head_dim = q_ref.shape[1:]
    span = kv_ref.shape[1] - (block - HALF)
    factor = scale * LOG2E

    @pl.loop(0, block // HALF)
    def _(half):
        first = pl.multiple_of(half * HALF, HALF)
        keys = kv_ref[0, pl.ds(first, span), :head_dim]
        values = kv_ref[0, pl.ds(first, span), head_dim:]
        values = jnp.concatenate([values, jnp.ones_like(values)], axis=1)
        place = lax.broadcasted_iota(jnp.int32, (HALF, span), 1)
        local = lax.broadcasted_iota(jnp.int32, (HALF, span), 0)
        low = low_ref[0, pl.ds(first, HALF)] - first
        allowed = (place >= low) & (place <= local + (span - HALF))
        bias = jnp.where(allowed, 0.0, NEG)

        @pl.loop(0, heads // GROUP)
        def _(group):
            base = group * GROUP
            query = q_ref[0, pl.ds(base, GROUP), pl.ds(first, HALF)].reshape(
                GROUP * HALF, head_dim
            )
            score = right_times(query, keys).reshape(GROUP, HALF, span) + bias[None]
            peak = jnp.max(score, axis=-1, keepdims=True) * factor
            weights = jnp.exp2(score * factor - peak).astype(jnp.bfloat16)
            both = matmul(weights.reshape(GROUP * HALF, span), values)
            total = both[:, head_dim:]
            result = (both[:, :head_dim] / total).astype(jnp.bfloat16)
            o_ref[0, pl.ds(base, GROUP), pl.ds(first, HALF)] = result.reshape(
                GROUP, HALF, head_dim
            )
            log_total = jnp.log2(total) + peak.reshape(GROUP * HALF, 1)
            lse_ref[0, half, group] = log_total.T[:8]


def attend(query, pairs, low, scale):
    seqs, heads, block, head_dim = query.shape
    span = pairs.shape[1]
    return pl.pallas_call(
        functools.partial(attend_kernel, scale),
        grid=(seqs,),
        in_specs=[
            row((1, heads, block, head_dim), lambda b: (b, 0, 0, 0)),
            row((1, span, 2 * head_dim), lambda b: (b, 0, 0)),
            row((1, block, 1), lambda b: (b, 0, 0)),
        ],
        out_specs=[
            row((1, heads, block, head_dim), lambda b: (b, 0, 0, 0)),
            row(
                (1, block // HALF, heads // GROUP, 8, GROUP * HALF), lambda b: (b, 0, 0, 0, 0)
            ),
        ],
        out_shape=[
            jax.ShapeDtypeStruct(query.shape, jnp.bfloat16),
            jax.ShapeDtypeStruct(
                (seqs, block // HALF, heads // GROUP, 8, GROUP * HALF), jnp.float32
            ),
        ],
        compiler_params=params(),
        name="attend",
    )(query, pairs, low[:, :, None])


def attend_back_kernel(
    scale, q_ref, kv_ref, low_ref, lse_ref, o_ref, do_ref, cos_ref, sin_ref, dq_ref, dkv_ref
):
    heads, block, head_dim = q_ref.shape[1:]
    span = kv_ref.shape[1] - (block - HALF)
    factor = scale * LOG2E
    lanes = GROUP * HALF
    dkv_ref[...] = jnp.zeros_like(dkv_ref)

    @pl.loop(0, block // HALF)
    def _(half):
        first = pl.multiple_of(half * HALF, HALF)
        window = pl.ds(first, span)
        keys = kv_ref[0, window, :head_dim]
        values = kv_ref[0, window, head_dim:]
        keys_t = keys.T
        place = lax.broadcasted_iota(jnp.int32, (span, HALF), 0)
        local = lax.broadcasted_iota(jnp.int32, (span, HALF), 1)
        low = low_ref[0, :, pl.ds(first, HALF)] - first
        allowed = (place >= low) & (place <= local + (span - HALF))
        bias = jnp.where(allowed, 0.0, NEG)
        bias = jnp.concatenate([bias] * GROUP, axis=1)
        cosine = cos_ref[pl.ds(first, HALF)][None]
        sine = sin_ref[pl.ds(first, HALF)][None]

        @pl.loop(0, heads // GROUP)
        def _(group):
            base = group * GROUP
            here = (0, pl.ds(base, GROUP), pl.ds(first, HALF))
            query = q_ref[here].reshape(lanes, head_dim)
            grad = do_ref[here].reshape(lanes, head_dim)
            mixed = o_ref[here].reshape(lanes, head_dim)
            product = grad.astype(jnp.float32) * mixed.astype(jnp.float32)
            delta = jnp.sum(product.T, axis=0, keepdims=True)
            lse = lse_ref[0, half, group][0:1]
            score = right_times(keys, query)
            weights = jnp.exp2((score * factor - lse) + bias)
            low_weights = weights.astype(jnp.bfloat16)
            dkv_ref[0, window, head_dim:] += matmul(low_weights, grad)
            slope = right_times(values, grad)
            slope = (weights * (slope - delta)).astype(jnp.bfloat16)
            dkv_ref[0, window, :head_dim] += matmul(slope, query) * scale
            dq = (matmul(keys_t, slope).T * scale).reshape(GROUP, HALF, head_dim)
            turned = pltpu.roll(dq.reshape(lanes, head_dim), head_dim // 2, 1)
            dq = dq * cosine - turned.reshape(GROUP, HALF, head_dim) * sine
            dq_ref[here] = dq.astype(jnp.bfloat16)


def attend_back(query, pairs, low, lse, mixed, grad, cosine, sine, scale):
    seqs, heads, block, head_dim = query.shape
    span = pairs.shape[1]
    per_head = row((1, heads, block, head_dim), lambda b: (b, 0, 0, 0))
    table = row((block, head_dim), lambda b: (b, 0))
    return pl.pallas_call(
        functools.partial(attend_back_kernel, scale),
        grid=(seqs,),
        in_specs=[
            per_head,
            row((1, span, 2 * head_dim), lambda b: (b, 0, 0)),
            row((1, 1, block), lambda b: (b, 0, 0)),
            row((1,) + lse.shape[1:], lambda b: (b, 0, 0, 0, 0)),
            per_head,
            per_head,
            table,
            table,
        ],
        out_specs=[per_head, row((1, span, 2 * head_dim), lambda b: (b, 0, 0))],
        out_shape=[
            jax.ShapeDtypeStruct(query.shape, jnp.bfloat16),
            jax.ShapeDtypeStruct(pairs.shape, jnp.float32),
        ],
        compiler_params=params(),
        name="attend_back",
    )(query, pairs, low[:, None, :], lse, mixed, grad, cosine, sine)


def gelu_parts(gate):
    cube = 0.044715 * gate * gate
    bend = jnp.tanh(0.7978845608028654 * gate * (1.0 + cube))
    half = 0.5 * (1.0 + bend)
    value = gate * half
    slope = half + gate * (half * (1.0 - bend)) * (0.7978845608028654 * (1.0 + 3.0 * cube))
    return value, slope


def feed_kernel(
    start,
    x_ref,
    o_ref,
    g_ref,
    gains_ref,
    full_ref,
    y_ref,
    dx_ref,
    do_ref,
    dgain_ref,
    dout_ref,
    dff_ref,
    outw,
    ff,
    mixed,
    normed,
    normed_t,
    g_t,
    y_acc,
    dh_acc,
    m_all,
    dgate_all,
    dup_all,
    grads,
    in_sem,
    out_sem,
):
    rows, width = x_ref.shape
    seqs, heads, block, head_dim = o_ref.shape
    step = ff.shape[2] // 3
    tiles = rows // ROW_TILE
    gain = gains_ref[1:2]

    def load(chunk):
        return pltpu.make_async_copy(
            full_ref.at[:, pl.ds(start + width + chunk * 3 * step, 3 * step)],
            ff.at[chunk % 2],
            in_sem.at[chunk % 2],
        )

    out_load = pltpu.make_async_copy(full_ref.at[:, pl.ds(start, width)], outw, in_sem.at[2])
    out_load.start()
    load(0).start()
    out_load.wait()

    def here(tile):
        return pl.ds(pl.multiple_of(tile * ROW_TILE, ROW_TILE), ROW_TILE)

    @pl.loop(0, tiles)
    def _(tile):
        part = here(tile)
        attended = jnp.concatenate([o_ref[tile, h] for h in range(heads)], axis=1)
        x1 = x_ref[part].astype(jnp.float32) + right_times(attended, outw[...])
        mixed[part] = x1
        y_acc[part] = x1
        low = (x1 * inverse_rms(x1) * gain).astype(jnp.bfloat16)
        normed[part] = low
        normed_t[:, part] = low.T
        g_t[:, part] = g_ref[part].T
        dh_acc[part] = jnp.zeros((ROW_TILE, width), jnp.float32)

    for chunk in range(FF_CHUNKS):
        slot = chunk % 2
        load(chunk).wait()
        if chunk + 1 < FF_CHUNKS:
            load(chunk + 1).start()

        @pl.loop(0, tiles)
        def _(tile):
            part = here(tile)
            low, grad = normed[part], g_ref[part]
            gate = matmul(low, ff[slot, :, :step])
            up_part = matmul(low, ff[slot, :, step : 2 * step])
            dm = matmul(grad, ff[slot, :, 2 * step :])
            value, slope = gelu_parts(gate)
            m = (value * up_part).astype(jnp.bfloat16)
            dgate = (dm * up_part * slope).astype(jnp.bfloat16)
            dup = (dm * value).astype(jnp.bfloat16)
            m_all[part], dgate_all[part], dup_all[part] = m, dgate, dup
            y_acc[part] += right_times(m, ff[slot, :, 2 * step :])
            dh_acc[part] += right_times(dgate, ff[slot, :, :step]) + right_times(
                dup, ff[slot, :, step : 2 * step]
            )

        if chunk >= 2:
            pltpu.make_async_copy(grads.at[slot], dff_ref.at[chunk - 2], out_sem.at[slot]).wait()

        @pl.loop(0, width // ROW_TILE)
        def _(tile):
            part = here(tile)
            grads[slot, part, :step] = matmul(normed_t[part], dgate_all[...]).astype(jnp.bfloat16)
            grads[slot, part, step : 2 * step] = matmul(normed_t[part], dup_all[...]).astype(
                jnp.bfloat16
            )
            grads[slot, part, 2 * step :] = matmul(g_t[part], m_all[...]).astype(jnp.bfloat16)

        pltpu.make_async_copy(grads.at[slot], dff_ref.at[chunk], out_sem.at[slot]).start()

    dgain_ref[...] = jnp.zeros_like(dgain_ref)

    @pl.loop(0, tiles)
    def _(tile):
        part = here(tile)
        y_ref[part] = y_acc[part].astype(jnp.bfloat16)
        x1, dh = mixed[part], dh_acc[part]
        scale = inverse_rms(x1)
        dgain_ref[0:1] += jnp.sum(dh * x1 * scale, axis=0, keepdims=True)
        dx = g_ref[part].astype(jnp.float32) + rms_back(x1, scale, gain, dh)
        dx_ref[part] = dx
        low = dx.astype(jnp.bfloat16)
        g_t[:, part] = low.T
        back = matmul(low, outw[...]).astype(jnp.bfloat16)
        for h in range(heads):
            do_ref[tile, h] = back[:, h * head_dim : (h + 1) * head_dim]

    @pl.loop(0, width // ROW_TILE)
    def _(tile):
        part = here(tile)
        for h in range(heads):
            if h % 2 == 0:
                for s in range(seqs):
                    pair = jnp.concatenate([o_ref[s, h], o_ref[s, h + 1]], axis=1)
                    term = matmul(g_t[part, s * block : (s + 1) * block], pair)
                    total = term if s == 0 else total + term
                dout_ref[part, h * head_dim : (h + 2) * head_dim] = total.astype(jnp.bfloat16)

    for chunk in (FF_CHUNKS - 2, FF_CHUNKS - 1):
        pltpu.make_async_copy(grads.at[chunk % 2], dff_ref.at[chunk], out_sem.at[chunk % 2]).wait()


def feed(x, mixed_heads, grad, gains, full, start, hidden):
    rows, width = x.shape
    step = hidden // FF_CHUNKS
    low = jnp.bfloat16
    return pl.pallas_call(
        functools.partial(feed_kernel, start),
        in_specs=[vmem(), vmem(), vmem(), vmem(), hbm()],
        out_specs=[vmem(), vmem(), vmem(), vmem(), vmem(), hbm()],
        out_shape=[
            jax.ShapeDtypeStruct((rows, width), low),
            jax.ShapeDtypeStruct((rows, width), jnp.float32),
            jax.ShapeDtypeStruct(mixed_heads.shape, low),
            jax.ShapeDtypeStruct((8, width), jnp.float32),
            jax.ShapeDtypeStruct((width, width), low),
            jax.ShapeDtypeStruct((FF_CHUNKS, width, 3 * step), low),
        ],
        scratch_shapes=[
            pltpu.VMEM((width, width), low),
            pltpu.VMEM((2, width, 3 * step), low),
            pltpu.VMEM((rows, width), jnp.float32),
            pltpu.VMEM((rows, width), low),
            pltpu.VMEM((width, rows), low),
            pltpu.VMEM((width, rows), low),
            pltpu.VMEM((rows, width), jnp.float32),
            pltpu.VMEM((rows, width), jnp.float32),
            pltpu.VMEM((rows, step), low),
            pltpu.VMEM((rows, step), low),
            pltpu.VMEM((rows, step), low),
            pltpu.VMEM((2, width, 3 * step), low),
            pltpu.SemaphoreType.DMA((3,)),
            pltpu.SemaphoreType.DMA((2,)),
        ],
        compiler_params=params(),
        name="feed",
    )(x, mixed_heads, grad, gains, full)


def finish_kernel(x_ref, h_ref, dq_ref, dkv_ref, gains_ref, dx_ref, w_ref, dw_ref, dxo_ref, dgain_ref, h_t, dall):
    rows, width = x_ref.shape
    seqs, heads, block, head_dim = dq_ref.shape
    gain = gains_ref[0:1]
    dgain_ref[...] = jnp.zeros_like(dgain_ref)

    @pl.loop(0, seqs)
    def _(tile):
        part = pl.ds(pl.multiple_of(tile * block, block), block)
        h_t[:, part] = h_ref[part].T
        grad = jnp.concatenate([dq_ref[tile, h] for h in range(heads)] + [dkv_ref[tile]], axis=1)
        dall[part] = grad
        dh = right_times(grad, w_ref[:, : width + 2 * head_dim])
        x = x_ref[part].astype(jnp.float32)
        scale = inverse_rms(x)
        dgain_ref[0:1] += jnp.sum(dh * x * scale, axis=0, keepdims=True)
        dxo_ref[part] = (dx_ref[part] + rms_back(x, scale, gain, dh)).astype(jnp.bfloat16)

    @pl.loop(0, width // ROW_TILE)
    def _(tile):
        part = pl.ds(pl.multiple_of(tile * ROW_TILE, ROW_TILE), ROW_TILE)
        dw_ref[part] = matmul(h_t[part], dall[...]).astype(jnp.bfloat16)


def finish(x, normed, dq, dkv, gains, dx, weights):
    rows, width = x.shape
    columns = width + dkv.shape[2]
    return pl.pallas_call(
        finish_kernel,
        in_specs=[vmem()] * 7,
        out_specs=[vmem()] * 3,
        out_shape=[
            jax.ShapeDtypeStruct((width, columns), jnp.bfloat16),
            jax.ShapeDtypeStruct((rows, width), jnp.bfloat16),
            jax.ShapeDtypeStruct((8, width), jnp.float32),
        ],
        scratch_shapes=[
            pltpu.VMEM((width, rows), jnp.bfloat16),
            pltpu.VMEM((rows, columns), jnp.bfloat16),
        ],
        compiler_params=params(),
        name="finish",
    )(x, normed, dq, dkv, gains, dx, weights)


def columns_of(width, head_dim, heads, hidden):
    attention = width + 2 * head_dim + 128
    chunks = [(0, 640, attention), (attention, attention + width // 2, attention + width)]
    start = attention + width
    step = 3 * hidden // FF_CHUNKS
    for _ in range(FF_CHUNKS):
        chunks.append((start, start + step // 2, start + step))
        start += step
    return chunks


def stack_ff(gate, up_part, down_t):
    rows, hidden = gate.shape
    parts = [p.reshape(rows, FF_CHUNKS, hidden // FF_CHUNKS) for p in (gate, up_part, down_t)]
    return jnp.stack(parts, axis=2).reshape(rows, 3 * hidden)


def unstack_ff(stacked):
    rows, hidden = stacked.shape[0], stacked.shape[1] // 3
    parts = stacked.reshape(rows, FF_CHUNKS, 3, hidden // FF_CHUNKS)
    return [parts[:, :, i].reshape(rows, hidden) for i in range(3)]


def shifted(value, axis, steps):
    count = lax.axis_size(axis)
    initial, last = (max(0, -steps), min(count, count - steps))
    return lax.ppermute(value, axis, [(source, source + steps) for source in range(initial, last)])


def on_device(
    own_links,
    tokens,
    segments,
    cotangent,
    first_gain,
    query_weight,
    key_weight,
    value_weight,
    out_weight,
    second_gain,
    gate_weight,
    up_weight,
    down_weight,
):
    seqs, block_len, width = tokens.shape
    head_dim = key_weight.shape[1]
    heads = query_weight.shape[1] // head_dim
    hidden_width = gate_weight.shape[1]
    shard_rows = first_gain.shape[0]
    reach = (WINDOW - 1 + block_len - 1) // block_len
    span = (reach + 1) * block_len
    scale = head_dim ** (-0.5)
    rows = seqs * block_len
    chunks = columns_of(width, head_dim, heads, hidden_width)

    gains = jnp.zeros((shard_rows, 128), first_gain.dtype)
    gains = gains.at[:, 0].set(first_gain).at[:, 1].set(second_gain)
    shard = jnp.concatenate(
        [
            query_weight,
            key_weight,
            value_weight,
            gains,
            out_weight.T,
            stack_ff(gate_weight, up_weight, down_weight.T),
        ],
        axis=1,
    )
    if own_links:
        full = gather_all(shard, chunks)
    else:
        full = lax.all_gather(shard, ("batch", "seq"), axis=0, tiled=True)
    all_segments = lax.all_gather(segments, "seq", axis=1, tiled=True)
    starts = jnp.sum(all_segments[:, None, :] < segments[:, :, None], axis=-1, dtype=jnp.int32)
    query_place = jnp.arange(block_len, dtype=jnp.int32) + lax.axis_index("seq") * block_len
    low = jnp.maximum(starts, query_place[None, :] - (WINDOW - 1))
    low = low - (query_place[0] - reach * block_len)
    cosine, sine = tables((query_place[None, :] - starts).reshape(-1), head_dim)

    inputs = tokens.reshape(rows, width)
    qkv_weights = full[:, : chunks[0][2]]
    normed, query, own_pairs, gains = project(
        inputs, cosine, sine, qkv_weights, seqs, heads, head_dim
    )
    pieces = [shifted(own_pairs, "seq", distance) for distance in range(reach, 0, -1)]
    window_pairs = jnp.concatenate(pieces + [own_pairs], axis=1)
    mixed, log_total = attend(query, window_pairs, low, scale)
    output, grad_mixed, grad_heads, grad_gain_two, grad_out_t, grad_ff = feed(
        inputs, mixed, cotangent.reshape(rows, width), gains, full, chunks[1][0], hidden_width
    )
    grad_query, grad_pairs = attend_back(
        query, window_pairs, low, log_total, mixed, grad_heads, cosine, sine, scale
    )
    own_grad = grad_pairs[:, reach * block_len :]
    for distance in range(1, reach + 1):
        piece = grad_pairs[:, (reach - distance) * block_len : (reach - distance + 1) * block_len]
        own_grad = own_grad + shifted(piece.astype(jnp.bfloat16), "seq", -distance).astype(
            piece.dtype
        )
    grad_key = own_grad[..., :head_dim].reshape(rows, head_dim)
    grad_key = grad_key * cosine - jnp.roll(grad_key, head_dim // 2, axis=1) * sine
    grad_kv = jnp.concatenate(
        [grad_key.reshape(seqs, block_len, head_dim), own_grad[..., head_dim:]], axis=-1
    ).astype(jnp.bfloat16)
    grad_qkv_w, grad_input, grad_gain_one = finish(
        inputs, normed, grad_query, grad_kv, gains, grad_mixed, qkv_weights
    )
    grad_gains = jnp.zeros((width, 128), jnp.bfloat16)
    grad_gains = grad_gains.at[:, 0].set(grad_gain_one[0].astype(jnp.bfloat16))
    grad_gains = grad_gains.at[:, 1].set(grad_gain_two[0].astype(jnp.bfloat16))
    grads = jnp.concatenate([grad_qkv_w, grad_gains, grad_out_t] + list(grad_ff), axis=1)
    if own_links:
        share = scatter_all(grads, shard_rows, chunks)
    else:
        share = lax.psum_scatter(grads, ("batch", "seq"), scatter_dimension=0, tiled=True)
        share = share.astype(jnp.float32)
    share_gate, share_up, share_down_t = unstack_ff(share[:, chunks[2][0] :])
    return (
        output.reshape(tokens.shape),
        grad_input.reshape(tokens.shape),
        share[:, width + 2 * head_dim],
        share[:, :width],
        share[:, width : width + head_dim],
        share[:, width + head_dim : width + 2 * head_dim],
        share[:, chunks[1][0] : chunks[1][2]].T,
        share[:, width + 2 * head_dim + 1],
        share_gate,
        share_up,
        share_down_t.T,
    )


def solution(mesh):
    both = ("batch", "seq")
    rows_split, columns_split = P(both, None), P(None, both)
    tokens_split, gain_split = P("batch", "seq", None), P(both)
    weights = (
        gain_split,
        rows_split,
        rows_split,
        rows_split,
        columns_split,
        gain_split,
        rows_split,
        rows_split,
        columns_split,
    )
    in_specs = (tokens_split, P("batch", "seq"), tokens_split) + weights
    out_specs = (tokens_split, tokens_split) + weights
    own_links = (mesh.shape["batch"], mesh.shape["seq"]) == (4, 8)
    return jax.shard_map(
        functools.partial(on_device, own_links),
        mesh=mesh,
        in_specs=in_specs,
        out_specs=out_specs,
        check_vma=False,
    )
```

```python
import functools

import jax
import jax.numpy as jnp
from jax import lax
from jax.experimental import pallas as pl
from jax.experimental.pallas import tpu as pltpu
from jax.sharding import PartitionSpec as P

WINDOW = 1024
FF_CHUNKS = 6
SCATTERED = 4
MESH_ID = pl.DeviceIdType.MESH
MIB = 1 << 20


def tables(positions, head_dim):
    inverse = 10000.0 ** (-2.0 * jnp.arange(head_dim // 2, dtype=jnp.float32) / head_dim)
    angle = positions.astype(jnp.float32)[:, None] * inverse[None, :]
    cosine, sine = jnp.cos(angle), jnp.sin(angle)
    return (
        jnp.concatenate([cosine, cosine], axis=-1),
        jnp.concatenate([-sine, sine], axis=-1),
    )


def matmul(left, right):
    return jnp.dot(left, right, preferred_element_type=jnp.float32)


def right_times(left, right):
    return lax.dot_general(
        left, right, (((1,), (1,)), ((), ())), preferred_element_type=jnp.float32
    )


def place():
    batch, seq = lax.axis_index("batch"), lax.axis_index("seq")
    return batch // 2, lax.rem(batch, 2), seq // 2, lax.rem(seq, 2)


def device(x, c, z, y):
    return (x * 2 + c, z * 2 + y)


def greet(partners):
    barrier = pltpu.get_barrier_semaphore()
    for partner in partners:
        pl.semaphore_signal(barrier, inc=1, device_id=partner, device_id_type=MESH_ID)
    pl.semaphore_wait(barrier, len(partners))


def neighbours():
    x, c, z, y = place()
    return [
        device(x, c, lax.rem(z + 1, 4), y),
        device(x, c, lax.rem(z + 2, 4), y),
        device(x, c, lax.rem(z + 3, 4), y),
        device(1 - x, c, z, y),
        device(x, c, z, 1 - y),
        device(x, 1 - c, z, y),
    ]


def remote(source, target, send_sem, recv_sem, partner):
    return pltpu.make_async_remote_copy(
        src_ref=source,
        dst_ref=target,
        send_sem=send_sem,
        recv_sem=recv_sem,
        device_id=partner,
        device_id_type=MESH_ID,
    )


class Gather:
    STEPS = 5
    SEMS = 8

    def __init__(self, shard, full, sems, local_sems, chunks):
        self.shard, self.full, self.sems, self.local_sems = shard, full, sems, local_sems
        self.chunks = chunks

    @staticmethod
    def scratch(count):
        return [
            pltpu.SemaphoreType.DMA((2, count, Gather.SEMS)),
            pltpu.SemaphoreType.DMA((count,)),
        ]

    def keep(self, chunk):
        x, c, z, y = place()
        start, _, end = self.chunks[chunk]
        whole = pl.ds(start, end - start)
        return pltpu.make_async_copy(
            self.shard.at[:, whole], self.full.at[x, c, z, y, :, whole], self.local_sems.at[chunk]
        )

    def copy(self, chunk, slot):
        x, c, z, y = place()
        start, middle, end = self.chunks[chunk]
        full = self.full
        whole = pl.ds(start, end - start)
        first, second = pl.ds(start, middle - start), pl.ds(middle, end - middle)
        if slot < 3:
            source, target = self.shard.at[:, whole], full.at[x, c, z, y, :, whole]
            partner = device(x, c, lax.rem(z + slot + 1, 4), y)
        else:
            source, partner = {
                3: (full.at[x, c, :, y, :, first], device(x, c, z, 1 - y)),
                4: (full.at[x, c, :, y, :, second], device(1 - x, c, z, y)),
                5: (full.at[x, c, :, :, :, first], device(1 - x, c, z, y)),
                6: (full.at[:, c, :, y, :, second], device(x, c, z, 1 - y)),
                7: (full.at[:, c, :, :, :, whole], device(x, 1 - c, z, y)),
            }[slot]
            target = source
        return remote(
            source, target, self.sems.at[0, chunk, slot], self.sems.at[1, chunk, slot], partner
        )

    def step(self, number, chunk):
        if number == 0:
            self.keep(chunk).start()
            for slot in (0, 1, 2):
                self.copy(chunk, slot).start()
        elif number == 1:
            self.keep(chunk).wait()
            for slot in (0, 1, 2):
                self.copy(chunk, slot).wait_recv()
            self.copy(chunk, 3).start()
            self.copy(chunk, 4).start()
        elif number == 2:
            self.copy(chunk, 3).wait_recv()
            self.copy(chunk, 5).start()
            self.copy(chunk, 4).wait_recv()
            self.copy(chunk, 6).start()
        elif number == 3:
            self.copy(chunk, 5).wait_recv()
            self.copy(chunk, 6).wait_recv()
            self.copy(chunk, 7).start()
        else:
            self.copy(chunk, 7).wait_recv()
            for slot in range(self.SEMS):
                self.copy(chunk, slot).wait_send()

    def ticks(self, chunks):
        chunks = list(chunks)
        return [
            [(n, chunks[t - n]) for n in reversed(range(self.STEPS)) if 0 <= t - n < len(chunks)]
            for t in range(len(chunks) + self.STEPS - 1)
        ]


class Windows:
    KINDS = 5

    def __init__(self, window, sems, block):
        self.window, self.sems, self.block = window, sems, block

    def rows(self, seq, distance):
        start = (4 - distance) * self.block
        return self.window.at[seq, pl.ds(start, self.block)]

    def copy(self, kind, seq):
        x, c, z, y = place()
        down, over = device(x, c, lax.rem(z + 1, 4), y), device(x, c, z, 1 - y)
        source, target, partner = {
            0: (0, 2, down),
            1: (2, 4, down),
            2: (0, 1, over),
            3: (2, 3 - 2 * y, over),
            4: (4, 3, over),
        }[kind]
        return remote(
            self.rows(seq, source),
            self.rows(seq, target),
            self.sems.at[0, kind, seq],
            self.sems.at[1, kind, seq],
            partner,
        )

    def sends(self, kind):
        _, _, z, y = place()
        return {0: z < 3, 1: (z > 0) & (z < 3), 2: y == 0, 3: z > 0, 4: (z > 1) & (y == 1)}[kind]

    def gets(self, kind):
        _, _, z, y = place()
        return {0: z > 0, 1: z > 1, 2: y == 1, 3: z > 0, 4: (z > 1) & (y == 0)}[kind]

    def start(self, kind, seq):
        pl.when(self.sends(kind))(lambda: self.copy(kind, seq).start())

    def wait(self, kind, seq):
        pl.when(self.gets(kind))(lambda: self.copy(kind, seq).wait_recv())

    def own(self, seq):
        self.start(0, seq)
        self.start(2, seq)

    def once(self, seq):
        self.wait(0, seq)
        self.start(1, seq)
        self.start(3, seq)

    def twice(self, seq):
        self.wait(1, seq)
        self.start(4, seq)

    def all(self, seq):
        for kind in (2, 3, 4):
            self.wait(kind, seq)

    def drain(self, seq):
        for kind in range(self.KINDS):
            pl.when(self.sends(kind))(lambda: self.copy(kind, seq).wait_send())


class Scatter:
    SEMS = 8

    def __init__(self, plans, buffers, sems):
        self.plans, self.buffers, self.sems = plans, buffers, sems

    @staticmethod
    def scratch(widths, rows):
        out = []
        for n in widths:
            h = n // 256 * 128
            low = jnp.bfloat16
            out += [
                pltpu.VMEM((2, 4, 2, rows, n), low),
                pltpu.VMEM((4, 2, rows, h), low),
                pltpu.VMEM((2, 4, rows, n - h), low),
                pltpu.VMEM((4, rows, h), low),
                pltpu.VMEM((4, rows, n - h), low),
                pltpu.VMEM((3, rows, n), low),
            ]
        return out + [pltpu.SemaphoreType.DMA((2, max(1, len(widths)), Scatter.SEMS))]

    BUFFERS = 6

    def copy(self, chunk, slot):
        x, c, z, y = place()
        source = self.plans[chunk][0]
        one, two_a, two_b, three_a, three_b, last = self.buffers[chunk]
        half = two_a.shape[-1]
        first, second = slice(0, half), slice(half, one.shape[-1])
        if slot >= 5:
            hop = slot - 4
            source, target = one.at[0, lax.rem(z + hop, 4), 0], last.at[hop - 1]
            partner = device(x, c, lax.rem(z + hop, 4), y)
        else:
            over_x, over_y = device(1 - x, c, z, y), device(x, c, z, 1 - y)
            source, target, partner = {
                0: lambda: (source.at[:, 1 - c], one, device(x, 1 - c, z, y)),
                1: lambda: (one.at[1 - x, :, :, :, first], two_a, over_x),
                2: lambda: (one.at[:, :, 1 - y, :, second], two_b, over_y),
                3: lambda: (two_a.at[:, 1 - y], three_a, over_y),
                4: lambda: (two_b.at[1 - x], three_b, over_x),
            }[slot]()
        return remote(
            source, target, self.sems.at[0, chunk, slot], self.sems.at[1, chunk, slot], partner
        )

    def load(self, chunk):
        _, c, _, _ = place()
        source, mine, sem, _ = self.plans[chunk]
        return pltpu.make_async_copy(source.at[:, c], mine, sem)

    def step(self, number, chunk):
        x, c, z, y = place()
        source, mine, _, result = self.plans[chunk]
        one, two_a, two_b, three_a, three_b, last = self.buffers[chunk]
        half = two_a.shape[-1]
        first, second = slice(0, half), slice(half, one.shape[-1])
        if number == 0:
            self.copy(chunk, 0).start()
            if mine is not None:
                self.load(chunk).start()
        elif number == 1:
            if mine is not None:
                self.load(chunk).wait()
            else:
                mine = source.at[:, c]
            self.copy(chunk, 0).wait_recv()
            for i in range(2):

                @pl.loop(0, 4)
                def _(j):
                    for k in range(2):
                        add_rows(one.at[i, j, k], mine.at[i, j, k])

            self.copy(chunk, 1).start()
            self.copy(chunk, 2).start()
            self.copy(chunk, 0).wait_send()
        elif number == 2:
            self.copy(chunk, 1).wait_recv()

            @pl.loop(0, 4)
            def _(j):
                for k in range(2):
                    add_rows(two_a.at[j, k], one.at[x, j, k, :, first])

            self.copy(chunk, 3).start()
            self.copy(chunk, 2).wait_recv()

            @pl.loop(0, 4)
            def _(j):
                for i in range(2):
                    add_rows(two_b.at[i, j], one.at[i, j, y, :, second])

            self.copy(chunk, 4).start()
        elif number == 3:
            self.copy(chunk, 1).wait_send()
            self.copy(chunk, 2).wait_send()
            self.copy(chunk, 3).wait_recv()
            self.copy(chunk, 4).wait_recv()

            @pl.loop(0, 4)
            def _(k):
                left = three_a[k].astype(jnp.float32) + two_a[k, y].astype(jnp.float32)
                right = three_b[k].astype(jnp.float32) + two_b[x, k].astype(jnp.float32)
                one[0, k, 0, :, first] = left.astype(one.dtype)
                one[0, k, 0, :, second] = right.astype(one.dtype)

            for slot in (5, 6, 7):
                self.copy(chunk, slot).start()
        else:
            total = one[0, z, 0].astype(jnp.float32)
            for slot in (5, 6, 7):
                self.copy(chunk, slot).wait_recv()
                total += last[slot - 5].astype(jnp.float32)
            result[...] = total
            for slot in (3, 4, 5, 6, 7):
                self.copy(chunk, slot).wait_send()


def add_rows(target, other):
    target[...] = (target[...].astype(jnp.float32) + other[...].astype(jnp.float32)).astype(
        target.dtype
    )


ROW_TILE = 256
LOG2E = 1.4426950408889634
NEG = -1e30


def row(block, index):
    return pl.BlockSpec(block, index)


def vmem():
    return pl.BlockSpec(memory_space=pltpu.VMEM)


def hbm():
    return pl.BlockSpec(memory_space=pl.ANY)


def params(**more):
    return pltpu.CompilerParams(vmem_limit_bytes=62 * MIB, **more)


def inverse_rms(values):
    return lax.rsqrt(jnp.mean(values * values, axis=-1, keepdims=True) + 1e-06)


def rms_back(values, scale, gain, grad):
    inner = jnp.mean(values * gain * grad, axis=-1, keepdims=True)
    return scale * gain * grad - values * (scale * scale * scale * inner)


def project_block(x_ref, cos_ref, sin_ref, w_ref, gain, ht_ref, q_ref, kv_ref):
    heads, _, head_dim = q_ref.shape
    width = heads * head_dim
    x = x_ref[...].astype(jnp.float32)
    normed = (x * inverse_rms(x) * gain).astype(jnp.bfloat16)
    ht_ref[...] = normed.T
    cosine, sine = cos_ref[...], sin_ref[...]

    def turn(u):
        return (u * cosine + pltpu.roll(u, head_dim // 2, 1) * sine).astype(jnp.bfloat16)

    for pair in range(heads // 2):
        both = matmul(normed, w_ref[:, 2 * pair * head_dim : (2 * pair + 2) * head_dim])
        q_ref[2 * pair] = turn(both[:, :head_dim])
        q_ref[2 * pair + 1] = turn(both[:, head_dim:])
    both = matmul(normed, w_ref[:, width : width + 2 * head_dim])
    kv_ref[:, :head_dim] = turn(both[:, :head_dim])
    kv_ref[:, head_dim:] = both[:, head_dim:].astype(jnp.bfloat16)


def gain_rows(w_ref, columns):
    return w_ref[:, columns:].astype(jnp.float32).T[:8]


def project_kernel(x_ref, cos_ref, sin_ref, w_ref, ht_ref, q_ref, kv_ref, gains_ref):
    width = x_ref.shape[1]
    gains_ref[...] = gain_rows(w_ref, width + kv_ref.shape[2])
    project_block(
        x_ref, cos_ref, sin_ref, w_ref, gains_ref[0:1], ht_ref, q_ref.at[0], kv_ref.at[0]
    )


def project(x, cosine, sine, weights, seqs, heads, head_dim):
    rows, width = x.shape
    block = rows // seqs
    return pl.pallas_call(
        project_kernel,
        grid=(seqs,),
        in_specs=[
            row((block, width), lambda b: (b, 0)),
            row((block, head_dim), lambda b: (b, 0)),
            row((block, head_dim), lambda b: (b, 0)),
            row(weights.shape, lambda b: (0, 0)),
        ],
        out_specs=[
            row((width, block), lambda b: (0, b)),
            row((1, heads, block, head_dim), lambda b: (b, 0, 0, 0)),
            row((1, block, 2 * head_dim), lambda b: (b, 0, 0)),
            row((8, width), lambda b: (0, 0)),
        ],
        out_shape=[
            jax.ShapeDtypeStruct((width, rows), jnp.bfloat16),
            jax.ShapeDtypeStruct((seqs, heads, block, head_dim), jnp.bfloat16),
            jax.ShapeDtypeStruct((seqs, block, 2 * head_dim), jnp.bfloat16),
            jax.ShapeDtypeStruct((8, width), jnp.float32),
        ],
        compiler_params=params(),
        name="project",
    )(x, cosine, sine, weights)


HALF = 128
GROUP = 4


def attend_half(scale, half, q_ref, kv_ref, low_ref, o_ref, lse_ref):
    heads, block, head_dim = q_ref.shape
    span = kv_ref.shape[0] - (block - HALF)
    factor = scale * LOG2E
    first = half * HALF
    keys = kv_ref[first : first + span, :head_dim]
    values = kv_ref[first : first + span, head_dim:]
    values = jnp.concatenate([values, jnp.ones_like(values)], axis=1)
    place = lax.broadcasted_iota(jnp.int32, (HALF, span), 1)
    local = lax.broadcasted_iota(jnp.int32, (HALF, span), 0)
    low = low_ref[first : first + HALF] - first
    allowed = (place >= low) & (place <= local + (span - HALF))
    bias = jnp.where(allowed, 0.0, NEG)

    @pl.loop(0, heads // GROUP)
    def _(group):
        base = group * GROUP
        query = q_ref[pl.ds(base, GROUP), first : first + HALF].reshape(GROUP * HALF, head_dim)
        score = right_times(query, keys).reshape(GROUP, HALF, span) + bias[None]
        peak = jnp.max(score, axis=-1, keepdims=True) * factor
        weights = jnp.exp2(score * factor - peak).astype(jnp.bfloat16)
        both = matmul(weights.reshape(GROUP * HALF, span), values)
        total = both[:, head_dim:]
        result = (both[:, :head_dim] / total).astype(jnp.bfloat16)
        o_ref[pl.ds(base, GROUP), first : first + HALF] = result.reshape(GROUP, HALF, head_dim)
        log_total = jnp.log2(total) + peak.reshape(GROUP * HALF, 1)
        lse_ref[half, group] = log_total.T[:8]


def attend_kernel(scale, q_ref, kv_ref, low_ref, o_ref, lse_ref):
    for half in range(q_ref.shape[2] // HALF):
        attend_half(
            scale, half, q_ref.at[0], kv_ref.at[0], low_ref.at[0], o_ref.at[0], lse_ref.at[0]
        )


def attend(query, pairs, low, scale):
    seqs, heads, block, head_dim = query.shape
    span = pairs.shape[1]
    return pl.pallas_call(
        functools.partial(attend_kernel, scale),
        grid=(seqs,),
        in_specs=[
            row((1, heads, block, head_dim), lambda b: (b, 0, 0, 0)),
            row((1, span, 2 * head_dim), lambda b: (b, 0, 0)),
            row((1, block, 1), lambda b: (b, 0, 0)),
        ],
        out_specs=[
            row((1, heads, block, head_dim), lambda b: (b, 0, 0, 0)),
            row(
                (1, block // HALF, heads // GROUP, 8, GROUP * HALF), lambda b: (b, 0, 0, 0, 0)
            ),
        ],
        out_shape=[
            jax.ShapeDtypeStruct(query.shape, jnp.bfloat16),
            jax.ShapeDtypeStruct(
                (seqs, block // HALF, heads // GROUP, 8, GROUP * HALF), jnp.float32
            ),
        ],
        compiler_params=params(),
        name="attend",
    )(query, pairs, low[:, :, None])


def attend_back_half(
    scale, half, q_ref, kv_ref, low_ref, lse_ref, o_ref, do_ref, cos_ref, sin_ref, put_dq, dkv_ref
):
    heads, block, head_dim = q_ref.shape
    span = kv_ref.shape[0] - (block - HALF)
    factor = scale * LOG2E
    lanes = GROUP * HALF
    first = half * HALF
    window = slice(first, first + span)
    keys, values = kv_ref[window, :head_dim], kv_ref[window, head_dim:]
    keys_t = keys.T
    place = lax.broadcasted_iota(jnp.int32, (span, HALF), 0)
    local = lax.broadcasted_iota(jnp.int32, (span, HALF), 1)
    low = low_ref[:, first : first + HALF] - first
    allowed = (place >= low) & (place <= local + (span - HALF))
    bias = jnp.where(allowed, 0.0, NEG)
    bias = jnp.concatenate([bias] * GROUP, axis=1)
    cosine = cos_ref[first : first + HALF][None]
    sine = sin_ref[first : first + HALF][None]

    @pl.loop(0, heads // GROUP)
    def _(group):
        base = group * GROUP
        here = (pl.ds(base, GROUP), slice(first, first + HALF))
        query = q_ref[here].reshape(lanes, head_dim)
        grad = do_ref[here].reshape(lanes, head_dim)
        mixed = o_ref[here].reshape(lanes, head_dim)
        product = grad.astype(jnp.float32) * mixed.astype(jnp.float32)
        delta = jnp.sum(product.T, axis=0, keepdims=True)
        lse = lse_ref[half, group][0:1]
        score = right_times(keys, query)
        weights = jnp.exp2((score * factor - lse) + bias)
        low_weights = weights.astype(jnp.bfloat16)
        dkv_ref[window, head_dim:] += matmul(low_weights, grad)
        slope = right_times(values, grad)
        slope = (weights * (slope - delta)).astype(jnp.bfloat16)
        dkv_ref[window, :head_dim] += matmul(slope, query) * scale
        dq = (matmul(keys_t, slope).T * scale).reshape(GROUP, HALF, head_dim)
        turned = pltpu.roll(dq.reshape(lanes, head_dim), head_dim // 2, 1)
        dq = dq * cosine - turned.reshape(GROUP, HALF, head_dim) * sine
        put_dq(base, first, dq.astype(jnp.bfloat16))


def attend_back_kernel(
    scale, q_ref, kv_ref, low_ref, lse_ref, o_ref, do_ref, cos_ref, sin_ref, dq_ref, dkv_ref
):
    dkv_ref[...] = jnp.zeros_like(dkv_ref)

    def put_dq(base, first, dq):
        dq_ref[0, pl.ds(base, GROUP), first : first + HALF] = dq

    for half in range(q_ref.shape[2] // HALF):
        attend_back_half(
            scale,
            half,
            q_ref.at[0],
            kv_ref.at[0],
            low_ref.at[0],
            lse_ref.at[0],
            o_ref.at[0],
            do_ref.at[0],
            cos_ref,
            sin_ref,
            put_dq,
            dkv_ref.at[0],
        )


def attend_back(query, pairs, low, lse, mixed, grad, cosine, sine, scale):
    seqs, heads, block, head_dim = query.shape
    span = pairs.shape[1]
    per_head = row((1, heads, block, head_dim), lambda b: (b, 0, 0, 0))
    table = row((block, head_dim), lambda b: (b, 0))
    return pl.pallas_call(
        functools.partial(attend_back_kernel, scale),
        grid=(seqs,),
        in_specs=[
            per_head,
            row((1, span, 2 * head_dim), lambda b: (b, 0, 0)),
            row((1, 1, block), lambda b: (b, 0, 0)),
            row((1,) + lse.shape[1:], lambda b: (b, 0, 0, 0, 0)),
            per_head,
            per_head,
            table,
            table,
        ],
        out_specs=[per_head, row((1, span, 2 * head_dim), lambda b: (b, 0, 0))],
        out_shape=[
            jax.ShapeDtypeStruct(query.shape, jnp.bfloat16),
            jax.ShapeDtypeStruct(pairs.shape, jnp.float32),
        ],
        compiler_params=params(),
        name="attend_back",
    )(query, pairs, low[:, None, :], lse, mixed, grad, cosine, sine)


def gelu_parts(gate):
    cube = 0.044715 * gate * gate
    bend = jnp.tanh(0.7978845608028654 * gate * (1.0 + cube))
    half = 0.5 * (1.0 + bend)
    value = gate * half
    slope = half + gate * (half * (1.0 - bend)) * (0.7978845608028654 * (1.0 + 3.0 * cube))
    return value, slope


def feed_kernel(own, scattered, x_ref, o_ref, g_ref, gains_ref, full_ref, *refs):
    y_ref, dx_ref, do_ref, dgain_ref, dout_ref, dff_ref = refs[:6]
    shares, refs = refs[6 : 6 + scattered], refs[6 + scattered :]
    outw, ff, mixed, normed, normed_t, g_t, y_acc, dh_acc, m_all, dgate_all, dup_all, grads = refs[
        :12
    ]
    in_sem, out_sem = refs[12:14]
    rows, width = g_ref.shape
    seqs, heads, block, head_dim = o_ref.shape
    step = ff.shape[2] // 3
    tiles = rows // ROW_TILE
    shard_rows = width // 32
    gain = gains_ref[1:2]
    if own:
        greet(neighbours())
        count = Scatter.BUFFERS
        buffers = [refs[14 + count * k : 14 + count * (k + 1)] for k in range(scattered)]
        plans = [(grads.at[k % 2], None, None, shares[k]) for k in range(scattered)]
        scatter = Scatter(plans, buffers, refs[14 + count * scattered])

    def advance(steps):
        for number, chunk in steps:
            if own and 0 <= chunk < scattered:
                scatter.step(number, chunk)

    def load(chunk):
        return pltpu.make_async_copy(
            full_ref.at[:, pl.ds(width + chunk * 3 * step, 3 * step)],
            ff.at[chunk % 2],
            in_sem.at[chunk % 2],
        )

    def store(chunk):
        return pltpu.make_async_copy(
            grads.at[chunk % 2], dff_ref.at[chunk - scattered], out_sem.at[chunk % 2]
        )

    out_load = pltpu.make_async_copy(full_ref.at[:, pl.ds(0, width)], outw, in_sem.at[2])
    out_load.start()
    load(0).start()
    x_load = pltpu.make_async_copy(x_ref, normed, in_sem.at[3])
    x_load.start()
    x_load.wait()
    out_load.wait()

    def here(tile):
        return pl.ds(pl.multiple_of(tile * ROW_TILE, ROW_TILE), ROW_TILE)

    @pl.loop(0, tiles)
    def _(tile):
        part = here(tile)
        attended = jnp.concatenate([o_ref[tile, h] for h in range(heads)], axis=1)
        x1 = normed[part].astype(jnp.float32) + right_times(attended, outw[...])
        mixed[part] = x1
        y_acc[part] = x1
        low = (x1 * inverse_rms(x1) * gain).astype(jnp.bfloat16)
        normed[part] = low
        normed_t[:, part] = low.T
        g_t[:, part] = g_ref[part].T
        dh_acc[part] = jnp.zeros((ROW_TILE, width), jnp.float32)

    for chunk in range(FF_CHUNKS):
        slot = chunk % 2
        load(chunk).wait()
        if chunk + 1 < FF_CHUNKS:
            load(chunk + 1).start()

        @pl.loop(0, tiles)
        def _(tile):
            part = here(tile)
            low, grad = normed[part], g_ref[part]
            gate = matmul(low, ff[slot, :, :step])
            up_part = matmul(low, ff[slot, :, step : 2 * step])
            dm = matmul(grad, ff[slot, :, 2 * step :])
            value, slope = gelu_parts(gate)
            m = (value * up_part).astype(jnp.bfloat16)
            dgate = (dm * up_part * slope).astype(jnp.bfloat16)
            dup = (dm * value).astype(jnp.bfloat16)
            m_all[part], dgate_all[part], dup_all[part] = m, dgate, dup
            y_acc[part] += right_times(m, ff[slot, :, 2 * step :])
            dh_acc[part] += right_times(dgate, ff[slot, :, :step]) + right_times(
                dup, ff[slot, :, step : 2 * step]
            )

        advance([(4, chunk - 3), (2, chunk - 2), (1, chunk - 1)])
        if chunk - 2 >= scattered:
            store(chunk - 2).wait()

        @pl.loop(0, width // ROW_TILE)
        def _(tile):
            part = here(tile)
            where = (slot, tile // 2, lax.rem(tile, 2))
            for i, (left, right) in enumerate(
                ((normed_t, dgate_all), (normed_t, dup_all), (g_t, m_all))
            ):
                value = matmul(left[part], right[...]).astype(jnp.bfloat16)
                grads[where + (slice(None),) * 3 + (slice(i * step, (i + 1) * step),)] = (
                    value.reshape(4, 2, ROW_TILE // 8, step)
                )

        advance([(3, chunk - 2), (0, chunk)])
        if chunk >= scattered:
            store(chunk).start()

    dgain_ref[...] = jnp.zeros_like(dgain_ref)
    advance([(4, FF_CHUNKS - 3), (2, FF_CHUNKS - 2), (1, FF_CHUNKS - 1)])

    @pl.loop(0, tiles)
    def _(tile):
        part = here(tile)
        normed[part] = y_acc[part].astype(jnp.bfloat16)
        x1, dh = mixed[part], dh_acc[part]
        scale = inverse_rms(x1)
        dgain_ref[0:1] += jnp.sum(dh * x1 * scale, axis=0, keepdims=True)
        dx = g_ref[part].astype(jnp.float32) + rms_back(x1, scale, gain, dh)
        mixed[part] = dx
        low = dx.astype(jnp.bfloat16)
        g_t[:, part] = low.T
        back = matmul(low, outw[...]).astype(jnp.bfloat16)
        for h in range(heads):
            do_ref[tile, h] = back[:, h * head_dim : (h + 1) * head_dim]

    outs = [
        pltpu.make_async_copy(normed, y_ref, in_sem.at[0]),
        pltpu.make_async_copy(mixed, dx_ref, in_sem.at[1]),
    ]
    for out in outs:
        out.start()
    advance([(3, FF_CHUNKS - 2)])

    @pl.loop(0, width // ROW_TILE)
    def _(tile):
        part = here(tile)
        for h in range(0, heads, 2):
            for s in range(seqs):
                pair = jnp.concatenate([o_ref[s, h], o_ref[s, h + 1]], axis=1)
                term = matmul(g_t[part, s * block : (s + 1) * block], pair)
                total = term if s == 0 else total + term
            ff[0, part, h * head_dim : (h + 2) * head_dim] = total.astype(jnp.bfloat16)

    outs.append(pltpu.make_async_copy(ff.at[0, :, pl.ds(0, width)], dout_ref, in_sem.at[2]))
    outs[-1].start()
    advance([(4, FF_CHUNKS - 2), (2, FF_CHUNKS - 1), (3, FF_CHUNKS - 1), (4, FF_CHUNKS - 1)])
    for chunk in range(max(scattered, FF_CHUNKS - 2), FF_CHUNKS):
        store(chunk).wait()
    for out in outs:
        out.wait()


def feed(own, scattered, x, mixed_heads, grad, gains, full, hidden):
    rows, width = x.shape
    step = hidden // FF_CHUNKS
    low = jnp.bfloat16
    chunk = (2, 2, 4, 2, width // 32, 3 * step)
    kept = FF_CHUNKS - scattered
    options = {"collective_id": 3, "has_side_effects": True} if own else {}
    return pl.pallas_call(
        functools.partial(feed_kernel, own, scattered),
        in_specs=[hbm(), vmem(), vmem(), vmem(), hbm()],
        out_specs=[hbm(), hbm(), vmem(), vmem(), hbm(), hbm()] + [vmem()] * scattered,
        out_shape=[
            jax.ShapeDtypeStruct((rows, width), low),
            jax.ShapeDtypeStruct((rows, width), jnp.float32),
            jax.ShapeDtypeStruct(mixed_heads.shape, low),
            jax.ShapeDtypeStruct((8, width), jnp.float32),
            jax.ShapeDtypeStruct((width, width), low),
            jax.ShapeDtypeStruct((kept,) + chunk, low),
        ]
        + [jax.ShapeDtypeStruct((width // 32, 3 * step), jnp.float32)] * scattered,
        scratch_shapes=[
            pltpu.VMEM((width, width), low),
            pltpu.VMEM((2, width, 3 * step), low),
            pltpu.VMEM((rows, width), jnp.float32),
            pltpu.VMEM((rows, width), low),
            pltpu.VMEM((width, rows), low),
            pltpu.VMEM((width, rows), low),
            pltpu.VMEM((rows, width), jnp.float32),
            pltpu.VMEM((rows, width), jnp.float32),
            pltpu.VMEM((rows, step), low),
            pltpu.VMEM((rows, step), low),
            pltpu.VMEM((rows, step), low),
            pltpu.VMEM((2,) + chunk, low),
            pltpu.SemaphoreType.DMA((4,)),
            pltpu.SemaphoreType.DMA((2,)),
        ]
        + (Scatter.scratch([3 * step] * scattered, width // 32) if own else []),
        compiler_params=params(**options),
        name="feed",
    )(x, mixed_heads, grad, gains, full)


def finish_rows(x, dx, grad, w_ref, gain):
    dh = right_times(grad, w_ref[:, : grad.shape[1]])
    x = x.astype(jnp.float32)
    scale = inverse_rms(x)
    total = (dx + rms_back(x, scale, gain, dh)).astype(jnp.bfloat16)
    return total, jnp.sum(dh * x * scale, axis=0, keepdims=True)


def finish_kernel(
    x_ref, ht_ref, dq_ref, dkv_ref, gains_ref, dx_ref, w_ref, dw_ref, dxo_ref, dgain_ref, dall
):
    width = x_ref.shape[1]
    seqs, heads, block, _ = dq_ref.shape
    dgain_ref[...] = jnp.zeros_like(dgain_ref)

    @pl.loop(0, seqs)
    def _(tile):
        part = pl.ds(pl.multiple_of(tile * block, block), block)
        grad = jnp.concatenate([dq_ref[tile, h] for h in range(heads)] + [dkv_ref[tile]], axis=1)
        dall[part] = grad
        dxo_ref[part], terms = finish_rows(
            x_ref[part], dx_ref[part], grad, w_ref, gains_ref[0:1]
        )
        dgain_ref[0:1] += terms

    @pl.loop(0, width // ROW_TILE)
    def _(tile):
        part = pl.ds(pl.multiple_of(tile * ROW_TILE, ROW_TILE), ROW_TILE)
        dw_ref[part] = matmul(ht_ref[part], dall[...]).astype(jnp.bfloat16)


def finish(x, normed_t, dq, dkv, gains, dx, weights):
    rows, width = x.shape
    columns = width + dkv.shape[2]
    return pl.pallas_call(
        finish_kernel,
        in_specs=[vmem()] * 7,
        out_specs=[vmem()] * 3,
        out_shape=[
            jax.ShapeDtypeStruct((width, columns), jnp.bfloat16),
            jax.ShapeDtypeStruct((rows, width), jnp.bfloat16),
            jax.ShapeDtypeStruct((8, width), jnp.float32),
        ],
        scratch_shapes=[pltpu.VMEM((rows, columns), jnp.bfloat16)],
        compiler_params=params(),
        name="finish",
    )(x, normed_t, dq, dkv, gains, dx, weights)


def first_kernel(chunks, shard_ref, segments_ref, full_ref, all_ref, sems, local_sems, seg_sems):
    x, c, z, y = place()
    others = [
        device(x, c, lax.rem(z + hop, 4), target)
        for hop in range(4)
        for target in (y, 1 - y)
        if (hop, target is y) != (0, True)
    ]
    greet(others + [device(1 - x, c, z, y), device(x, 1 - c, z, y)])
    gather = Gather(shard_ref, full_ref, sems, local_sems, chunks)
    mine = all_ref.at[z * 2 + y]
    keep = pltpu.make_async_copy(segments_ref, mine, seg_sems.at[2, 0])
    keep.start()
    copies = [
        remote(segments_ref, mine, seg_sems.at[0, i], seg_sems.at[1, i], partner)
        for i, partner in enumerate(others)
    ]
    for copy in copies:
        copy.start()
    for tick in gather.ticks(range(len(chunks))):
        for number, chunk in tick:
            gather.step(number, chunk)
    keep.wait()
    for copy in copies:
        copy.wait()


def gather_first(shard, segments, chunks):
    rows, columns = shard.shape
    full, everything = pl.pallas_call(
        functools.partial(first_kernel, chunks),
        out_shape=[
            jax.ShapeDtypeStruct((2, 2, 4, 2, rows, columns), shard.dtype),
            jax.ShapeDtypeStruct((8,) + segments.shape, segments.dtype),
        ],
        in_specs=[hbm(), hbm()],
        out_specs=[hbm(), hbm()],
        scratch_shapes=Gather.scratch(len(chunks)) + [pltpu.SemaphoreType.DMA((3, 8))],
        compiler_params=pltpu.CompilerParams(collective_id=0, has_side_effects=True),
        name="gather_first",
    )(shard, segments)
    return full.reshape(32 * rows, columns), everything


def front_kernel(
    scale,
    chunks,
    x_ref,
    cos_ref,
    sin_ref,
    w_ref,
    low_ref,
    shard_ref,
    h_ref,
    q_ref,
    pairs_ref,
    gains_ref,
    o_ref,
    lse_ref,
    full_ref,
    window,
    sems,
    local_sems,
    window_sems,
    out_sem,
):
    seqs, heads, block, head_dim = q_ref.shape
    width = heads * head_dim
    reach = window.shape[1] - block
    window[:, :reach] = jnp.zeros((seqs, reach, 2 * head_dim), window.dtype)
    greet(neighbours())
    gather = Gather(shard_ref, full_ref, sems, local_sems, chunks)
    windows = Windows(window, window_sems, block)
    ticks = gather.ticks(range(len(chunks)))

    def tick(number):
        for step, chunk in ticks[number]:
            gather.step(step, chunk)

    tick(0)
    gains_ref[...] = gain_rows(w_ref, width + 2 * head_dim)

    @pl.loop(0, seqs)
    def _(seq):
        part = pl.ds(pl.multiple_of(seq * block, block), block)
        project_block(
            x_ref.at[part],
            cos_ref.at[part],
            sin_ref.at[part],
            w_ref,
            gains_ref[0:1],
            h_ref.at[:, part],
            q_ref.at[seq],
            window.at[seq, pl.ds(reach, block)],
        )
        windows.own(seq)

    tick(1)
    windows.once(0)
    windows.once(1)
    windows.twice(0)
    halves = block // HALF

    @pl.loop(0, seqs)
    def _(seq):
        @pl.when(seq + 2 < seqs)
        def _():
            windows.once(seq + 2)

        @pl.when(seq + 1 < seqs)
        def _():
            windows.twice(seq + 1)

        windows.all(seq)
        for half in range(halves):
            attend_half(
                scale,
                half,
                q_ref.at[seq],
                window.at[seq],
                low_ref.at[seq],
                o_ref.at[seq],
                lse_ref.at[seq],
            )
            for number in range(2 + half, len(ticks), halves):
                if number < 2 + halves * seqs:
                    pl.when(seq == (number - 2) // halves)(lambda: tick(number))

    out = pltpu.make_async_copy(window, pairs_ref, out_sem)
    out.start()
    for number in range(2 + halves * seqs, len(ticks)):
        tick(number)

    @pl.loop(0, seqs)
    def _(seq):
        windows.drain(seq)

    out.wait()


def front(x, cosine, sine, weights, low, shard, scale, chunks, seqs, heads, head_dim):
    rows, width = x.shape
    block = rows // seqs
    shard_rows, columns = shard.shape
    low_type = jnp.bfloat16
    span = 5 * block
    lse = (seqs, block // HALF, heads // GROUP, 8, GROUP * HALF)
    out = pl.pallas_call(
        functools.partial(front_kernel, scale, chunks),
        in_specs=[vmem()] * 5 + [hbm()],
        out_specs=[vmem(), vmem(), hbm(), vmem(), vmem(), vmem(), hbm()],
        out_shape=[
            jax.ShapeDtypeStruct((width, rows), low_type),
            jax.ShapeDtypeStruct((seqs, heads, block, head_dim), low_type),
            jax.ShapeDtypeStruct((seqs, span, 2 * head_dim), low_type),
            jax.ShapeDtypeStruct((8, width), jnp.float32),
            jax.ShapeDtypeStruct((seqs, heads, block, head_dim), low_type),
            jax.ShapeDtypeStruct(lse, jnp.float32),
            jax.ShapeDtypeStruct((2, 2, 4, 2, shard_rows, columns), low_type),
        ],
        scratch_shapes=[
            pltpu.VMEM((seqs, span, 2 * head_dim), low_type),
        ]
        + Gather.scratch(len(chunks))
        + [pltpu.SemaphoreType.DMA((2, Windows.KINDS, seqs)), pltpu.SemaphoreType.DMA],
        compiler_params=params(collective_id=2, has_side_effects=True),
        name="front",
    )(x, cosine, sine, weights, low[:, :, None], shard)
    return tuple(out[:-1]) + (out[-1].reshape(32 * shard_rows, columns),)


class WindowGrads:
    def __init__(self, windows, grads, out, came, sems, block):
        self.windows, self.grads, self.out, self.came = windows, grads, out, came
        self.sems, self.block = sems, block

    def rows(self, seq, distance):
        start = (4 - distance) * self.block
        if not isinstance(distance, int):
            start = pl.multiple_of(start, self.block)
        return self.grads.at[seq, pl.ds(start, self.block)]

    def copy(self, kind, seq):
        x, c, z, y = place()
        over = device(x, c, z, 1 - y)
        partner = device(x, c, lax.rem(z + 3, 4), y) if kind < 2 else over
        return remote(
            self.out.at[kind, seq],
            self.came.at[kind, seq],
            self.sems.at[0, kind, seq],
            self.sems.at[1, kind, seq],
            partner,
        )

    def start(self, kind, seq, distance):
        @pl.when(self.windows.gets(kind))
        def _():
            self.out[kind, seq] = self.rows(seq, distance)[...].astype(jnp.bfloat16)
            self.copy(kind, seq).start()

    def add(self, kind, seq, distance):
        @pl.when(self.windows.sends(kind))
        def _():
            self.copy(kind, seq).wait_recv()
            target = self.rows(seq, distance)
            target[...] += self.came[kind, seq].astype(jnp.float32)

    def step(self, number, seq):
        _, _, _, y = place()
        if number == 0:
            self.start(4, seq, 3)
            self.start(3, seq, 1 + 2 * y)
            self.start(2, seq, 1)
        elif number == 1:
            self.add(4, seq, 4)
            self.start(1, seq, 4)
            self.add(3, seq, 2)
        elif number == 2:
            self.add(1, seq, 2)
            self.start(0, seq, 2)
        else:
            self.add(0, seq, 0)
            self.add(2, seq, 0)

    def drain(self, seq):
        for kind in range(Windows.KINDS):
            pl.when(self.windows.gets(kind))(lambda: self.copy(kind, seq).wait_send())


def back_kernel(scale, kept, last_chunks, *refs):
    (
        q_ref,
        pairs_ref,
        low_ref,
        lse_ref,
        o_ref,
        do_ref,
        cos_ref,
        sin_ref,
        x_ref,
        ht_ref,
        gains_ref,
        dgain_ref,
        w_ref,
        dx_ref,
        dout_ref,
        dff_ref,
    ) = refs[:16]
    dxo_ref, refs = refs[16], refs[17:]
    total = kept + 1 + len(last_chunks)
    shares, refs = refs[:total], refs[total:]
    grads, out, came, dall, dx, dgains, dw, load_sems, dx_sems, grad_sems = refs[:10]
    mines, refs = refs[10 : 11 + kept], refs[11 + kept :]
    count = Scatter.BUFFERS
    buffers = [refs[count * k : count * (k + 1)] for k in range(total)]
    sems = refs[count * total]
    seqs, heads, block, head_dim = q_ref.shape
    width = heads * head_dim

    grads[...] = jnp.zeros_like(grads)
    dgains[...] = jnp.zeros_like(dgains)
    dgains[1:2] = dgain_ref[0:1]
    greet(neighbours())
    sources = [dff_ref.at[k] for k in range(kept)] + [dout_ref]
    plans = [(s, mines[k], load_sems.at[k], shares[k]) for k, s in enumerate(sources)]
    for k, (start, end) in enumerate(last_chunks):
        source = dw.at[:, :, :, :, :, pl.ds(start, end - start)]
        plans.append((source, None, None, shares[kept + 1 + k]))
    scatter = Scatter(plans, buffers, sems)
    windows = Windows(None, None, block)
    back = WindowGrads(windows, grads, out, came, grad_sems, block)
    early = range(kept + 1)
    for chunk in early:
        scatter.step(0, chunk)
    halves = block // HALF
    places = halves * seqs
    ticks = [[] for _ in range(places)]
    for k in early:
        for number in (1, 2, 3, 4):
            ticks[min(places - 1, 2 * (number - 1) + k)].append((number, k))
    for tick in ticks:
        tick.sort(key=lambda item: -item[0])

    def load(seq):
        return pltpu.make_async_copy(
            dx_ref.at[pl.ds(seq * block, block)], dx.at[seq % 2], dx_sems.at[seq % 2]
        )

    load(0).start()
    load(1).start()

    @pl.loop(0, seqs)
    def _(seq):
        part = pl.ds(pl.multiple_of(seq * block, block), block)

        def put_dq(base, first, dq):
            there = pl.ds(pl.multiple_of(seq * block + first, HALF), HALF)
            for h in range(GROUP):
                lanes = pl.ds(pl.multiple_of((base + h) * head_dim, head_dim), head_dim)
                dall[there, lanes] = dq[h]

        for half in range(halves):
            attend_back_half(
                scale,
                half,
                q_ref.at[seq],
                pairs_ref.at[seq],
                low_ref.at[seq],
                lse_ref.at[seq],
                o_ref.at[seq],
                do_ref.at[seq],
                cos_ref.at[part],
                sin_ref.at[part],
                put_dq,
                grads.at[seq],
            )
            if half == halves - 1:
                back.step(0, seq)
                pl.when(seq >= 1)(lambda: back.step(1, seq - 1))
                pl.when(seq >= 2)(lambda: back.step(2, seq - 2))
                pl.when(seq >= 3)(lambda: back.step(3, seq - 3))
            for number in range(half, places, halves):
                if ticks[number]:

                    @pl.when(seq == number // halves)
                    def _():
                        for item in ticks[number]:
                            scatter.step(*item)

    def finish_one(seq):
        part = pl.ds(seq * block, block)
        own = grads[seq, 4 * block :]
        key, value = own[:, :head_dim], own[:, head_dim:]
        turned = pltpu.roll(key, head_dim // 2, 1)
        key = key * cos_ref[part] - turned * sin_ref[part]
        dall[part, width : width + head_dim] = key.astype(jnp.bfloat16)
        dall[part, width + head_dim :] = value.astype(jnp.bfloat16)
        load(seq).wait()
        dxo_ref[part], terms = finish_rows(
            x_ref[part], dx[seq % 2], dall[part], w_ref, gains_ref[0:1]
        )
        dgains[0:1] += terms
        if seq + 2 < seqs:
            load(seq + 2).start()

    back.step(1, seqs - 1)
    finish_one(0)
    back.step(2, seqs - 2)
    back.step(3, seqs - 3)
    back.step(2, seqs - 1)
    finish_one(1)
    back.step(3, seqs - 2)
    finish_one(2)
    back.step(3, seqs - 1)
    finish_one(3)

    for k, (start, end) in enumerate(last_chunks):
        last = min(end, width + 2 * head_dim)

        @pl.loop(0, width // ROW_TILE)
        def _(tile):
            part = pl.ds(pl.multiple_of(tile * ROW_TILE, ROW_TILE), ROW_TILE)
            value = matmul(ht_ref[part], dall[:, start:last]).astype(jnp.bfloat16)
            dw[tile // 2, lax.rem(tile, 2), :, :, :, start:last] = value.reshape(
                4, 2, ROW_TILE // 8, last - start
            )

        if last < end:
            gains = dgains[...].T.astype(jnp.bfloat16)
            dw[:, :, :, :, :, last:end] = gains.reshape(dw.shape[:5] + (end - last,))
        scatter.step(0, kept + 1 + k)
    chunks = [kept + 1 + k for k in range(len(last_chunks))]
    for number in (1, 2, 3, 4):
        for chunk in chunks:
            scatter.step(number, chunk)

    @pl.loop(0, seqs)
    def _(seq):
        back.drain(seq)


def back(
    query, pairs, low, lse, mixed, grad, cosine, sine, x, normed_t, gains, dgain, weights, dx, dout, dff, scale
):
    seqs, heads, block, head_dim = query.shape
    rows, width = x.shape
    columns = weights.shape[1]
    kept = dff.shape[0]
    shard_rows = dff.shape[-2]
    low_type = jnp.bfloat16
    span = pairs.shape[1]
    last_chunks = ((0, 640), (640, columns))
    widths = [dff.shape[-1]] * kept + [width] + [end - start for start, end in last_chunks]
    lanes = 2 * head_dim
    out = pl.pallas_call(
        functools.partial(back_kernel, scale, kept, last_chunks),
        in_specs=[vmem()] * 13 + [hbm()] * 3,
        out_specs=[vmem()] * (1 + len(widths)),
        out_shape=[jax.ShapeDtypeStruct((rows, width), low_type)]
        + [jax.ShapeDtypeStruct((shard_rows, n), jnp.float32) for n in widths],
        scratch_shapes=[
            pltpu.VMEM((seqs, span, lanes), jnp.float32),
            pltpu.VMEM((Windows.KINDS, seqs, block, lanes), low_type),
            pltpu.VMEM((Windows.KINDS, seqs, block, lanes), low_type),
            pltpu.VMEM((rows, width + lanes), low_type),
            pltpu.VMEM((2, block, width), jnp.float32),
            pltpu.VMEM((128, width), jnp.float32),
            pltpu.VMEM((2, 2, 4, 2, shard_rows, columns), low_type),
            pltpu.SemaphoreType.DMA((kept + 1,)),
            pltpu.SemaphoreType.DMA((2,)),
            pltpu.SemaphoreType.DMA((2, Windows.KINDS, seqs)),
        ]
        + [pltpu.VMEM((2, 4, 2, shard_rows, n), low_type) for n in widths[: kept + 1]]
        + Scatter.scratch(widths, shard_rows),
        compiler_params=params(collective_id=4, has_side_effects=True),
        name="back",
    )(
        query,
        pairs,
        low[:, None, :],
        lse,
        mixed,
        grad,
        cosine,
        sine,
        x,
        normed_t,
        gains,
        dgain,
        weights,
        dx,
        dout.reshape(2, 2, 4, 2, shard_rows, width),
        dff,
    )
    return out[0], out[1 : 1 + kept], out[1 + kept], jnp.concatenate(out[2 + kept :], axis=1)


def stack_ff(gate, up_part, down_t):
    rows, hidden = gate.shape
    parts = [p.reshape(rows, FF_CHUNKS, hidden // FF_CHUNKS) for p in (gate, up_part, down_t)]
    return jnp.stack(parts, axis=2).reshape(rows, 3 * hidden)


def unstack_ff(stacked):
    rows, hidden = stacked.shape[0], stacked.shape[1] // 3
    parts = stacked.reshape(rows, FF_CHUNKS, 3, hidden // FF_CHUNKS)
    return [parts[:, :, i].reshape(rows, hidden) for i in range(3)]


def shifted(value, axis, steps):
    count = lax.axis_size(axis)
    initial, last = (max(0, -steps), min(count, count - steps))
    return lax.ppermute(value, axis, [(source, source + steps) for source in range(initial, last)])


def on_device(
    own_links,
    tokens,
    segments,
    cotangent,
    first_gain,
    query_weight,
    key_weight,
    value_weight,
    out_weight,
    second_gain,
    gate_weight,
    up_weight,
    down_weight,
):
    seqs, block_len, width = tokens.shape
    head_dim = key_weight.shape[1]
    heads = query_weight.shape[1] // head_dim
    hidden = gate_weight.shape[1]
    shard_rows = first_gain.shape[0]
    reach = (WINDOW - 1 + block_len - 1) // block_len
    scale = head_dim ** (-0.5)
    rows = seqs * block_len
    keys_from = width + 2 * head_dim
    inputs = tokens.reshape(rows, width)
    grad_rows = cotangent.reshape(rows, width)

    gains = jnp.zeros((shard_rows, 128), first_gain.dtype)
    gains = gains.at[:, 0].set(first_gain).at[:, 1].set(second_gain)
    shard = jnp.concatenate([query_weight, key_weight, value_weight, gains], axis=1)
    later = jnp.concatenate(
        [out_weight.T, stack_ff(gate_weight, up_weight, down_weight.T)], axis=1
    )
    if own_links:
        weights, all_segments = gather_first(shard, segments, [(0, 640, keys_from + 128)])
        earlier = all_segments.transpose(1, 0, 2).reshape(seqs, -1)
    else:
        weights = lax.all_gather(shard, ("batch", "seq"), axis=0, tiled=True)
        full = lax.all_gather(later, ("batch", "seq"), axis=0, tiled=True)
        earlier = lax.all_gather(segments, "seq", axis=1, tiled=True)

    starts = jnp.sum(earlier[:, None, :] < segments[:, :, None], axis=-1, dtype=jnp.int32)
    query_place = jnp.arange(block_len, dtype=jnp.int32) + lax.axis_index("seq") * block_len
    low = jnp.maximum(starts, query_place[None, :] - (WINDOW - 1))
    low = low - (query_place[0] - reach * block_len)
    cosine, sine = tables((query_place[None, :] - starts).reshape(-1), head_dim)

    if own_links:
        chunks = [(0, width // 2, width)]
        step = 3 * hidden // FF_CHUNKS
        for start in range(width, width + 3 * hidden, step):
            chunks.append((start, start + step // 2, start + step))
        normed_t, query, pairs, gains, mixed, lse, full = front(
            inputs, cosine, sine, weights, low, later, scale, chunks, seqs, heads, head_dim
        )
        scattered = SCATTERED
    else:
        normed_t, query, own_pairs, gains = project(
            inputs, cosine, sine, weights, seqs, heads, head_dim
        )
        pieces = [shifted(own_pairs, "seq", distance) for distance in range(reach, 0, -1)]
        pairs = jnp.concatenate(pieces + [own_pairs], axis=1)
        mixed, lse = attend(query, pairs, low, scale)
        scattered = 0
    output, grad_mixed, grad_heads, dgain_two, grad_out_t, grad_ff, *shares = feed(
        own_links, scattered, inputs, mixed, grad_rows, gains, full, hidden
    )
    if own_links:
        grad_input, more, share_out, share_first = back(
            query,
            pairs,
            low,
            lse,
            mixed,
            grad_heads,
            cosine,
            sine,
            inputs,
            normed_t,
            gains,
            dgain_two,
            weights,
            grad_mixed,
            grad_out_t,
            grad_ff,
            scale,
        )
        share_ff = jnp.concatenate(list(shares) + list(more), axis=1)
    else:
        grad_query, grad_pairs = attend_back(
            query, pairs, low, lse, mixed, grad_heads, cosine, sine, scale
        )
        own_grad = grad_pairs[:, reach * block_len :]
        for distance in range(1, reach + 1):
            start = (reach - distance) * block_len
            piece = grad_pairs[:, start : start + block_len].astype(jnp.bfloat16)
            own_grad = own_grad + shifted(piece, "seq", -distance).astype(own_grad.dtype)
        grad_key = own_grad[..., :head_dim].reshape(rows, head_dim)
        grad_key = grad_key * cosine - jnp.roll(grad_key, head_dim // 2, axis=1) * sine
        grad_kv = jnp.concatenate(
            [grad_key.reshape(seqs, block_len, head_dim), own_grad[..., head_dim:]], axis=-1
        ).astype(jnp.bfloat16)
        grad_qkv_w, grad_input, dgain_one = finish(
            inputs, normed_t, grad_query, grad_kv, gains, grad_mixed, weights
        )
        grad_gains = jnp.zeros((width, 128), jnp.bfloat16)
        grad_gains = grad_gains.at[:, 0].set(dgain_one[0].astype(jnp.bfloat16))
        grad_gains = grad_gains.at[:, 1].set(dgain_two[0].astype(jnp.bfloat16))
        grad_ff = grad_ff.reshape(FF_CHUNKS, width, -1)
        grads = jnp.concatenate([grad_qkv_w, grad_gains, grad_out_t] + list(grad_ff), axis=1)
        share = lax.psum_scatter(grads, ("batch", "seq"), scatter_dimension=0, tiled=True)
        share = share.astype(jnp.float32)
        share_first = share[:, : keys_from + 128]
        share_out = share[:, keys_from + 128 : keys_from + 128 + width]
        share_ff = share[:, keys_from + 128 + width :]
    share_gate, share_up, share_down_t = unstack_ff(share_ff)
    return (
        output.reshape(tokens.shape),
        grad_input.reshape(tokens.shape),
        share_first[:, keys_from],
        share_first[:, :width],
        share_first[:, width : width + head_dim],
        share_first[:, width + head_dim : keys_from],
        share_out.T,
        share_first[:, keys_from + 1],
        share_gate,
        share_up,
        share_down_t.T,
    )


def solution(mesh):
    both = ("batch", "seq")
    rows_split, columns_split = P(both, None), P(None, both)
    tokens_split, gain_split = P("batch", "seq", None), P(both)
    weights = (
        gain_split,
        rows_split,
        rows_split,
        rows_split,
        columns_split,
        gain_split,
        rows_split,
        rows_split,
        columns_split,
    )
    in_specs = (tokens_split, P("batch", "seq"), tokens_split) + weights
    out_specs = (tokens_split, tokens_split) + weights
    own_links = (mesh.shape["batch"], mesh.shape["seq"]) == (4, 8)
    return jax.shard_map(
        functools.partial(on_device, own_links),
        mesh=mesh,
        in_specs=in_specs,
        out_specs=out_specs,
        check_vma=False,
    )
```

```python
import functools

import jax
import jax.numpy as jnp
from jax import lax
from jax.experimental import pallas as pl
from jax.experimental.pallas import tpu as pltpu
from jax.sharding import PartitionSpec as P

WINDOW = 1024
FF_CHUNKS = 6
SCATTERED = 4
FAR = 2
FEED_TILE = 512
MESH_ID = pl.DeviceIdType.MESH
MIB = 1 << 20


def tables(positions, head_dim):
    inverse = 10000.0 ** (-2.0 * jnp.arange(head_dim // 2, dtype=jnp.float32) / head_dim)
    angle = positions.astype(jnp.float32)[:, None] * inverse[None, :]
    cosine, sine = jnp.cos(angle), jnp.sin(angle)
    return (
        jnp.concatenate([cosine, cosine], axis=-1),
        jnp.concatenate([-sine, sine], axis=-1),
    )


def matmul(left, right):
    return jnp.dot(left, right, preferred_element_type=jnp.float32)


def right_times(left, right):
    return lax.dot_general(
        left, right, (((1,), (1,)), ((), ())), preferred_element_type=jnp.float32
    )


def place():
    batch, seq = lax.axis_index("batch"), lax.axis_index("seq")
    return batch // 2, lax.rem(batch, 2), seq // 2, lax.rem(seq, 2)


def device(x, c, z, y):
    return (x * 2 + c, z * 2 + y)


def greet(partners):
    barrier = pltpu.get_barrier_semaphore()
    for partner in partners:
        pl.semaphore_signal(barrier, inc=1, device_id=partner, device_id_type=MESH_ID)
    pl.semaphore_wait(barrier, len(partners))


def neighbours():
    x, c, z, y = place()
    return [
        device(x, c, lax.rem(z + 1, 4), y),
        device(x, c, lax.rem(z + 2, 4), y),
        device(x, c, lax.rem(z + 3, 4), y),
        device(1 - x, c, z, y),
        device(x, c, z, 1 - y),
        device(x, 1 - c, z, y),
    ]


def remote(source, target, send_sem, recv_sem, partner):
    return pltpu.make_async_remote_copy(
        src_ref=source,
        dst_ref=target,
        send_sem=send_sem,
        recv_sem=recv_sem,
        device_id=partner,
        device_id_type=MESH_ID,
    )


FRONT_ORDER = (
    ((0, 0, 0), (0, 0, 1), (0, 0, 2), (0, 0, 3), (0, 1, 0), (0, 1, 1), (0, 2, 0), (0, 0, 4), (0, 1, 2), (0, 2, 1), (0, 0, 5), (0, 1, 3), (0, 3, 0), (0, 2, 2), (0, 0, 6), (0, 1, 4), (0, 4, 0), (0, 3, 1), (0, 2, 3), (0, 0, 7), (0, 1, 5), (0, 4, 1), (0, 3, 2), (0, 2, 4), (0, 0, 8), (0, 4, 2), (0, 1, 6),),
    ((0, 3, 3),),
    ((0, 2, 5), (0, 1, 7), (0, 4, 3), (0, 0, 9),),
    ((0, 3, 4), (0, 2, 6), (0, 1, 8), (0, 0, 10),),
    ((1, 0, 0), (0, 4, 4), (1, 0, 1), (0, 3, 5), (0, 2, 7), (0, 0, 11), (0, 4, 5), (0, 1, 9), (1, 0, 2), (0, 3, 6), (0, 2, 8), (0, 0, 12), (0, 4, 6), (0, 1, 10), (1, 1, 0), (1, 0, 3), (1, 1, 1), (0, 3, 7), (0, 2, 9), (0, 4, 7), (0, 1, 11), (1, 1, 2), (0, 3, 8), (0, 1, 12), (0, 2, 10), (0, 4, 8), (1, 2, 0),),
    ((1, 1, 3),),
    ((1, 2, 1),),
    (),
    ((0, 3, 9), (0, 2, 11), (1, 2, 2),),
    ((0, 4, 9),),
    ((0, 2, 12), (0, 3, 10), (1, 2, 3),),
    ((0, 4, 10),),
    ((0, 3, 11), (0, 3, 12), (0, 4, 11), (0, 4, 12),),
)

FEED_ORDER = (
    ((0, 0, 0), (0, 0, 1),),
    (),
    (),
    (),
    ((0, 1, 0),),
    (),
    ((0, 2, 0), (0, 1, 1),),
    (),
    ((1, 0, 0),),
    (),
    ((0, 3, 0), (1, 1, 0),),
    ((0, 2, 1),),
    ((1, 0, 1), (0, 4, 0),),
    (),
    ((1, 2, 0), (1, 1, 1),),
    (),
    ((0, 3, 1), (1, 0, 2),),
    ((1, 3, 0),),
    ((0, 4, 1),),
    ((1, 1, 2),),
    ((1, 2, 1), (1, 4, 0), (1, 0, 3),),
    (),
    ((1, 2, 2), (1, 1, 3),),
    ((1, 3, 1),),
    (),
    ((1, 3, 2),),
    ((1, 4, 1), (1, 2, 3),),
    (),
    (),
    ((1, 4, 2), (1, 3, 3),),
    ((1, 4, 3),),
)

BACK_ORDER = (
    ((0, 0, 0), (0, 0, 1), (0, 0, 2),),
    (),
    ((1, 0, 0), (0, 1, 0),),
    ((1, 1, 0), (0, 1, 1), (0, 1, 2),),
    ((1, 2, 0), (1, 0, 1),),
    ((0, 2, 0), (1, 3, 0),),
    ((1, 0, 2),),
    (),
    ((1, 1, 1), (1, 0, 3), (0, 2, 1), (2, 0, 0), (0, 0, 3), (0, 0, 4), (1, 2, 1), (3, 0, 0), (0, 1, 3), (0, 2, 2), (0, 1, 4), (0, 3, 0), (1, 3, 1), (1, 1, 2), (3, 1, 0), (1, 1, 3), (0, 4, 0), (1, 2, 2), (0, 3, 1), (1, 2, 3), (0, 2, 3), (1, 3, 2), (3, 2, 0), (0, 3, 2), (0, 2, 4), (0, 3, 3), (0, 3, 4), (0, 4, 1), (1, 3, 3), (3, 3, 0), (4, 0, 0), (0, 0, 5), (0, 4, 2), (0, 1, 5), (0, 4, 3), (0, 2, 5), (0, 4, 4), (0, 3, 5), (0, 4, 5),),
)


class Gather:
    STEPS = 5
    SEMS = 8

    def __init__(self, sems, local_sems, chunks):
        self.sems, self.local_sems, self.chunks = sems, local_sems, chunks

    @staticmethod
    def scratch(count):
        return [
            pltpu.SemaphoreType.DMA((2, count, Gather.SEMS)),
            pltpu.SemaphoreType.DMA((count,)),
        ]

    def keep(self, chunk):
        x, c, z, y = place()
        shard, full, start, _, end = self.chunks[chunk]
        whole = pl.ds(start, end - start)
        return pltpu.make_async_copy(
            shard.at[:, whole], full.at[x, c, z, y, :, whole], self.local_sems.at[chunk]
        )

    def copy(self, chunk, slot):
        x, c, z, y = place()
        shard, full, start, middle, end = self.chunks[chunk]
        whole = pl.ds(start, end - start)
        first, second = pl.ds(start, middle - start), pl.ds(middle, end - middle)
        if slot < 3:
            source, target = shard.at[:, whole], full.at[x, c, z, y, :, whole]
            partner = device(x, c, lax.rem(z + slot + 1, 4), y)
        else:
            source, partner = {
                3: (full.at[x, c, :, y, :, first], device(x, c, z, 1 - y)),
                4: (full.at[x, c, :, y, :, second], device(1 - x, c, z, y)),
                5: (full.at[x, c, :, :, :, first], device(1 - x, c, z, y)),
                6: (full.at[:, c, :, y, :, second], device(x, c, z, 1 - y)),
                7: (full.at[:, c, :, :, :, whole], device(x, 1 - c, z, y)),
            }[slot]
            target = source
        return remote(
            source, target, self.sems.at[0, chunk, slot], self.sems.at[1, chunk, slot], partner
        )

    def step(self, number, chunk):
        if number == 0:
            self.keep(chunk).start()
            for slot in (0, 1, 2):
                self.copy(chunk, slot).start()
        elif number == 1:
            self.keep(chunk).wait()
            for slot in (0, 1, 2):
                self.copy(chunk, slot).wait_recv()
            self.copy(chunk, 3).start()
            self.copy(chunk, 4).start()
        elif number == 2:
            self.copy(chunk, 3).wait_recv()
            self.copy(chunk, 5).start()
            self.copy(chunk, 4).wait_recv()
            self.copy(chunk, 6).start()
        elif number == 3:
            self.copy(chunk, 5).wait_recv()
            self.copy(chunk, 6).wait_recv()
            self.copy(chunk, 7).start()
        else:
            self.copy(chunk, 7).wait_recv()
            for slot in range(self.SEMS):
                self.copy(chunk, slot).wait_send()


class Windows:
    KINDS = 5

    def __init__(self, window, sems, block):
        self.window, self.sems, self.block = window, sems, block

    def rows(self, seq, distance):
        start = (4 - distance) * self.block
        return self.window.at[seq, pl.ds(start, self.block)]

    def copy(self, kind, seq):
        x, c, z, y = place()
        down, over = device(x, c, lax.rem(z + 1, 4), y), device(x, c, z, 1 - y)
        source, target, partner = {
            0: (0, 2, down),
            1: (2, 4, down),
            2: (0, 1, over),
            3: (2, 3 - 2 * y, over),
            4: (4, 3, over),
        }[kind]
        return remote(
            self.rows(seq, source),
            self.rows(seq, target),
            self.sems.at[0, kind, seq],
            self.sems.at[1, kind, seq],
            partner,
        )

    def sends(self, kind):
        _, _, z, y = place()
        return {0: z < 3, 1: (z > 0) & (z < 3), 2: y == 0, 3: z > 0, 4: (z > 1) & (y == 1)}[kind]

    def gets(self, kind):
        _, _, z, y = place()
        return {0: z > 0, 1: z > 1, 2: y == 1, 3: z > 0, 4: (z > 1) & (y == 0)}[kind]

    def start(self, kind, seq):
        pl.when(self.sends(kind))(lambda: self.copy(kind, seq).start())

    def wait(self, kind, seq):
        pl.when(self.gets(kind))(lambda: self.copy(kind, seq).wait_recv())

    def own(self, seq):
        self.start(0, seq)
        self.start(2, seq)

    def once(self, seq):
        self.wait(0, seq)
        self.start(1, seq)
        self.start(3, seq)

    def twice(self, seq):
        self.wait(1, seq)
        self.start(4, seq)

    def all(self, seq):
        for kind in (2, 3, 4):
            self.wait(kind, seq)

    def drain(self, seq):
        for kind in range(self.KINDS):
            pl.when(self.sends(kind))(lambda: self.copy(kind, seq).wait_send())


class Scatter:
    SEMS = 8

    def __init__(self, plans, buffers, sems):
        self.plans, self.buffers, self.sems = plans, buffers, sems

    @staticmethod
    def scratch(widths, rows, share=0.5):
        out = []
        for n in widths:
            h = round(n * share / 128) * 128
            low = jnp.bfloat16
            out += [
                pltpu.VMEM((2, 4, 2, rows, n), low),
                pltpu.VMEM((4, 2, rows, h), low),
                pltpu.VMEM((2, 4, rows, n - h), low),
                pltpu.VMEM((4, rows, h), low),
                pltpu.VMEM((4, rows, n - h), low),
                pltpu.VMEM((3, rows, n), low),
            ]
        return out + [pltpu.SemaphoreType.DMA((2, max(1, len(widths)), Scatter.SEMS))]

    BUFFERS = 6

    def copy(self, chunk, slot):
        x, c, z, y = place()
        source = self.plans[chunk][0]
        one, two_a, two_b, three_a, three_b, last = self.buffers[chunk]
        half = two_a.shape[-1]
        first, second = slice(0, half), slice(half, one.shape[-1])
        if slot >= 5:
            hop = slot - 4
            source, target = one.at[0, lax.rem(z + hop, 4), 0], last.at[hop - 1]
            partner = device(x, c, lax.rem(z + hop, 4), y)
        else:
            over_x, over_y = device(1 - x, c, z, y), device(x, c, z, 1 - y)
            source, target, partner = {
                0: lambda: (source.at[:, 1 - c], one, device(x, 1 - c, z, y)),
                1: lambda: (one.at[1 - x, :, :, :, first], two_a, over_x),
                2: lambda: (one.at[:, :, 1 - y, :, second], two_b, over_y),
                3: lambda: (two_a.at[:, 1 - y], three_a, over_y),
                4: lambda: (two_b.at[1 - x], three_b, over_x),
            }[slot]()
        return remote(
            source, target, self.sems.at[0, chunk, slot], self.sems.at[1, chunk, slot], partner
        )

    def load(self, chunk):
        _, c, _, _ = place()
        source, mine, sem, _ = self.plans[chunk]
        return pltpu.make_async_copy(source.at[:, c], mine, sem)

    def step(self, number, chunk):
        x, c, z, y = place()
        source, mine, _, result = self.plans[chunk]
        one, two_a, two_b, three_a, three_b, last = self.buffers[chunk]
        half = two_a.shape[-1]
        first, second = slice(0, half), slice(half, one.shape[-1])
        if number == 0:
            self.copy(chunk, 0).start()
            if mine is not None:
                self.load(chunk).start()
        elif number == 1:
            if mine is not None:
                self.load(chunk).wait()
            else:
                mine = source.at[:, c]
            self.copy(chunk, 0).wait_recv()
            for i in range(2):

                @pl.loop(0, 4)
                def _(j):
                    for k in range(2):
                        add_rows(one.at[i, j, k], mine.at[i, j, k])

            self.copy(chunk, 1).start()
            self.copy(chunk, 2).start()
            self.copy(chunk, 0).wait_send()
        elif number == 2:
            self.copy(chunk, 1).wait_recv()

            @pl.loop(0, 4)
            def _(j):
                for k in range(2):
                    add_rows(two_a.at[j, k], one.at[x, j, k, :, first])

            self.copy(chunk, 3).start()
            self.copy(chunk, 2).wait_recv()

            @pl.loop(0, 4)
            def _(j):
                for i in range(2):
                    add_rows(two_b.at[i, j], one.at[i, j, y, :, second])

            self.copy(chunk, 4).start()
        elif number == 3:
            self.copy(chunk, 1).wait_send()
            self.copy(chunk, 2).wait_send()
            self.copy(chunk, 3).wait_recv()
            self.copy(chunk, 4).wait_recv()

            @pl.loop(0, 4)
            def _(k):
                left = three_a[k].astype(jnp.float32) + two_a[k, y].astype(jnp.float32)
                right = three_b[k].astype(jnp.float32) + two_b[x, k].astype(jnp.float32)
                one[0, k, 0, :, first] = left.astype(one.dtype)
                one[0, k, 0, :, second] = right.astype(one.dtype)

            for slot in (5, 6, 7):
                self.copy(chunk, slot).start()
        else:
            total = one[0, z, 0].astype(jnp.float32)
            for slot in (5, 6, 7):
                self.copy(chunk, slot).wait_recv()
                total += last[slot - 5].astype(jnp.float32)
            result[...] = total
            for slot in (3, 4, 5, 6, 7):
                self.copy(chunk, slot).wait_send()


def add_rows(target, other):
    target[...] = (target[...].astype(jnp.float32) + other[...].astype(jnp.float32)).astype(
        target.dtype
    )


ROW_TILE = 256
LOG2E = 1.4426950408889634
NEG = -1e30


def row(block, index):
    return pl.BlockSpec(block, index)


def vmem():
    return pl.BlockSpec(memory_space=pltpu.VMEM)


def hbm():
    return pl.BlockSpec(memory_space=pl.ANY)


def params(**more):
    return pltpu.CompilerParams(vmem_limit_bytes=62 * MIB, **more)


def inverse_rms(values):
    return lax.rsqrt(jnp.mean(values * values, axis=-1, keepdims=True) + 1e-06)


def rms_back(values, scale, gain, grad):
    inner = jnp.mean(values * gain * grad, axis=-1, keepdims=True)
    return scale * gain * grad - values * (scale * scale * scale * inner)


def project_block(x_ref, cos_ref, sin_ref, columns, gain, ht_ref, q_ref, kv_ref):
    heads, _, head_dim = q_ref.shape
    width = heads * head_dim
    x = x_ref[...].astype(jnp.float32)
    normed = (x * inverse_rms(x) * gain).astype(jnp.bfloat16)
    ht_ref[...] = normed.T
    cosine, sine = cos_ref[...], sin_ref[...]

    def turn(u):
        return (u * cosine + pltpu.roll(u, head_dim // 2, 1) * sine).astype(jnp.bfloat16)

    for pair in range(heads // 2):
        both = matmul(normed, columns(2 * pair * head_dim, (2 * pair + 2) * head_dim))
        q_ref[2 * pair] = turn(both[:, :head_dim])
        q_ref[2 * pair + 1] = turn(both[:, head_dim:])
    both = matmul(normed, columns(width, width + 2 * head_dim))
    kv_ref[:, :head_dim] = turn(both[:, :head_dim])
    kv_ref[:, head_dim:] = both[:, head_dim:].astype(jnp.bfloat16)


def gain_rows(columns, start):
    return columns(start, start + 128).astype(jnp.float32).T[:8]


def project_kernel(x_ref, cos_ref, sin_ref, w_ref, ht_ref, q_ref, kv_ref, gains_ref):
    width = x_ref.shape[1]

    def columns(start, end):
        return w_ref[:, start:end]

    gains_ref[...] = gain_rows(columns, width + kv_ref.shape[2])
    project_block(
        x_ref, cos_ref, sin_ref, columns, gains_ref[0:1], ht_ref, q_ref.at[0], kv_ref.at[0]
    )


def project(x, cosine, sine, weights, seqs, heads, head_dim):
    rows, width = x.shape
    block = rows // seqs
    return pl.pallas_call(
        project_kernel,
        grid=(seqs,),
        in_specs=[
            row((block, width), lambda b: (b, 0)),
            row((block, head_dim), lambda b: (b, 0)),
            row((block, head_dim), lambda b: (b, 0)),
            row(weights.shape, lambda b: (0, 0)),
        ],
        out_specs=[
            row((width, block), lambda b: (0, b)),
            row((1, heads, block, head_dim), lambda b: (b, 0, 0, 0)),
            row((1, block, 2 * head_dim), lambda b: (b, 0, 0)),
            row((8, width), lambda b: (0, 0)),
        ],
        out_shape=[
            jax.ShapeDtypeStruct((width, rows), jnp.bfloat16),
            jax.ShapeDtypeStruct((seqs, heads, block, head_dim), jnp.bfloat16),
            jax.ShapeDtypeStruct((seqs, block, 2 * head_dim), jnp.bfloat16),
            jax.ShapeDtypeStruct((8, width), jnp.float32),
        ],
        compiler_params=params(),
        name="project",
    )(x, cosine, sine, weights)


HALF = 128
GROUP = 8


def window_bias(low_ref, first, span):
    place = lax.broadcasted_iota(jnp.int32, (span, HALF), 0)
    local = lax.broadcasted_iota(jnp.int32, (span, HALF), 1)
    low = low_ref[:, first : first + HALF] - first
    allowed = (place >= low) & (place <= local + (span - HALF))
    bias = jnp.where(allowed, 0.0, NEG)
    return jnp.concatenate([bias] * GROUP, axis=1)


def attend_half(scale, half, q_ref, kv_ref, low_ref, o_ref, lse_ref):
    heads, block, head_dim = q_ref.shape
    span = kv_ref.shape[0] - (block - HALF)
    factor = scale * LOG2E
    first = half * HALF
    keys = kv_ref[first : first + span, :head_dim]
    values_t = kv_ref[first : first + span, head_dim:].T
    values_t = jnp.concatenate([values_t, jnp.ones((16, span), values_t.dtype)], axis=0)
    bias = window_bias(low_ref, first, span)

    for base in range(0, heads, GROUP):
        query = q_ref[base : base + GROUP, first : first + HALF].reshape(GROUP * HALF, head_dim)
        score = right_times(keys, query) * factor + bias
        peak = jnp.max(score, axis=0, keepdims=True)
        weights = jnp.exp2(score - peak).astype(jnp.bfloat16)
        both = matmul(values_t, weights)
        total = both[head_dim : head_dim + 8]
        result = (both[:head_dim] / total[0:1]).T.astype(jnp.bfloat16)
        o_ref[base : base + GROUP, first : first + HALF] = result.reshape(GROUP, HALF, head_dim)
        lse_ref[half, base // GROUP] = jnp.log2(total) + peak


def attend_kernel(scale, q_ref, kv_ref, low_ref, o_ref, lse_ref):
    for half in range(q_ref.shape[2] // HALF):
        attend_half(
            scale, half, q_ref.at[0], kv_ref.at[0], low_ref.at[0], o_ref.at[0], lse_ref.at[0]
        )


def attend(query, pairs, low, scale):
    seqs, heads, block, head_dim = query.shape
    span = pairs.shape[1]
    return pl.pallas_call(
        functools.partial(attend_kernel, scale),
        grid=(seqs,),
        in_specs=[
            row((1, heads, block, head_dim), lambda b: (b, 0, 0, 0)),
            row((1, span, 2 * head_dim), lambda b: (b, 0, 0)),
            row((1, 1, block), lambda b: (b, 0, 0)),
        ],
        out_specs=[
            row((1, heads, block, head_dim), lambda b: (b, 0, 0, 0)),
            row(
                (1, block // HALF, heads // GROUP, 8, GROUP * HALF), lambda b: (b, 0, 0, 0, 0)
            ),
        ],
        out_shape=[
            jax.ShapeDtypeStruct(query.shape, jnp.bfloat16),
            jax.ShapeDtypeStruct(
                (seqs, block // HALF, heads // GROUP, 8, GROUP * HALF), jnp.float32
            ),
        ],
        compiler_params=params(),
        name="attend",
    )(query, pairs, low[:, None, :])


def attend_back_half(
    scale, half, q_ref, kv_ref, low_ref, lse_ref, o_ref, do_ref, cos_ref, sin_ref, put_dq, dkv_ref
):
    heads, block, head_dim = q_ref.shape
    span = kv_ref.shape[0] - (block - HALF)
    factor = scale * LOG2E
    lanes = GROUP * HALF
    first = half * HALF
    window = slice(first, first + span)
    keys, values = kv_ref[window, :head_dim], kv_ref[window, head_dim:]
    keys_t = keys.T
    bias = window_bias(low_ref, first, span)
    cosine = cos_ref[first : first + HALF][None]
    sine = sin_ref[first : first + HALF][None]

    for base in range(0, heads, GROUP):
        here = (slice(base, base + GROUP), slice(first, first + HALF))
        query = q_ref[here].reshape(lanes, head_dim)
        grad = do_ref[here].reshape(lanes, head_dim)
        mixed = o_ref[here].reshape(lanes, head_dim)
        product = grad.astype(jnp.float32) * mixed.astype(jnp.float32)
        delta = jnp.sum(product.T, axis=0, keepdims=True)
        lse = lse_ref[half, base // GROUP, 0:1]
        score = right_times(keys, query)
        weights = jnp.exp2((score * factor - lse) + bias)
        low_weights = weights.astype(jnp.bfloat16)
        dkv_ref[window, head_dim:] += matmul(low_weights, grad)
        slope = right_times(values, grad)
        slope = (weights * (slope - delta)).astype(jnp.bfloat16)
        dkv_ref[window, :head_dim] += matmul(slope, query) * scale
        dq = (matmul(keys_t, slope).T * scale).reshape(GROUP, HALF, head_dim)
        turned = pltpu.roll(dq.reshape(lanes, head_dim), head_dim // 2, 1)
        dq = dq * cosine - turned.reshape(GROUP, HALF, head_dim) * sine
        put_dq(base, first, dq.astype(jnp.bfloat16))


def attend_back_kernel(
    scale, q_ref, kv_ref, low_ref, lse_ref, o_ref, do_ref, cos_ref, sin_ref, dq_ref, dkv_ref
):
    dkv_ref[...] = jnp.zeros_like(dkv_ref)

    def put_dq(base, first, dq):
        dq_ref[0, base : base + GROUP, first : first + HALF] = dq

    for half in range(q_ref.shape[2] // HALF):
        attend_back_half(
            scale,
            half,
            q_ref.at[0],
            kv_ref.at[0],
            low_ref.at[0],
            lse_ref.at[0],
            o_ref.at[0],
            do_ref.at[0],
            cos_ref,
            sin_ref,
            put_dq,
            dkv_ref.at[0],
        )


def attend_back(query, pairs, low, lse, mixed, grad, cosine, sine, scale):
    seqs, heads, block, head_dim = query.shape
    span = pairs.shape[1]
    per_head = row((1, heads, block, head_dim), lambda b: (b, 0, 0, 0))
    table = row((block, head_dim), lambda b: (b, 0))
    return pl.pallas_call(
        functools.partial(attend_back_kernel, scale),
        grid=(seqs,),
        in_specs=[
            per_head,
            row((1, span, 2 * head_dim), lambda b: (b, 0, 0)),
            row((1, 1, block), lambda b: (b, 0, 0)),
            row((1,) + lse.shape[1:], lambda b: (b, 0, 0, 0, 0)),
            per_head,
            per_head,
            table,
            table,
        ],
        out_specs=[per_head, row((1, span, 2 * head_dim), lambda b: (b, 0, 0))],
        out_shape=[
            jax.ShapeDtypeStruct(query.shape, jnp.bfloat16),
            jax.ShapeDtypeStruct(pairs.shape, jnp.float32),
        ],
        compiler_params=params(),
        name="attend_back",
    )(query, pairs, low[:, None, :], lse, mixed, grad, cosine, sine)


def gelu_parts(gate):
    cube = 0.044715 * gate * gate
    bend = jnp.tanh(0.7978845608028654 * gate * (1.0 + cube))
    half = 0.5 * (1.0 + bend)
    value = gate * half
    slope = half + gate * (half * (1.0 - bend)) * (0.7978845608028654 * (1.0 + 3.0 * cube))
    return value, slope


def feed_kernel(own, scattered, far, x_ref, o_ref, g_ref, gains_ref, full_ref, shard_ref, *refs):
    y_ref, dx_ref, do_ref, dgain_ref, dout_ref, dff_ref = refs[:6]
    far_ref, refs = refs[6], refs[7:]
    shares, refs = refs[:scattered], refs[scattered:]
    outw, ff, mixed, normed, normed_t, g_t, y_acc, dh_acc, m_all, dgate_all, dup_all, grads = refs[
        :12
    ]
    in_sem, out_sem = refs[12:14]
    rows, width = g_ref.shape
    seqs, heads, block, head_dim = o_ref.shape
    step = ff.shape[-1] // 3
    tiles = rows // ROW_TILE
    shard_rows = width // 32
    near = FF_CHUNKS - far
    gain = gains_ref[1:2]
    if own:
        greet(neighbours())
        count = Scatter.BUFFERS
        buffers = [refs[14 + count * k : 14 + count * (k + 1)] for k in range(scattered)]
        plans = [(grads.at[k % 2], None, None, shares[k]) for k in range(scattered)]
        refs = refs[14 + count * scattered :]
        scatter = Scatter(plans, buffers, refs[0])
        if far:
            wide = 3 * step
            pieces = [
                (shard_ref, far_ref, k * wide, k * wide + wide // 2, (k + 1) * wide)
                for k in range(far)
            ]
            gather = Gather(refs[1], refs[2], pieces)

    def run(place):
        if own:
            for kind, number, chunk in FEED_ORDER[place]:
                (gather, scatter)[kind].step(number, chunk)

    def load(chunk):
        source, start = full_ref, width + chunk * 3 * step
        if chunk >= near:
            source, start = far_ref, (chunk - near) * 3 * step
        return pltpu.make_async_copy(
            source.at[:, :, :, :, :, pl.ds(start, 3 * step)], ff.at[chunk % 2], in_sem.at[chunk % 2]
        )

    def weights(slot, index):
        return ff[slot, :, :, :, :, :, index * step : (index + 1) * step].reshape(width, step)

    def store(chunk):
        return pltpu.make_async_copy(
            grads.at[chunk % 2], dff_ref.at[chunk - scattered], out_sem.at[chunk % 2]
        )

    run(0)
    out_load = pltpu.make_async_copy(
        full_ref.at[:, :, :, :, :, pl.ds(0, width)], outw, in_sem.at[2]
    )
    out_load.start()
    load(0).start()
    x_load = pltpu.make_async_copy(x_ref, normed, in_sem.at[3])
    x_load.start()
    x_load.wait()
    out_load.wait()

    def here(tile):
        return pl.ds(pl.multiple_of(tile * ROW_TILE, ROW_TILE), ROW_TILE)

    def prologue(tile):
        part = here(tile)
        attended = jnp.concatenate([o_ref[tile, h] for h in range(heads)], axis=1)
        x1 = normed[part].astype(jnp.float32) + right_times(attended, outw[...].reshape(width, width))
        mixed[part] = x1
        y_acc[part] = x1
        low = (x1 * inverse_rms(x1) * gain).astype(jnp.bfloat16)
        normed[part] = low
        normed_t[:, part] = low.T
        g_t[:, part] = g_ref[part].T
        dh_acc[part] = jnp.zeros((ROW_TILE, width), jnp.float32)

    for tile in range(tiles):
        prologue(tile)
        run(1 + tile)
    at = 1 + tiles
    for chunk in range(FF_CHUNKS):
        slot = chunk % 2
        if chunk >= near:
            load(chunk).start()
        load(chunk).wait()
        if chunk + 1 < near:
            load(chunk + 1).start()

        def forth(tile):
            part = pl.ds(tile * FEED_TILE, FEED_TILE)
            low, grad = normed[part], g_ref[part]
            gate = matmul(low, weights(slot, 0))
            up_part = matmul(low, weights(slot, 1))
            dm = matmul(grad, weights(slot, 2))
            value, slope = gelu_parts(gate)
            m = (value * up_part).astype(jnp.bfloat16)
            dgate = (dm * up_part * slope).astype(jnp.bfloat16)
            dup = (dm * value).astype(jnp.bfloat16)
            m_all[part], dgate_all[part], dup_all[part] = m, dgate, dup
            y_acc[part] += right_times(m, weights(slot, 2))
            dh_acc[part] += right_times(dgate, weights(slot, 0)) + right_times(
                dup, weights(slot, 1)
            )

        def grads_of(tile):
            part = pl.ds(tile * (width // 2), width // 2)
            for i, (left, right) in enumerate(
                ((normed_t, dgate_all), (normed_t, dup_all), (g_t, m_all))
            ):
                value = matmul(left[part], right[...]).astype(jnp.bfloat16)
                grads[slot, tile, :, :, :, :, i * step : (i + 1) * step] = value.reshape(
                    2, 4, 2, shard_rows, step
                )

        for tile in range(2):
            forth(tile)
            run(at + tile)
        if chunk - 2 >= scattered:
            store(chunk - 2).wait()
        for tile in range(2):
            grads_of(tile)
            run(at + 2 + tile)
        at += 4
        if chunk >= scattered:
            store(chunk).start()

    dgain_ref[...] = jnp.zeros_like(dgain_ref)

    @pl.loop(0, tiles)
    def _(tile):
        part = here(tile)
        normed[part] = y_acc[part].astype(jnp.bfloat16)
        x1, dh = mixed[part], dh_acc[part]
        scale = inverse_rms(x1)
        dgain_ref[0:1] += jnp.sum(dh * x1 * scale, axis=0, keepdims=True)
        dx = g_ref[part].astype(jnp.float32) + rms_back(x1, scale, gain, dh)
        mixed[part] = dx
        low = dx.astype(jnp.bfloat16)
        g_t[:, part] = low.T
        back = matmul(low, outw[...].reshape(width, width)).astype(jnp.bfloat16)
        for h in range(heads):
            do_ref[tile, h] = back[:, h * head_dim : (h + 1) * head_dim]

    outs = [
        pltpu.make_async_copy(normed, y_ref, in_sem.at[0]),
        pltpu.make_async_copy(mixed, dx_ref, in_sem.at[1]),
    ]
    for out in outs:
        out.start()
    run(at)

    @pl.loop(0, width // ROW_TILE)
    def _(tile):
        part = here(tile)
        for h in range(0, heads, 2):
            for s in range(seqs):
                pair = jnp.concatenate([o_ref[s, h], o_ref[s, h + 1]], axis=1)
                term = matmul(g_t[part, s * block : (s + 1) * block], pair)
                total = term if s == 0 else total + term
            lanes = slice(h * head_dim, (h + 2) * head_dim)
            ff[0, tile // 2, lax.rem(tile, 2), :, :, :, lanes] = total.astype(
                jnp.bfloat16
            ).reshape(4, 2, shard_rows, 2 * head_dim)

    outs.append(
        pltpu.make_async_copy(
            ff.at[0, :, :, :, :, :, pl.ds(0, width)], dout_ref, in_sem.at[2]
        )
    )
    outs[-1].start()
    run(at + 1)
    for chunk in range(max(scattered, FF_CHUNKS - 2), FF_CHUNKS):
        store(chunk).wait()
    for out in outs:
        out.wait()


def feed(own, scattered, far, x, mixed_heads, grad, gains, full, shard, hidden):
    rows, width = x.shape
    step = hidden // FF_CHUNKS
    low = jnp.bfloat16
    chunk = (2, 2, 4, 2, width // 32, 3 * step)
    kept = FF_CHUNKS - scattered
    options = {"collective_id": 3, "has_side_effects": True} if own else {}
    return pl.pallas_call(
        functools.partial(feed_kernel, own, scattered, far),
        in_specs=[hbm(), vmem(), vmem(), vmem(), hbm(), hbm()],
        out_specs=[hbm(), hbm(), vmem(), vmem(), hbm(), hbm(), hbm()] + [vmem()] * scattered,
        out_shape=[
            jax.ShapeDtypeStruct((rows, width), low),
            jax.ShapeDtypeStruct((rows, width), jnp.float32),
            jax.ShapeDtypeStruct(mixed_heads.shape, low),
            jax.ShapeDtypeStruct((8, width), jnp.float32),
            jax.ShapeDtypeStruct(chunk[:-1] + (width,), low),
            jax.ShapeDtypeStruct((kept,) + chunk, low),
            jax.ShapeDtypeStruct(chunk[:-1] + (max(1, far) * 3 * step,), low),
        ]
        + [jax.ShapeDtypeStruct((width // 32, 3 * step), jnp.float32)] * scattered,
        scratch_shapes=[
            pltpu.VMEM(chunk[:-1] + (width,), low),
            pltpu.VMEM((2,) + chunk, low),
            pltpu.VMEM((rows, width), jnp.float32),
            pltpu.VMEM((rows, width), low),
            pltpu.VMEM((width, rows), low),
            pltpu.VMEM((width, rows), low),
            pltpu.VMEM((rows, width), jnp.float32),
            pltpu.VMEM((rows, width), jnp.float32),
            pltpu.VMEM((rows, step), low),
            pltpu.VMEM((rows, step), low),
            pltpu.VMEM((rows, step), low),
            pltpu.VMEM((2,) + chunk, low),
            pltpu.SemaphoreType.DMA((4,)),
            pltpu.SemaphoreType.DMA((2,)),
        ]
        + (Scatter.scratch([3 * step] * scattered, width // 32) if own else [])
        + (Gather.scratch(far) if far else []),
        compiler_params=params(**options),
        name="feed",
    )(x, mixed_heads, grad, gains, full, shard)


def finish_rows(x, dx, grad, w_ref, gain):
    dh = right_times(grad, w_ref[:, : grad.shape[1]])
    x = x.astype(jnp.float32)
    scale = inverse_rms(x)
    total = (dx + rms_back(x, scale, gain, dh)).astype(jnp.bfloat16)
    return total, jnp.sum(dh * x * scale, axis=0, keepdims=True)


def finish_kernel(
    x_ref, ht_ref, dq_ref, dkv_ref, gains_ref, dx_ref, w_ref, dw_ref, dxo_ref, dgain_ref, dall
):
    width = x_ref.shape[1]
    seqs, heads, block, _ = dq_ref.shape
    dgain_ref[...] = jnp.zeros_like(dgain_ref)

    @pl.loop(0, seqs)
    def _(tile):
        part = pl.ds(pl.multiple_of(tile * block, block), block)
        grad = jnp.concatenate([dq_ref[tile, h] for h in range(heads)] + [dkv_ref[tile]], axis=1)
        dall[part] = grad
        dxo_ref[part], terms = finish_rows(
            x_ref[part], dx_ref[part], grad, w_ref, gains_ref[0:1]
        )
        dgain_ref[0:1] += terms

    @pl.loop(0, width // ROW_TILE)
    def _(tile):
        part = pl.ds(pl.multiple_of(tile * ROW_TILE, ROW_TILE), ROW_TILE)
        dw_ref[part] = matmul(ht_ref[part], dall[...]).astype(jnp.bfloat16)


def finish(x, normed_t, dq, dkv, gains, dx, weights):
    rows, width = x.shape
    columns = width + dkv.shape[2]
    return pl.pallas_call(
        finish_kernel,
        in_specs=[vmem()] * 7,
        out_specs=[vmem()] * 3,
        out_shape=[
            jax.ShapeDtypeStruct((width, columns), jnp.bfloat16),
            jax.ShapeDtypeStruct((rows, width), jnp.bfloat16),
            jax.ShapeDtypeStruct((8, width), jnp.float32),
        ],
        scratch_shapes=[pltpu.VMEM((rows, columns), jnp.bfloat16)],
        compiler_params=params(),
        name="finish",
    )(x, normed_t, dq, dkv, gains, dx, weights)


def segments_kernel(segments_ref, all_ref, sems):
    x, c, z, y = place()
    others = [device(x, c, z, 1 - y)]
    for hop in (1, 2, 3):
        others += [device(x, c, lax.rem(z + hop, 4), there) for there in (y, 1 - y)]
    greet(others)
    mine = all_ref.at[z * 2 + y]
    keep = pltpu.make_async_copy(segments_ref, mine, sems.at[2, 0])
    keep.start()
    copies = [
        remote(segments_ref, mine, sems.at[0, i], sems.at[1, i], partner)
        for i, partner in enumerate(others)
    ]
    for copy in copies:
        copy.start()
    keep.wait()
    for copy in copies:
        copy.wait()


def gather_segments(segments):
    return pl.pallas_call(
        segments_kernel,
        out_shape=jax.ShapeDtypeStruct((8,) + segments.shape, segments.dtype),
        in_specs=[hbm()],
        out_specs=hbm(),
        scratch_shapes=[pltpu.SemaphoreType.DMA((3, 8))],
        compiler_params=pltpu.CompilerParams(collective_id=0, has_side_effects=True),
        name="gather_segments",
    )(segments)


def front_kernel(
    scale,
    ranges,
    x_ref,
    cos_ref,
    sin_ref,
    low_ref,
    first_ref,
    shard_ref,
    ht_ref,
    q_ref,
    pairs_ref,
    gains_ref,
    o_ref,
    lse_ref,
    full_ref,
    w_ref,
    window,
    w_all,
    sems,
    local_sems,
    window_sems,
    out_sems,
):
    seqs, heads, block, head_dim = q_ref.shape
    width = heads * head_dim
    reach = window.shape[1] - block
    window[:, :reach] = jnp.zeros((seqs, reach, 2 * head_dim), window.dtype)
    greet(neighbours())
    refs = ((first_ref, w_all), (shard_ref, full_ref))
    gather = Gather(sems, local_sems, [refs[i] + tuple(rest) for i, *rest in ranges])
    windows = Windows(window, window_sems, block)

    def run(place):
        for kind, number, index in FRONT_ORDER[place]:
            if kind == 0:
                gather.step(number, index)
            else:
                (windows.once, windows.twice, windows.all)[number](index)

    def columns(start, end):
        return w_all[:, :, :, :, :, start:end].reshape(width, end - start)

    run(0)
    gains_ref[...] = gain_rows(columns, width + 2 * head_dim)

    @pl.loop(0, seqs)
    def _(seq):
        part = pl.ds(pl.multiple_of(seq * block, block), block)
        project_block(
            x_ref.at[part],
            cos_ref.at[part],
            sin_ref.at[part],
            columns,
            gains_ref[0:1],
            ht_ref.at[:, part],
            q_ref.at[seq],
            window.at[seq, pl.ds(reach, block)],
        )
        windows.own(seq)
        for index in range(seqs - 1):
            if FRONT_ORDER[1 + index]:
                pl.when(seq == index)(lambda: run(1 + index))

    run(seqs)
    halves = block // HALF

    @pl.loop(0, seqs)
    def _(seq):
        for half in range(halves):
            attend_half(
                scale,
                half,
                q_ref.at[seq],
                window.at[seq],
                low_ref.at[seq],
                o_ref.at[seq],
                lse_ref.at[seq],
            )
            for index in range(seqs):
                number = seqs + 1 + index * halves + half
                if FRONT_ORDER[number] and number < seqs * (1 + halves):
                    pl.when(seq == index)(lambda: run(number))

    outs = [
        pltpu.make_async_copy(window, pairs_ref, out_sems.at[0]),
        pltpu.make_async_copy(w_all, w_ref, out_sems.at[1]),
    ]
    for out in outs:
        out.start()
    run(seqs * (1 + halves))

    @pl.loop(0, seqs)
    def _(seq):
        windows.drain(seq)

    for out in outs:
        out.wait()


def front(x, cosine, sine, low, first, shard, scale, ranges, seqs, heads, head_dim):
    rows, width = x.shape
    block = rows // seqs
    shard_rows, columns = shard.shape
    low_type = jnp.bfloat16
    span = 5 * block
    lse = (seqs, block // HALF, heads // GROUP, 8, GROUP * HALF)
    stacked = (2, 2, 4, 2, shard_rows)
    return pl.pallas_call(
        functools.partial(front_kernel, scale, ranges),
        in_specs=[vmem()] * 4 + [hbm()] * 2,
        out_specs=[vmem(), vmem(), hbm(), vmem(), vmem(), vmem(), hbm(), hbm()],
        out_shape=[
            jax.ShapeDtypeStruct((width, rows), low_type),
            jax.ShapeDtypeStruct((seqs, heads, block, head_dim), low_type),
            jax.ShapeDtypeStruct((seqs, span, 2 * head_dim), low_type),
            jax.ShapeDtypeStruct((8, width), jnp.float32),
            jax.ShapeDtypeStruct((seqs, heads, block, head_dim), low_type),
            jax.ShapeDtypeStruct(lse, jnp.float32),
            jax.ShapeDtypeStruct(stacked + (columns,), low_type),
            jax.ShapeDtypeStruct(stacked + (first.shape[1],), low_type),
        ],
        scratch_shapes=[
            pltpu.VMEM((seqs, span, 2 * head_dim), low_type),
            pltpu.VMEM(stacked + (first.shape[1],), low_type),
        ]
        + Gather.scratch(len(ranges))
        + [
            pltpu.SemaphoreType.DMA((2, Windows.KINDS, seqs)),
            pltpu.SemaphoreType.DMA((2,)),
        ],
        compiler_params=params(collective_id=2, has_side_effects=True),
        name="front",
    )(x, cosine, sine, low[:, None, :], first, shard)


class WindowGrads:
    def __init__(self, windows, grads, out, came, sems, block):
        self.windows, self.grads, self.out, self.came = windows, grads, out, came
        self.sems, self.block = sems, block

    def rows(self, seq, distance):
        start = (4 - distance) * self.block
        if not isinstance(distance, int):
            start = pl.multiple_of(start, self.block)
        return self.grads.at[seq, pl.ds(start, self.block)]

    def copy(self, kind, seq):
        x, c, z, y = place()
        over = device(x, c, z, 1 - y)
        partner = device(x, c, lax.rem(z + 3, 4), y) if kind < 2 else over
        return remote(
            self.out.at[kind, seq],
            self.came.at[kind, seq],
            self.sems.at[0, kind, seq],
            self.sems.at[1, kind, seq],
            partner,
        )

    def start(self, kind, seq, distance):
        @pl.when(self.windows.gets(kind))
        def _():
            self.out[kind, seq] = self.rows(seq, distance)[...].astype(jnp.bfloat16)
            self.copy(kind, seq).start()

    def add(self, kind, seq, distance):
        @pl.when(self.windows.sends(kind))
        def _():
            self.copy(kind, seq).wait_recv()
            target = self.rows(seq, distance)
            target[...] += self.came[kind, seq].astype(jnp.float32)

    def step(self, number, seq):
        _, _, _, y = place()
        if number == 0:
            self.start(4, seq, 3)
            self.start(3, seq, 1 + 2 * y)
            self.start(2, seq, 1)
        elif number == 1:
            self.add(4, seq, 4)
            self.start(1, seq, 4)
            self.add(3, seq, 2)
        elif number == 2:
            self.add(1, seq, 2)
            self.start(0, seq, 2)
        else:
            self.add(0, seq, 0)
            self.add(2, seq, 0)

    def drain(self, seq):
        for kind in range(Windows.KINDS):
            pl.when(self.windows.gets(kind))(lambda: self.copy(kind, seq).wait_send())


def back_kernel(scale, kept, last_chunks, *refs):
    (
        q_ref,
        pairs_ref,
        low_ref,
        lse_ref,
        o_ref,
        do_ref,
        cos_ref,
        sin_ref,
        x_ref,
        ht_ref,
        gains_ref,
        dgain_ref,
        w_ref,
        dx_ref,
        dout_ref,
        dff_ref,
    ) = refs[:16]
    dxo_ref, refs = refs[16], refs[17:]
    total = kept + 1 + len(last_chunks)
    shares, refs = refs[:total], refs[total:]
    grads, out, came, dall, dx, dgains, dw, load_sems, dx_sems, grad_sems = refs[:10]
    mines, refs = refs[10 : 11 + kept], refs[11 + kept :]
    count = Scatter.BUFFERS
    buffers = [refs[count * k : count * (k + 1)] for k in range(total)]
    sems = refs[count * total]
    seqs, heads, block, head_dim = q_ref.shape
    width = heads * head_dim

    grads[...] = jnp.zeros_like(grads)
    dgains[...] = jnp.zeros_like(dgains)
    dgains[1:2] = dgain_ref[0:1]
    greet(neighbours())
    sources = [dff_ref.at[k] for k in range(kept)] + [dout_ref]
    plans = [(s, mines[k], load_sems.at[k], shares[k]) for k, s in enumerate(sources)]
    for k, (start, end) in enumerate(last_chunks):
        source = dw.at[:, :, :, :, :, pl.ds(start, end - start)]
        plans.append((source, None, None, shares[kept + 1 + k]))
    scatter = Scatter(plans, buffers, sems)
    windows = Windows(None, None, block)
    back = WindowGrads(windows, grads, out, came, grad_sems, block)
    halves = block // HALF

    def load(seq):
        return pltpu.make_async_copy(
            dx_ref.at[pl.ds(seq * block, block)], dx.at[seq % 2], dx_sems.at[seq % 2]
        )

    load(0).start()
    load(1).start()

    def finish_one(seq):
        part = pl.ds(seq * block, block)
        own = grads[seq, 4 * block :]
        key, value = own[:, :head_dim], own[:, head_dim:]
        turned = pltpu.roll(key, head_dim // 2, 1)
        key = key * cos_ref[part] - turned * sin_ref[part]
        dall[part, width : width + head_dim] = key.astype(jnp.bfloat16)
        dall[part, width + head_dim :] = value.astype(jnp.bfloat16)
        load(seq).wait()
        dxo_ref[part], terms = finish_rows(
            x_ref[part], dx[seq % 2], dall[part], w_ref, gains_ref[0:1]
        )
        dgains[0:1] += terms
        if seq + 2 < seqs:
            load(seq + 2).start()

    def weight_grads(start, end):
        @pl.loop(0, 2)
        def _(tile):
            part = pl.ds(pl.multiple_of(tile * (width // 2), width // 2), width // 2)
            value = matmul(ht_ref[part], dall[:, start:end]).astype(jnp.bfloat16)
            dw[tile, :, :, :, :, start:end] = value.reshape(
                (2,) + dw.shape[2:5] + (end - start,)
            )

    def weight_tail():
        weight_grads(width, width + 2 * head_dim)
        gains = dgains[...].T.astype(jnp.bfloat16)
        dw[:, :, :, :, :, width + 2 * head_dim :] = gains.reshape(
            dw.shape[:5] + (gains.shape[1],)
        )

    def run(place):
        for kind, number, index in BACK_ORDER[place]:
            if kind == 0:
                scatter.step(number, index)
            elif kind == 1:
                back.step(number, index)
            elif kind == 2:
                weight_grads(0, width)
            elif kind == 3:
                finish_one(number)
            else:
                weight_tail()

    run(0)

    @pl.loop(0, seqs)
    def _(seq):
        part = pl.ds(pl.multiple_of(seq * block, block), block)

        def put_dq(base, first, dq):
            there = pl.ds(pl.multiple_of(seq * block + first, HALF), HALF)
            for h in range(GROUP):
                dall[there, (base + h) * head_dim : (base + h + 1) * head_dim] = dq[h]

        for half in range(halves):
            attend_back_half(
                scale,
                half,
                q_ref.at[seq],
                pairs_ref.at[seq],
                low_ref.at[seq],
                lse_ref.at[seq],
                o_ref.at[seq],
                do_ref.at[seq],
                cos_ref.at[part],
                sin_ref.at[part],
                put_dq,
                grads.at[seq],
            )
            for index in range(seqs):
                number = 1 + index * halves + half
                if BACK_ORDER[number] and number < seqs * halves:
                    pl.when(seq == index)(lambda: run(number))

    run(seqs * halves)

    @pl.loop(0, seqs)
    def _(seq):
        back.drain(seq)


def back(
    query, pairs, low, lse, mixed, grad, cosine, sine, x, normed_t, gains, dgain, weights, dx, dout, dff, scale
):
    seqs, heads, block, head_dim = query.shape
    rows, width = x.shape
    columns = weights.shape[1]
    kept = dff.shape[0]
    shard_rows = dff.shape[-2]
    low_type = jnp.bfloat16
    span = pairs.shape[1]
    last_chunks = ((0, width // 2), (width // 2, width), (width, columns))
    widths = [dff.shape[-1]] * kept + [width] + [end - start for start, end in last_chunks]
    lanes = 2 * head_dim
    out = pl.pallas_call(
        functools.partial(back_kernel, scale, kept, last_chunks),
        in_specs=[vmem()] * 13 + [hbm()] * 3,
        out_specs=[vmem()] * (1 + len(widths)),
        out_shape=[jax.ShapeDtypeStruct((rows, width), low_type)]
        + [jax.ShapeDtypeStruct((shard_rows, n), jnp.float32) for n in widths],
        scratch_shapes=[
            pltpu.VMEM((seqs, span, lanes), jnp.float32),
            pltpu.VMEM((Windows.KINDS, seqs, block, lanes), low_type),
            pltpu.VMEM((Windows.KINDS, seqs, block, lanes), low_type),
            pltpu.VMEM((rows, width + lanes), low_type),
            pltpu.VMEM((2, block, width), jnp.float32),
            pltpu.VMEM((128, width), jnp.float32),
            pltpu.VMEM((2, 2, 4, 2, shard_rows, columns), low_type),
            pltpu.SemaphoreType.DMA((kept + 1,)),
            pltpu.SemaphoreType.DMA((2,)),
            pltpu.SemaphoreType.DMA((2, Windows.KINDS, seqs)),
        ]
        + [pltpu.VMEM((2, 4, 2, shard_rows, n), low_type) for n in widths[: kept + 1]]
        + Scatter.scratch(widths, shard_rows, 2 / 3),
        compiler_params=params(collective_id=4, has_side_effects=True),
        name="back",
    )(
        query,
        pairs,
        low[:, None, :],
        lse,
        mixed,
        grad,
        cosine,
        sine,
        x,
        normed_t,
        gains,
        dgain,
        weights,
        dx,
        dout,
        dff,
    )
    return out[0], out[1 : 1 + kept], out[1 + kept], jnp.concatenate(out[2 + kept :], axis=1)


def stack_ff(gate, up_part, down_t):
    rows, hidden = gate.shape
    parts = [p.reshape(rows, FF_CHUNKS, hidden // FF_CHUNKS) for p in (gate, up_part, down_t)]
    return jnp.stack(parts, axis=2).reshape(rows, 3 * hidden)


def unstack_ff(stacked):
    rows, hidden = stacked.shape[0], stacked.shape[1] // 3
    parts = stacked.reshape(rows, FF_CHUNKS, 3, hidden // FF_CHUNKS)
    return [parts[:, :, i].reshape(rows, hidden) for i in range(3)]


def shifted(value, axis, steps):
    count = lax.axis_size(axis)
    initial, last = (max(0, -steps), min(count, count - steps))
    return lax.ppermute(value, axis, [(source, source + steps) for source in range(initial, last)])


def on_device(
    own_links,
    tokens,
    segments,
    cotangent,
    first_gain,
    query_weight,
    key_weight,
    value_weight,
    out_weight,
    second_gain,
    gate_weight,
    up_weight,
    down_weight,
):
    seqs, block_len, width = tokens.shape
    head_dim = key_weight.shape[1]
    heads = query_weight.shape[1] // head_dim
    hidden = gate_weight.shape[1]
    shard_rows = first_gain.shape[0]
    reach = (WINDOW - 1 + block_len - 1) // block_len
    scale = head_dim ** (-0.5)
    rows = seqs * block_len
    keys_from = width + 2 * head_dim
    inputs = tokens.reshape(rows, width)
    grad_rows = cotangent.reshape(rows, width)

    gains = jnp.zeros((shard_rows, 128), first_gain.dtype)
    gains = gains.at[:, 0].set(first_gain).at[:, 1].set(second_gain)
    shard = jnp.concatenate([query_weight, key_weight, value_weight, gains], axis=1)
    later = jnp.concatenate(
        [out_weight.T, stack_ff(gate_weight, up_weight, down_weight.T)], axis=1
    )
    if own_links:
        all_segments = gather_segments(segments)
        earlier = all_segments.transpose(1, 0, 2).reshape(seqs, -1)
    else:
        weights = lax.all_gather(shard, ("batch", "seq"), axis=0, tiled=True)
        full = lax.all_gather(later, ("batch", "seq"), axis=0, tiled=True)
        earlier = lax.all_gather(segments, "seq", axis=1, tiled=True)

    starts = jnp.sum(earlier[:, None, :] < segments[:, :, None], axis=-1, dtype=jnp.int32)
    query_place = jnp.arange(block_len, dtype=jnp.int32) + lax.axis_index("seq") * block_len
    low = jnp.maximum(starts, query_place[None, :] - (WINDOW - 1))
    low = low - (query_place[0] - reach * block_len)
    cosine, sine = tables((query_place[None, :] - starts).reshape(-1), head_dim)

    if own_links:
        step = 3 * hidden // FF_CHUNKS
        near, rest = later[:, : width + (FF_CHUNKS - FAR) * step], later[:, -FAR * step :]
        ranges = [(0, 0, 256, 512), (0, 512, 768, width), (0, width, width + 256, keys_from + 128)]
        ranges += [(1, start, start + 384, start + 512) for start in range(0, width, 512)]
        half = step // 2
        for start in range(width, near.shape[1], half):
            ranges.append((1, start, start + 2 * half // 3, start + half))
        normed_t, query, pairs, gains, mixed, lse, full, weights = front(
            inputs, cosine, sine, low, shard, near, scale, ranges, seqs, heads, head_dim
        )
        weights = weights.reshape(width, -1)
        scattered, far = SCATTERED, FAR
    else:
        normed_t, query, own_pairs, gains = project(
            inputs, cosine, sine, weights, seqs, heads, head_dim
        )
        pieces = [shifted(own_pairs, "seq", distance) for distance in range(reach, 0, -1)]
        pairs = jnp.concatenate(pieces + [own_pairs], axis=1)
        mixed, lse = attend(query, pairs, low, scale)
        scattered, far, rest = 0, 0, later
        full = full.reshape(2, 2, 4, 2, width // 32, -1)
    output, grad_mixed, grad_heads, dgain_two, grad_out_t, grad_ff, _, *shares = feed(
        own_links, scattered, far, inputs, mixed, grad_rows, gains, full, rest, hidden
    )
    if own_links:
        grad_input, more, share_out, share_first = back(
            query,
            pairs,
            low,
            lse,
            mixed,
            grad_heads,
            cosine,
            sine,
            inputs,
            normed_t,
            gains,
            dgain_two,
            weights,
            grad_mixed,
            grad_out_t,
            grad_ff,
            scale,
        )
        share_ff = jnp.concatenate(list(shares) + list(more), axis=1)
    else:
        grad_query, grad_pairs = attend_back(
            query, pairs, low, lse, mixed, grad_heads, cosine, sine, scale
        )
        own_grad = grad_pairs[:, reach * block_len :]
        for distance in range(1, reach + 1):
            start = (reach - distance) * block_len
            piece = grad_pairs[:, start : start + block_len].astype(jnp.bfloat16)
            own_grad = own_grad + shifted(piece, "seq", -distance).astype(own_grad.dtype)
        grad_key = own_grad[..., :head_dim].reshape(rows, head_dim)
        grad_key = grad_key * cosine - jnp.roll(grad_key, head_dim // 2, axis=1) * sine
        grad_kv = jnp.concatenate(
            [grad_key.reshape(seqs, block_len, head_dim), own_grad[..., head_dim:]], axis=-1
        ).astype(jnp.bfloat16)
        grad_qkv_w, grad_input, dgain_one = finish(
            inputs, normed_t, grad_query, grad_kv, gains, grad_mixed, weights
        )
        grad_gains = jnp.zeros((width, 128), jnp.bfloat16)
        grad_gains = grad_gains.at[:, 0].set(dgain_one[0].astype(jnp.bfloat16))
        grad_gains = grad_gains.at[:, 1].set(dgain_two[0].astype(jnp.bfloat16))
        grad_ff = grad_ff.reshape(FF_CHUNKS, width, -1)
        grad_out_t = grad_out_t.reshape(width, -1)
        grads = jnp.concatenate([grad_qkv_w, grad_gains, grad_out_t] + list(grad_ff), axis=1)
        share = lax.psum_scatter(grads, ("batch", "seq"), scatter_dimension=0, tiled=True)
        share = share.astype(jnp.float32)
        share_first = share[:, : keys_from + 128]
        share_out = share[:, keys_from + 128 : keys_from + 128 + width]
        share_ff = share[:, keys_from + 128 + width :]
    share_gate, share_up, share_down_t = unstack_ff(share_ff)
    return (
        output.reshape(tokens.shape),
        grad_input.reshape(tokens.shape),
        share_first[:, keys_from],
        share_first[:, :width],
        share_first[:, width : width + head_dim],
        share_first[:, width + head_dim : keys_from],
        share_out.T,
        share_first[:, keys_from + 1],
        share_gate,
        share_up,
        share_down_t.T,
    )


def solution(mesh):
    both = ("batch", "seq")
    rows_split, columns_split = P(both, None), P(None, both)
    tokens_split, gain_split = P("batch", "seq", None), P(both)
    weights = (
        gain_split,
        rows_split,
        rows_split,
        rows_split,
        columns_split,
        gain_split,
        rows_split,
        rows_split,
        columns_split,
    )
    in_specs = (tokens_split, P("batch", "seq"), tokens_split) + weights
    out_specs = (tokens_split, tokens_split) + weights
    own_links = (mesh.shape["batch"], mesh.shape["seq"]) == (4, 8)
    return jax.shard_map(
        functools.partial(on_device, own_links),
        mesh=mesh,
        in_specs=in_specs,
        out_specs=out_specs,
        check_vma=False,
    )
```

```python
import functools

import jax
import jax.numpy as jnp
from jax import lax
from jax.experimental import pallas as pl
from jax.experimental.pallas import tpu as pltpu
from jax.sharding import PartitionSpec as P

WINDOW = 1024
FF_CHUNKS = 6
SCATTERED = 4
FAR = 2
FEED_TILE = 512
MESH_ID = pl.DeviceIdType.MESH
MIB = 1 << 20


def tables(positions, head_dim):
    inverse = 10000.0 ** (-2.0 * jnp.arange(head_dim // 2, dtype=jnp.float32) / head_dim)
    angle = positions.astype(jnp.float32)[:, None] * inverse[None, :]
    cosine, sine = jnp.cos(angle), jnp.sin(angle)
    return (
        jnp.concatenate([cosine, cosine], axis=-1),
        jnp.concatenate([-sine, sine], axis=-1),
    )


def matmul(left, right):
    return jnp.dot(left, right, preferred_element_type=jnp.float32)


def right_times(left, right):
    return lax.dot_general(
        left, right, (((1,), (1,)), ((), ())), preferred_element_type=jnp.float32
    )


def place():
    batch, seq = lax.axis_index("batch"), lax.axis_index("seq")
    return batch // 2, lax.rem(batch, 2), seq // 2, lax.rem(seq, 2)


def device(x, c, z, y):
    return (x * 2 + c, z * 2 + y)


def greet(partners):
    barrier = pltpu.get_barrier_semaphore()
    for partner in partners:
        pl.semaphore_signal(barrier, inc=1, device_id=partner, device_id_type=MESH_ID)
    pl.semaphore_wait(barrier, len(partners))


def neighbours():
    x, c, z, y = place()
    return [
        device(x, c, lax.rem(z + 1, 4), y),
        device(x, c, lax.rem(z + 2, 4), y),
        device(x, c, lax.rem(z + 3, 4), y),
        device(1 - x, c, z, y),
        device(x, c, z, 1 - y),
        device(x, 1 - c, z, y),
    ]


def remote(source, target, send_sem, recv_sem, partner):
    return pltpu.make_async_remote_copy(
        src_ref=source,
        dst_ref=target,
        send_sem=send_sem,
        recv_sem=recv_sem,
        device_id=partner,
        device_id_type=MESH_ID,
    )


FRONT_ORDER = (
    ((0, 0, 0), (0, 0, 1), (0, 0, 2), (0, 0, 3), (0, 1, 0), (0, 1, 1), (0, 2, 0), (0, 0, 4), (0, 1, 2), (0, 2, 1), (0, 0, 5), (0, 1, 3), (0, 3, 0), (0, 2, 2), (0, 0, 6), (0, 1, 4), (0, 4, 0), (0, 3, 1), (0, 2, 3), (0, 0, 7), (0, 1, 5), (0, 4, 1), (0, 3, 2), (0, 2, 4), (0, 0, 8), (0, 4, 2), (0, 1, 6),),
    ((0, 3, 3),),
    ((0, 2, 5), (0, 1, 7), (0, 4, 3), (0, 0, 9),),
    ((0, 3, 4), (0, 2, 6), (0, 1, 8), (0, 0, 10),),
    ((1, 0, 0), (0, 4, 4), (1, 0, 1), (0, 3, 5), (0, 2, 7), (0, 0, 11), (0, 4, 5), (0, 1, 9), (1, 0, 2), (0, 3, 6), (0, 2, 8), (0, 0, 12), (0, 4, 6), (0, 1, 10), (1, 1, 0), (1, 0, 3), (1, 1, 1), (0, 3, 7), (0, 2, 9), (0, 4, 7), (0, 1, 11), (1, 1, 2), (0, 3, 8), (0, 1, 12), (0, 2, 10), (0, 4, 8), (1, 2, 0),),
    ((1, 1, 3),),
    ((1, 2, 1),),
    (),
    ((0, 3, 9), (0, 2, 11), (1, 2, 2),),
    ((0, 4, 9),),
    ((0, 2, 12), (0, 3, 10), (1, 2, 3),),
    ((0, 4, 10),),
    ((0, 3, 11), (0, 3, 12), (0, 4, 11), (0, 4, 12),),
)

FEED_ORDER = (
    ((0, 0, 0), (0, 0, 1),),
    (),
    (),
    (),
    ((0, 1, 0),),
    (),
    ((0, 2, 0), (0, 1, 1),),
    (),
    ((1, 0, 0),),
    (),
    ((0, 3, 0), (1, 1, 0),),
    ((0, 2, 1),),
    ((1, 0, 1), (0, 4, 0),),
    (),
    ((1, 2, 0), (1, 1, 1),),
    (),
    ((0, 3, 1), (1, 0, 2),),
    ((1, 3, 0),),
    ((0, 4, 1),),
    ((1, 1, 2),),
    ((1, 2, 1), (1, 4, 0), (1, 0, 3),),
    (),
    ((1, 2, 2), (1, 1, 3),),
    ((1, 3, 1),),
    (),
    ((1, 3, 2),),
    ((1, 4, 1), (1, 2, 3),),
    (),
    (),
    ((1, 4, 2), (1, 3, 3),),
    ((1, 4, 3),),
)

BACK_ORDER = (
    ((0, 0, 0), (0, 0, 1), (0, 0, 2),),
    (),
    ((1, 0, 0), (0, 1, 0),),
    ((1, 1, 0), (0, 1, 1), (0, 1, 2),),
    ((1, 2, 0), (1, 0, 1),),
    ((0, 2, 0), (1, 3, 0),),
    ((1, 0, 2),),
    (),
    ((1, 1, 1), (1, 0, 3), (0, 2, 1), (2, 0, 0), (0, 0, 3), (0, 0, 4), (1, 2, 1), (3, 0, 0), (0, 1, 3), (0, 2, 2), (0, 1, 4), (0, 3, 0), (1, 3, 1), (1, 1, 2), (3, 1, 0), (1, 1, 3), (0, 4, 0), (1, 2, 2), (0, 3, 1), (1, 2, 3), (0, 2, 3), (1, 3, 2), (3, 2, 0), (0, 3, 2), (0, 2, 4), (0, 3, 3), (0, 3, 4), (0, 4, 1), (1, 3, 3), (3, 3, 0), (4, 0, 0), (0, 0, 5), (0, 4, 2), (0, 1, 5), (0, 4, 3), (0, 2, 5), (0, 4, 4), (0, 3, 5), (0, 4, 5),),
)


class Gather:
    STEPS = 5
    SEMS = 8

    def __init__(self, sems, local_sems, chunks):
        self.sems, self.local_sems, self.chunks = sems, local_sems, chunks

    @staticmethod
    def scratch(count):
        return [
            pltpu.SemaphoreType.DMA((2, count, Gather.SEMS)),
            pltpu.SemaphoreType.DMA((count,)),
        ]

    def keep(self, chunk):
        x, c, z, y = place()
        shard, full, start, _, end = self.chunks[chunk]
        whole = pl.ds(start, end - start)
        return pltpu.make_async_copy(
            shard.at[:, whole], full.at[x, c, z, y, :, whole], self.local_sems.at[chunk]
        )

    def copy(self, chunk, slot):
        x, c, z, y = place()
        shard, full, start, middle, end = self.chunks[chunk]
        whole = pl.ds(start, end - start)
        first, second = pl.ds(start, middle - start), pl.ds(middle, end - middle)
        if slot < 3:
            source, target = shard.at[:, whole], full.at[x, c, z, y, :, whole]
            partner = device(x, c, lax.rem(z + slot + 1, 4), y)
        else:
            source, partner = {
                3: (full.at[x, c, :, y, :, first], device(x, c, z, 1 - y)),
                4: (full.at[x, c, :, y, :, second], device(1 - x, c, z, y)),
                5: (full.at[x, c, :, :, :, first], device(1 - x, c, z, y)),
                6: (full.at[:, c, :, y, :, second], device(x, c, z, 1 - y)),
                7: (full.at[:, c, :, :, :, whole], device(x, 1 - c, z, y)),
            }[slot]
            target = source
        return remote(
            source, target, self.sems.at[0, chunk, slot], self.sems.at[1, chunk, slot], partner
        )

    def step(self, number, chunk):
        if number == 0:
            self.keep(chunk).start()
            for slot in (0, 1, 2):
                self.copy(chunk, slot).start()
        elif number == 1:
            self.keep(chunk).wait()
            for slot in (0, 1, 2):
                self.copy(chunk, slot).wait_recv()
            self.copy(chunk, 3).start()
            self.copy(chunk, 4).start()
        elif number == 2:
            self.copy(chunk, 3).wait_recv()
            self.copy(chunk, 5).start()
            self.copy(chunk, 4).wait_recv()
            self.copy(chunk, 6).start()
        elif number == 3:
            self.copy(chunk, 5).wait_recv()
            self.copy(chunk, 6).wait_recv()
            self.copy(chunk, 7).start()
        else:
            self.copy(chunk, 7).wait_recv()
            for slot in range(self.SEMS):
                self.copy(chunk, slot).wait_send()


class Windows:
    KINDS = 5

    def __init__(self, window, sems, block):
        self.window, self.sems, self.block = window, sems, block

    def rows(self, seq, distance):
        start = (4 - distance) * self.block
        return self.window.at[seq, pl.ds(start, self.block)]

    def copy(self, kind, seq):
        x, c, z, y = place()
        down, over = device(x, c, lax.rem(z + 1, 4), y), device(x, c, z, 1 - y)
        source, target, partner = {
            0: (0, 2, down),
            1: (2, 4, down),
            2: (0, 1, over),
            3: (2, 3 - 2 * y, over),
            4: (4, 3, over),
        }[kind]
        return remote(
            self.rows(seq, source),
            self.rows(seq, target),
            self.sems.at[0, kind, seq],
            self.sems.at[1, kind, seq],
            partner,
        )

    def sends(self, kind):
        _, _, z, y = place()
        return {0: z < 3, 1: (z > 0) & (z < 3), 2: y == 0, 3: z > 0, 4: (z > 1) & (y == 1)}[kind]

    def gets(self, kind):
        _, _, z, y = place()
        return {0: z > 0, 1: z > 1, 2: y == 1, 3: z > 0, 4: (z > 1) & (y == 0)}[kind]

    def start(self, kind, seq):
        pl.when(self.sends(kind))(lambda: self.copy(kind, seq).start())

    def wait(self, kind, seq):
        pl.when(self.gets(kind))(lambda: self.copy(kind, seq).wait_recv())

    def own(self, seq):
        self.start(0, seq)
        self.start(2, seq)

    def once(self, seq):
        self.wait(0, seq)
        self.start(1, seq)
        self.start(3, seq)

    def twice(self, seq):
        self.wait(1, seq)
        self.start(4, seq)

    def all(self, seq):
        for kind in (2, 3, 4):
            self.wait(kind, seq)

    def drain(self, seq):
        for kind in range(self.KINDS):
            pl.when(self.sends(kind))(lambda: self.copy(kind, seq).wait_send())


class Scatter:
    SEMS = 8

    def __init__(self, plans, buffers, sems):
        self.plans, self.buffers, self.sems = plans, buffers, sems

    @staticmethod
    def scratch(widths, rows, share=0.5):
        out = []
        for n in widths:
            h = round(n * share / 128) * 128
            low = jnp.bfloat16
            out += [
                pltpu.VMEM((2, 4, 2, rows, n), low),
                pltpu.VMEM((4, 2, rows, h), low),
                pltpu.VMEM((2, 4, rows, n - h), low),
                pltpu.VMEM((4, rows, h), low),
                pltpu.VMEM((4, rows, n - h), low),
                pltpu.VMEM((3, rows, n), low),
            ]
        return out + [pltpu.SemaphoreType.DMA((2, max(1, len(widths)), Scatter.SEMS))]

    BUFFERS = 6

    def copy(self, chunk, slot):
        x, c, z, y = place()
        source = self.plans[chunk][0]
        one, two_a, two_b, three_a, three_b, last = self.buffers[chunk]
        half = two_a.shape[-1]
        first, second = slice(0, half), slice(half, one.shape[-1])
        if slot >= 5:
            hop = slot - 4
            source, target = one.at[0, lax.rem(z + hop, 4), 0], last.at[hop - 1]
            partner = device(x, c, lax.rem(z + hop, 4), y)
        else:
            over_x, over_y = device(1 - x, c, z, y), device(x, c, z, 1 - y)
            source, target, partner = {
                0: lambda: (source.at[:, 1 - c], one, device(x, 1 - c, z, y)),
                1: lambda: (one.at[1 - x, :, :, :, first], two_a, over_x),
                2: lambda: (one.at[:, :, 1 - y, :, second], two_b, over_y),
                3: lambda: (two_a.at[:, 1 - y], three_a, over_y),
                4: lambda: (two_b.at[1 - x], three_b, over_x),
            }[slot]()
        return remote(
            source, target, self.sems.at[0, chunk, slot], self.sems.at[1, chunk, slot], partner
        )

    def load(self, chunk):
        _, c, _, _ = place()
        source, mine, sem, _ = self.plans[chunk]
        return pltpu.make_async_copy(source.at[:, c], mine, sem)

    def step(self, number, chunk):
        x, c, z, y = place()
        source, mine, _, result = self.plans[chunk]
        one, two_a, two_b, three_a, three_b, last = self.buffers[chunk]
        half = two_a.shape[-1]
        first, second = slice(0, half), slice(half, one.shape[-1])
        if number == 0:
            self.copy(chunk, 0).start()
            if mine is not None:
                self.load(chunk).start()
        elif number == 1:
            if mine is not None:
                self.load(chunk).wait()
            else:
                mine = source.at[:, c]
            self.copy(chunk, 0).wait_recv()
            for i in range(2):

                @pl.loop(0, 4)
                def _(j):
                    for k in range(2):
                        add_rows(one.at[i, j, k], mine.at[i, j, k])

            self.copy(chunk, 1).start()
            self.copy(chunk, 2).start()
            self.copy(chunk, 0).wait_send()
        elif number == 2:
            self.copy(chunk, 1).wait_recv()

            @pl.loop(0, 4)
            def _(j):
                for k in range(2):
                    add_rows(two_a.at[j, k], one.at[x, j, k, :, first])

            self.copy(chunk, 3).start()
            self.copy(chunk, 2).wait_recv()

            @pl.loop(0, 4)
            def _(j):
                for i in range(2):
                    add_rows(two_b.at[i, j], one.at[i, j, y, :, second])

            self.copy(chunk, 4).start()
        elif number == 3:
            self.copy(chunk, 1).wait_send()
            self.copy(chunk, 2).wait_send()
            self.copy(chunk, 3).wait_recv()
            self.copy(chunk, 4).wait_recv()

            @pl.loop(0, 4)
            def _(k):
                left = three_a[k].astype(jnp.float32) + two_a[k, y].astype(jnp.float32)
                right = three_b[k].astype(jnp.float32) + two_b[x, k].astype(jnp.float32)
                one[0, k, 0, :, first] = left.astype(one.dtype)
                one[0, k, 0, :, second] = right.astype(one.dtype)

            for slot in (5, 6, 7):
                self.copy(chunk, slot).start()
        else:
            total = one[0, z, 0].astype(jnp.float32)
            for slot in (5, 6, 7):
                self.copy(chunk, slot).wait_recv()
                total += last[slot - 5].astype(jnp.float32)
            result(total)
            for slot in (3, 4, 5, 6, 7):
                self.copy(chunk, slot).wait_send()


def add_rows(target, other):
    target[...] = (target[...].astype(jnp.float32) + other[...].astype(jnp.float32)).astype(
        target.dtype
    )


ROW_TILE = 256
LOG2E = 1.4426950408889634
NEG = -1e30


def row(block, index):
    return pl.BlockSpec(block, index)


def vmem():
    return pl.BlockSpec(memory_space=pltpu.VMEM)


def hbm():
    return pl.BlockSpec(memory_space=pl.ANY)


def params(**more):
    return pltpu.CompilerParams(vmem_limit_bytes=62 * MIB, **more)


def inverse_rms(values):
    return lax.rsqrt(jnp.mean(values * values, axis=-1, keepdims=True) + 1e-06)


def rms_back(values, scale, gain, grad):
    inner = jnp.mean(values * gain * grad, axis=-1, keepdims=True)
    return scale * gain * grad - values * (scale * scale * scale * inner)


def project_block(x_ref, cos_ref, sin_ref, columns, gain, ht_ref, q_ref, kv_ref):
    heads, _, head_dim = q_ref.shape
    width = heads * head_dim
    x = x_ref[...].astype(jnp.float32)
    normed = (x * inverse_rms(x) * gain).astype(jnp.bfloat16)
    ht_ref[...] = normed.T
    cosine, sine = cos_ref[...], sin_ref[...]

    def turn(u):
        return (u * cosine + pltpu.roll(u, head_dim // 2, 1) * sine).astype(jnp.bfloat16)

    for pair in range(heads // 2):
        both = matmul(normed, columns(2 * pair * head_dim, (2 * pair + 2) * head_dim))
        q_ref[2 * pair] = turn(both[:, :head_dim])
        q_ref[2 * pair + 1] = turn(both[:, head_dim:])
    both = matmul(normed, columns(width, width + 2 * head_dim))
    kv_ref[:, :head_dim] = turn(both[:, :head_dim])
    kv_ref[:, head_dim:] = both[:, head_dim:].astype(jnp.bfloat16)


def gain_rows(columns, start):
    return columns(start, start + 128).astype(jnp.float32).T[:8]


def project_kernel(x_ref, cos_ref, sin_ref, w_ref, ht_ref, q_ref, kv_ref, gains_ref):
    width = x_ref.shape[1]

    def columns(start, end):
        return w_ref[:, start:end]

    gains_ref[...] = gain_rows(columns, width + kv_ref.shape[2])
    project_block(
        x_ref, cos_ref, sin_ref, columns, gains_ref[0:1], ht_ref, q_ref.at[0], kv_ref.at[0]
    )


def project(x, cosine, sine, weights, seqs, heads, head_dim):
    rows, width = x.shape
    block = rows // seqs
    return pl.pallas_call(
        project_kernel,
        grid=(seqs,),
        in_specs=[
            row((block, width), lambda b: (b, 0)),
            row((block, head_dim), lambda b: (b, 0)),
            row((block, head_dim), lambda b: (b, 0)),
            row(weights.shape, lambda b: (0, 0)),
        ],
        out_specs=[
            row((width, block), lambda b: (0, b)),
            row((1, heads, block, head_dim), lambda b: (b, 0, 0, 0)),
            row((1, block, 2 * head_dim), lambda b: (b, 0, 0)),
            row((8, width), lambda b: (0, 0)),
        ],
        out_shape=[
            jax.ShapeDtypeStruct((width, rows), jnp.bfloat16),
            jax.ShapeDtypeStruct((seqs, heads, block, head_dim), jnp.bfloat16),
            jax.ShapeDtypeStruct((seqs, block, 2 * head_dim), jnp.bfloat16),
            jax.ShapeDtypeStruct((8, width), jnp.float32),
        ],
        compiler_params=params(),
        name="project",
    )(x, cosine, sine, weights)


HALF = 128
GROUP = 8


def window_bias(low_ref, first, span):
    place = lax.broadcasted_iota(jnp.int32, (span, HALF), 0)
    local = lax.broadcasted_iota(jnp.int32, (span, HALF), 1)
    low = low_ref[:, first : first + HALF] - first
    allowed = (place >= low) & (place <= local + (span - HALF))
    bias = jnp.where(allowed, 0.0, NEG)
    return jnp.concatenate([bias] * GROUP, axis=1)


def attend_half(scale, half, q_ref, kv_ref, low_ref, o_ref, lse_ref):
    heads, block, head_dim = q_ref.shape
    span = kv_ref.shape[0] - (block - HALF)
    factor = scale * LOG2E
    first = half * HALF
    keys = kv_ref[first : first + span, :head_dim]
    values_t = kv_ref[first : first + span, head_dim:].T
    values_t = jnp.concatenate([values_t, jnp.ones((16, span), values_t.dtype)], axis=0)
    bias = window_bias(low_ref, first, span)

    for base in range(0, heads, GROUP):
        query = q_ref[base : base + GROUP, first : first + HALF].reshape(GROUP * HALF, head_dim)
        score = right_times(keys, query) * factor + bias
        peak = jnp.max(score, axis=0, keepdims=True)
        weights = jnp.exp2(score - peak).astype(jnp.bfloat16)
        both = matmul(values_t, weights)
        total = both[head_dim : head_dim + 8]
        result = (both[:head_dim] / total[0:1]).T.astype(jnp.bfloat16)
        o_ref[base : base + GROUP, first : first + HALF] = result.reshape(GROUP, HALF, head_dim)
        lse_ref[half, base // GROUP] = jnp.log2(total) + peak


def attend_kernel(scale, q_ref, kv_ref, low_ref, o_ref, lse_ref):
    for half in range(q_ref.shape[2] // HALF):
        attend_half(
            scale, half, q_ref.at[0], kv_ref.at[0], low_ref.at[0], o_ref.at[0], lse_ref.at[0]
        )


def attend(query, pairs, low, scale):
    seqs, heads, block, head_dim = query.shape
    span = pairs.shape[1]
    return pl.pallas_call(
        functools.partial(attend_kernel, scale),
        grid=(seqs,),
        in_specs=[
            row((1, heads, block, head_dim), lambda b: (b, 0, 0, 0)),
            row((1, span, 2 * head_dim), lambda b: (b, 0, 0)),
            row((1, 1, block), lambda b: (b, 0, 0)),
        ],
        out_specs=[
            row((1, heads, block, head_dim), lambda b: (b, 0, 0, 0)),
            row(
                (1, block // HALF, heads // GROUP, 8, GROUP * HALF), lambda b: (b, 0, 0, 0, 0)
            ),
        ],
        out_shape=[
            jax.ShapeDtypeStruct(query.shape, jnp.bfloat16),
            jax.ShapeDtypeStruct(
                (seqs, block // HALF, heads // GROUP, 8, GROUP * HALF), jnp.float32
            ),
        ],
        compiler_params=params(),
        name="attend",
    )(query, pairs, low[:, None, :])


def attend_back_half(
    scale, half, q_ref, kv_ref, low_ref, lse_ref, o_ref, do_ref, cos_ref, sin_ref, put_dq, dkv_ref
):
    heads, block, head_dim = q_ref.shape
    span = kv_ref.shape[0] - (block - HALF)
    factor = scale * LOG2E
    lanes = GROUP * HALF
    first = half * HALF
    window = slice(first, first + span)
    keys, values = kv_ref[window, :head_dim], kv_ref[window, head_dim:]
    keys_t = keys.T
    bias = window_bias(low_ref, first, span)
    cosine = cos_ref[first : first + HALF][None]
    sine = sin_ref[first : first + HALF][None]

    for base in range(0, heads, GROUP):
        here = (slice(base, base + GROUP), slice(first, first + HALF))
        query = q_ref[here].reshape(lanes, head_dim)
        grad = do_ref[here].reshape(lanes, head_dim)
        mixed = o_ref[here].reshape(lanes, head_dim)
        product = grad.astype(jnp.float32) * mixed.astype(jnp.float32)
        delta = jnp.sum(product.T, axis=0, keepdims=True)
        lse = lse_ref[half, base // GROUP, 0:1]
        score = right_times(keys, query)
        weights = jnp.exp2((score * factor - lse) + bias)
        low_weights = weights.astype(jnp.bfloat16)
        dkv_ref[window, head_dim:] += matmul(low_weights, grad)
        slope = right_times(values, grad)
        slope = (weights * (slope - delta)).astype(jnp.bfloat16)
        dkv_ref[window, :head_dim] += matmul(slope, query) * scale
        dq = (matmul(keys_t, slope).T * scale).reshape(GROUP, HALF, head_dim)
        turned = pltpu.roll(dq.reshape(lanes, head_dim), head_dim // 2, 1)
        dq = dq * cosine - turned.reshape(GROUP, HALF, head_dim) * sine
        put_dq(base, first, dq.astype(jnp.bfloat16))


def attend_back_kernel(
    scale, q_ref, kv_ref, low_ref, lse_ref, o_ref, do_ref, cos_ref, sin_ref, dq_ref, dkv_ref
):
    dkv_ref[...] = jnp.zeros_like(dkv_ref)

    def put_dq(base, first, dq):
        dq_ref[0, base : base + GROUP, first : first + HALF] = dq

    for half in range(q_ref.shape[2] // HALF):
        attend_back_half(
            scale,
            half,
            q_ref.at[0],
            kv_ref.at[0],
            low_ref.at[0],
            lse_ref.at[0],
            o_ref.at[0],
            do_ref.at[0],
            cos_ref,
            sin_ref,
            put_dq,
            dkv_ref.at[0],
        )


def attend_back(query, pairs, low, lse, mixed, grad, cosine, sine, scale):
    seqs, heads, block, head_dim = query.shape
    span = pairs.shape[1]
    per_head = row((1, heads, block, head_dim), lambda b: (b, 0, 0, 0))
    table = row((block, head_dim), lambda b: (b, 0))
    return pl.pallas_call(
        functools.partial(attend_back_kernel, scale),
        grid=(seqs,),
        in_specs=[
            per_head,
            row((1, span, 2 * head_dim), lambda b: (b, 0, 0)),
            row((1, 1, block), lambda b: (b, 0, 0)),
            row((1,) + lse.shape[1:], lambda b: (b, 0, 0, 0, 0)),
            per_head,
            per_head,
            table,
            table,
        ],
        out_specs=[per_head, row((1, span, 2 * head_dim), lambda b: (b, 0, 0))],
        out_shape=[
            jax.ShapeDtypeStruct(query.shape, jnp.bfloat16),
            jax.ShapeDtypeStruct(pairs.shape, jnp.float32),
        ],
        compiler_params=params(),
        name="attend_back",
    )(query, pairs, low[:, None, :], lse, mixed, grad, cosine, sine)


def gelu_parts(gate):
    cube = 0.044715 * gate * gate
    bend = jnp.tanh(0.7978845608028654 * gate * (1.0 + cube))
    half = 0.5 * (1.0 + bend)
    value = gate * half
    slope = half + gate * (half * (1.0 - bend)) * (0.7978845608028654 * (1.0 + 3.0 * cube))
    return value, slope


def put_parts(refs, chunk, step):
    def put(total):
        for i, ref in enumerate(refs):
            ref[:, chunk * step : (chunk + 1) * step] = total[:, i * step : (i + 1) * step]

    return put


def put_columns(ref, start):
    def put(total):
        ref[:, start : start + total.shape[1]] = total

    return put


def feed_kernel(own, scattered, far, x_ref, o_ref, g_ref, gains_ref, full_ref, *refs):
    pieces, refs = refs[:4], refs[4:]
    y_ref, dx_ref, do_ref, dgain_ref, dout_ref, dff_ref = refs[:6]
    far_ref, refs = refs[6], refs[7:]
    shares, refs = refs[:3], refs[3:]
    outw, ff, mixed, normed, normed_t, g_t, y_acc, dh_acc, m_all, dgate_all, dup_all, grads = refs[
        :12
    ]
    in_sem, out_sem = refs[12:14]
    rows, width = g_ref.shape
    seqs, heads, block, head_dim = o_ref.shape
    step = ff.shape[-1] // 3
    tiles = rows // ROW_TILE
    shard_rows = width // 32
    near = FF_CHUNKS - far
    gain = gains_ref[1:2]
    if far:
        stacked = stack_columns(pieces, refs[-2], refs[-1], range(near, FF_CHUNKS), 0)
        for copy in stacked:
            copy.start()
    if own:
        greet(neighbours())
        count = Scatter.BUFFERS
        buffers = [refs[14 + count * k : 14 + count * (k + 1)] for k in range(scattered)]
        plans = [
            (grads.at[k % 2], None, None, put_parts(shares, k, step)) for k in range(scattered)
        ]
        refs = refs[14 + count * scattered :]
        scatter = Scatter(plans, buffers, refs[0])
        if far:
            wide = 3 * step
            ranges = [
                (refs[3], far_ref, k * wide, k * wide + wide // 2, (k + 1) * wide)
                for k in range(far)
            ]
            gather = Gather(refs[1], refs[2], ranges)
            for copy in stacked:
                copy.wait()

    def run(place):
        if own:
            for kind, number, chunk in FEED_ORDER[place]:
                (gather, scatter)[kind].step(number, chunk)

    def load(chunk):
        source, start = full_ref, width + chunk * 3 * step
        if chunk >= near:
            source, start = far_ref, (chunk - near) * 3 * step
        return pltpu.make_async_copy(
            source.at[:, :, :, :, :, pl.ds(start, 3 * step)], ff.at[chunk % 2], in_sem.at[chunk % 2]
        )

    def weights(slot, index):
        return ff[slot, :, :, :, :, :, index * step : (index + 1) * step].reshape(width, step)

    def store(chunk):
        return pltpu.make_async_copy(
            grads.at[chunk % 2], dff_ref.at[chunk - scattered], out_sem.at[chunk % 2]
        )

    run(0)
    out_load = pltpu.make_async_copy(
        full_ref.at[:, :, :, :, :, pl.ds(0, width)], outw, in_sem.at[2]
    )
    out_load.start()
    load(0).start()
    x_load = pltpu.make_async_copy(x_ref, normed, in_sem.at[3])
    x_load.start()
    x_load.wait()
    out_load.wait()

    def here(tile):
        return pl.ds(pl.multiple_of(tile * ROW_TILE, ROW_TILE), ROW_TILE)

    def prologue(tile):
        part = here(tile)
        attended = jnp.concatenate([o_ref[tile, h] for h in range(heads)], axis=1)
        x1 = normed[part].astype(jnp.float32) + right_times(attended, outw[...].reshape(width, width))
        mixed[part] = x1
        y_acc[part] = x1
        low = (x1 * inverse_rms(x1) * gain).astype(jnp.bfloat16)
        normed[part] = low
        normed_t[:, part] = low.T
        g_t[:, part] = g_ref[part].T
        dh_acc[part] = jnp.zeros((ROW_TILE, width), jnp.float32)

    for tile in range(tiles):
        prologue(tile)
        run(1 + tile)
    at = 1 + tiles
    for chunk in range(FF_CHUNKS):
        slot = chunk % 2
        if chunk >= near:
            load(chunk).start()
        load(chunk).wait()
        if chunk + 1 < near:
            load(chunk + 1).start()

        def forth(tile):
            part = pl.ds(tile * FEED_TILE, FEED_TILE)
            low, grad = normed[part], g_ref[part]
            gate = matmul(low, weights(slot, 0))
            up_part = matmul(low, weights(slot, 1))
            dm = matmul(grad, weights(slot, 2))
            value, slope = gelu_parts(gate)
            m = (value * up_part).astype(jnp.bfloat16)
            dgate = (dm * up_part * slope).astype(jnp.bfloat16)
            dup = (dm * value).astype(jnp.bfloat16)
            m_all[part], dgate_all[part], dup_all[part] = m, dgate, dup
            y_acc[part] += right_times(m, weights(slot, 2))
            dh_acc[part] += right_times(dgate, weights(slot, 0)) + right_times(
                dup, weights(slot, 1)
            )

        def grads_of(tile):
            part = pl.ds(tile * (width // 2), width // 2)
            for i, (left, right) in enumerate(
                ((normed_t, dgate_all), (normed_t, dup_all), (g_t, m_all))
            ):
                value = matmul(left[part], right[...]).astype(jnp.bfloat16)
                grads[slot, tile, :, :, :, :, i * step : (i + 1) * step] = value.reshape(
                    2, 4, 2, shard_rows, step
                )

        for tile in range(2):
            forth(tile)
            run(at + tile)
        if chunk - 2 >= scattered:
            store(chunk - 2).wait()
        for tile in range(2):
            grads_of(tile)
            run(at + 2 + tile)
        at += 4
        if chunk >= scattered:
            store(chunk).start()

    dgain_ref[...] = jnp.zeros_like(dgain_ref)

    @pl.loop(0, tiles)
    def _(tile):
        part = here(tile)
        normed[part] = y_acc[part].astype(jnp.bfloat16)
        x1, dh = mixed[part], dh_acc[part]
        scale = inverse_rms(x1)
        dgain_ref[0:1] += jnp.sum(dh * x1 * scale, axis=0, keepdims=True)
        dx = g_ref[part].astype(jnp.float32) + rms_back(x1, scale, gain, dh)
        mixed[part] = dx
        low = dx.astype(jnp.bfloat16)
        g_t[:, part] = low.T
        back = matmul(low, outw[...].reshape(width, width)).astype(jnp.bfloat16)
        for h in range(heads):
            do_ref[tile, h] = back[:, h * head_dim : (h + 1) * head_dim]

    outs = [
        pltpu.make_async_copy(normed, y_ref, in_sem.at[0]),
        pltpu.make_async_copy(mixed, dx_ref, in_sem.at[1]),
    ]
    for out in outs:
        out.start()
    run(at)

    @pl.loop(0, width // ROW_TILE)
    def _(tile):
        part = here(tile)
        for h in range(0, heads, 2):
            for s in range(seqs):
                pair = jnp.concatenate([o_ref[s, h], o_ref[s, h + 1]], axis=1)
                term = matmul(g_t[part, s * block : (s + 1) * block], pair)
                total = term if s == 0 else total + term
            lanes = slice(h * head_dim, (h + 2) * head_dim)
            ff[0, tile // 2, lax.rem(tile, 2), :, :, :, lanes] = total.astype(
                jnp.bfloat16
            ).reshape(4, 2, shard_rows, 2 * head_dim)

    outs.append(
        pltpu.make_async_copy(
            ff.at[0, :, :, :, :, :, pl.ds(0, width)], dout_ref, in_sem.at[2]
        )
    )
    outs[-1].start()
    run(at + 1)
    for chunk in range(max(scattered, FF_CHUNKS - 2), FF_CHUNKS):
        store(chunk).wait()
    for out in outs:
        out.wait()


def feed(own, scattered, far, x, mixed_heads, grad, gains, full, pieces):
    rows, width = x.shape
    step = pieces[1].shape[1] // FF_CHUNKS
    low = jnp.bfloat16
    chunk = (2, 2, 4, 2, width // 32, 3 * step)
    kept = FF_CHUNKS - scattered
    options = {"collective_id": 3, "has_side_effects": True} if own else {}
    return pl.pallas_call(
        functools.partial(feed_kernel, own, scattered, far),
        in_specs=[hbm(), vmem(), vmem(), vmem()] + [hbm()] * 5,
        out_specs=[hbm(), hbm(), vmem(), vmem(), hbm(), hbm(), hbm()] + [vmem()] * 3,
        out_shape=[
            jax.ShapeDtypeStruct((rows, width), low),
            jax.ShapeDtypeStruct((rows, width), jnp.float32),
            jax.ShapeDtypeStruct(mixed_heads.shape, low),
            jax.ShapeDtypeStruct((8, width), jnp.float32),
            jax.ShapeDtypeStruct(chunk[:-1] + (width,), low),
            jax.ShapeDtypeStruct((kept,) + chunk, low),
            jax.ShapeDtypeStruct(chunk[:-1] + (max(1, far) * 3 * step,), low),
        ]
        + [jax.ShapeDtypeStruct((width // 32, max(1, scattered) * step), jnp.float32)] * 3,
        scratch_shapes=[
            pltpu.VMEM(chunk[:-1] + (width,), low),
            pltpu.VMEM((2,) + chunk, low),
            pltpu.VMEM((rows, width), jnp.float32),
            pltpu.VMEM((rows, width), low),
            pltpu.VMEM((width, rows), low),
            pltpu.VMEM((width, rows), low),
            pltpu.VMEM((rows, width), jnp.float32),
            pltpu.VMEM((rows, width), jnp.float32),
            pltpu.VMEM((rows, step), low),
            pltpu.VMEM((rows, step), low),
            pltpu.VMEM((rows, step), low),
            pltpu.VMEM((2,) + chunk, low),
            pltpu.SemaphoreType.DMA((4,)),
            pltpu.SemaphoreType.DMA((2,)),
        ]
        + (Scatter.scratch([3 * step] * scattered, width // 32) if own else [])
        + (Gather.scratch(far) if far else [])
        + (
            [
                pltpu.VMEM((width // 32, far * 3 * step), low),
                pltpu.SemaphoreType.DMA((3 * far,)),
            ]
            if far
            else []
        ),
        compiler_params=params(**options),
        name="feed",
    )(x, mixed_heads, grad, gains, full, *pieces)


def finish_rows(x, dx, grad, w_ref, gain):
    dh = right_times(grad, w_ref[:, : grad.shape[1]])
    x = x.astype(jnp.float32)
    scale = inverse_rms(x)
    total = (dx + rms_back(x, scale, gain, dh)).astype(jnp.bfloat16)
    return total, jnp.sum(dh * x * scale, axis=0, keepdims=True)


def finish_kernel(
    x_ref, ht_ref, dq_ref, dkv_ref, gains_ref, dx_ref, w_ref, dw_ref, dxo_ref, dgain_ref, dall
):
    width = x_ref.shape[1]
    seqs, heads, block, _ = dq_ref.shape
    dgain_ref[...] = jnp.zeros_like(dgain_ref)

    @pl.loop(0, seqs)
    def _(tile):
        part = pl.ds(pl.multiple_of(tile * block, block), block)
        grad = jnp.concatenate([dq_ref[tile, h] for h in range(heads)] + [dkv_ref[tile]], axis=1)
        dall[part] = grad
        dxo_ref[part], terms = finish_rows(
            x_ref[part], dx_ref[part], grad, w_ref, gains_ref[0:1]
        )
        dgain_ref[0:1] += terms

    @pl.loop(0, width // ROW_TILE)
    def _(tile):
        part = pl.ds(pl.multiple_of(tile * ROW_TILE, ROW_TILE), ROW_TILE)
        dw_ref[part] = matmul(ht_ref[part], dall[...]).astype(jnp.bfloat16)


def finish(x, normed_t, dq, dkv, gains, dx, weights):
    rows, width = x.shape
    columns = width + dkv.shape[2]
    return pl.pallas_call(
        finish_kernel,
        in_specs=[vmem()] * 7,
        out_specs=[vmem()] * 3,
        out_shape=[
            jax.ShapeDtypeStruct((width, columns), jnp.bfloat16),
            jax.ShapeDtypeStruct((rows, width), jnp.bfloat16),
            jax.ShapeDtypeStruct((8, width), jnp.float32),
        ],
        scratch_shapes=[pltpu.VMEM((rows, columns), jnp.bfloat16)],
        compiler_params=params(),
        name="finish",
    )(x, normed_t, dq, dkv, gains, dx, weights)


def segment_partners():
    x, c, z, y = place()
    partners = [device(x, c, z, 1 - y)]
    for hop in (1, 2, 3):
        partners += [device(x, c, lax.rem(z + hop, 4), there) for there in (y, 1 - y)]
    return partners


def place_rows(all_ref, frequencies, cos_ref, sin_ref, low_ref):
    _, _, z, y = place()
    _, seqs, block = all_ref.shape
    offset = (z * 2 + y) * block
    place_of = lax.broadcasted_iota(jnp.int32, (block, 1), 0) + offset
    lanes = lax.broadcasted_iota(jnp.int32, (block, cos_ref.shape[1]), 1)
    for seq in range(seqs):
        mine = all_ref[z * 2 + y, seq : seq + 1].astype(jnp.float32)
        mine = jnp.broadcast_to(mine, (128, block)).T[:, 0:1].astype(jnp.int32)
        smaller = jnp.zeros((block, block), jnp.float32)
        for other in range(all_ref.shape[0]):
            smaller += jnp.where(all_ref[other, seq : seq + 1] < mine, 1.0, 0.0)
        starts = jnp.sum(smaller, axis=1, keepdims=True).astype(jnp.int32)
        angle = (place_of - starts).astype(jnp.float32) * frequencies
        rows = slice(seq * block, (seq + 1) * block)
        cos_ref[rows] = jnp.cos(angle)
        sine = jnp.sin(angle)
        sin_ref[rows] = jnp.where(lanes < cos_ref.shape[1] // 2, -sine, sine)
        low = jnp.maximum(starts, place_of - (WINDOW - 1)) - (offset - 4 * block)
        low = jnp.broadcast_to(low.astype(jnp.float32), lanes.shape)
        low_ref[seq] = low.T[0:1].astype(jnp.int32)


def stack_columns(pieces, target, sems, chunks, start):
    out, *parts = pieces
    copies = []
    if start:
        copies.append(pltpu.make_async_copy(out, target.at[:, pl.ds(0, start)], sems.at[0]))
    step = parts[0].shape[1] // FF_CHUNKS
    for chunk in chunks:
        for part in parts:
            source = part.at[:, pl.ds(chunk * step, step)]
            there = target.at[:, pl.ds(start, step)]
            copies.append(pltpu.make_async_copy(source, there, sems.at[len(copies)]))
            start += step
    return copies


def front_kernel(
    scale,
    ranges,
    ranges_ff,
    x_ref,
    frequency_ref,
    segments_ref,
    first_ref,
    *refs,
):
    pieces, refs = refs[:4], refs[4:]
    (
        ht_ref,
        q_ref,
        pairs_ref,
        gains_ref,
        o_ref,
        lse_ref,
        cos_ref,
        sin_ref,
        low_ref,
        full_ref,
        w_ref,
        window,
        w_all,
        all_segments,
        sems,
        local_sems,
        window_sems,
        out_sems,
        segment_sems,
        stack,
        stack_sems,
    ) = refs
    seqs, heads, block, head_dim = q_ref.shape
    width = heads * head_dim
    reach = window.shape[1] - block
    window[:, :reach] = jnp.zeros((seqs, reach, 2 * head_dim), window.dtype)
    stacked = stack_columns(pieces, stack, stack_sems, ranges_ff, width)
    for copy in stacked:
        copy.start()
    partners = segment_partners()
    x, c, z, y = place()
    greet(partners + [device(1 - x, c, z, y), device(x, 1 - c, z, y)])
    mine = all_segments.at[z * 2 + y]
    keep = pltpu.make_async_copy(segments_ref, mine, segment_sems.at[2, 0])
    keep.start()
    copies = [
        remote(segments_ref, mine, segment_sems.at[0, i], segment_sems.at[1, i], partner)
        for i, partner in enumerate(partners)
    ]
    for copy in copies:
        copy.start()
    refs = ((first_ref, w_all), (stack, full_ref))
    gather = Gather(sems, local_sems, [refs[i] + tuple(rest) for i, *rest in ranges])
    windows = Windows(window, window_sems, block)

    def run(place, first=0, last=None):
        for kind, number, index in FRONT_ORDER[place][first:last]:
            if kind == 0:
                gather.step(number, index)
            else:
                (windows.once, windows.twice, windows.all)[number](index)

    def columns(start, end):
        return w_all[:, :, :, :, :, start:end].reshape(width, end - start)

    ahead = [item[1] for item in FRONT_ORDER[0]].index(1)
    for copy in stacked:
        copy.wait()
    run(0, 0, ahead)
    keep.wait()
    for copy in copies:
        copy.wait()
    place_rows(all_segments, frequency_ref[0:1], cos_ref, sin_ref, low_ref)
    run(0, ahead)
    gains_ref[...] = gain_rows(columns, width + 2 * head_dim)

    @pl.loop(0, seqs)
    def _(seq):
        part = pl.ds(pl.multiple_of(seq * block, block), block)
        project_block(
            x_ref.at[part],
            cos_ref.at[part],
            sin_ref.at[part],
            columns,
            gains_ref[0:1],
            ht_ref.at[:, part],
            q_ref.at[seq],
            window.at[seq, pl.ds(reach, block)],
        )
        windows.own(seq)
        for index in range(seqs - 1):
            if FRONT_ORDER[1 + index]:
                pl.when(seq == index)(lambda: run(1 + index))

    run(seqs)
    halves = block // HALF

    @pl.loop(0, seqs)
    def _(seq):
        for half in range(halves):
            attend_half(
                scale,
                half,
                q_ref.at[seq],
                window.at[seq],
                low_ref.at[seq],
                o_ref.at[seq],
                lse_ref.at[seq],
            )
            for index in range(seqs):
                number = seqs + 1 + index * halves + half
                if FRONT_ORDER[number] and number < seqs * (1 + halves):
                    pl.when(seq == index)(lambda: run(number))

    outs = [
        pltpu.make_async_copy(window, pairs_ref, out_sems.at[0]),
        pltpu.make_async_copy(w_all, w_ref, out_sems.at[1]),
    ]
    for out in outs:
        out.start()
    run(seqs * (1 + halves))

    @pl.loop(0, seqs)
    def _(seq):
        windows.drain(seq)

    for out in outs:
        out.wait()


def front(x, segments, first, pieces, scale, ranges, near, heads, head_dim):
    rows, width = x.shape
    seqs, block = segments.shape
    shard_rows, hidden = pieces[1].shape
    columns = width + near * 3 * hidden // FF_CHUNKS
    half = head_dim // 2
    inverse = 10000.0 ** (-2.0 * jnp.arange(half, dtype=jnp.float32) / head_dim)
    frequencies = jnp.broadcast_to(jnp.concatenate([inverse, inverse]), (8, head_dim))
    low_type = jnp.bfloat16
    span = 5 * block
    lse = (seqs, block // HALF, heads // GROUP, 8, GROUP * HALF)
    stacked = (2, 2, 4, 2, shard_rows)
    return pl.pallas_call(
        functools.partial(front_kernel, scale, ranges, range(near)),
        in_specs=[vmem()] * 2 + [hbm()] * 6,
        out_specs=[vmem(), vmem(), hbm()] + [vmem()] * 6 + [hbm(), hbm()],
        out_shape=[
            jax.ShapeDtypeStruct((width, rows), low_type),
            jax.ShapeDtypeStruct((seqs, heads, block, head_dim), low_type),
            jax.ShapeDtypeStruct((seqs, span, 2 * head_dim), low_type),
            jax.ShapeDtypeStruct((8, width), jnp.float32),
            jax.ShapeDtypeStruct((seqs, heads, block, head_dim), low_type),
            jax.ShapeDtypeStruct(lse, jnp.float32),
            jax.ShapeDtypeStruct((rows, head_dim), jnp.float32),
            jax.ShapeDtypeStruct((rows, head_dim), jnp.float32),
            jax.ShapeDtypeStruct((seqs, 1, block), jnp.int32),
            jax.ShapeDtypeStruct(stacked + (columns,), low_type),
            jax.ShapeDtypeStruct(stacked + (first.shape[1],), low_type),
        ],
        scratch_shapes=[
            pltpu.VMEM((seqs, span, 2 * head_dim), low_type),
            pltpu.VMEM(stacked + (first.shape[1],), low_type),
            pltpu.VMEM((8, seqs, block), jnp.int32),
        ]
        + Gather.scratch(len(ranges))
        + [
            pltpu.SemaphoreType.DMA((2, Windows.KINDS, seqs)),
            pltpu.SemaphoreType.DMA((2,)),
            pltpu.SemaphoreType.DMA((3, 7)),
            pltpu.VMEM((shard_rows, columns), low_type),
            pltpu.SemaphoreType.DMA((1 + 3 * near,)),
        ],
        compiler_params=params(collective_id=2, has_side_effects=True),
        name="front",
    )(x, frequencies, segments, first, *pieces)


class WindowGrads:
    def __init__(self, windows, grads, out, came, sems, block):
        self.windows, self.grads, self.out, self.came = windows, grads, out, came
        self.sems, self.block = sems, block

    def rows(self, seq, distance):
        start = (4 - distance) * self.block
        if not isinstance(distance, int):
            start = pl.multiple_of(start, self.block)
        return self.grads.at[seq, pl.ds(start, self.block)]

    def copy(self, kind, seq):
        x, c, z, y = place()
        over = device(x, c, z, 1 - y)
        partner = device(x, c, lax.rem(z + 3, 4), y) if kind < 2 else over
        return remote(
            self.out.at[kind, seq],
            self.came.at[kind, seq],
            self.sems.at[0, kind, seq],
            self.sems.at[1, kind, seq],
            partner,
        )

    def start(self, kind, seq, distance):
        @pl.when(self.windows.gets(kind))
        def _():
            self.out[kind, seq] = self.rows(seq, distance)[...].astype(jnp.bfloat16)
            self.copy(kind, seq).start()

    def add(self, kind, seq, distance):
        @pl.when(self.windows.sends(kind))
        def _():
            self.copy(kind, seq).wait_recv()
            target = self.rows(seq, distance)
            target[...] += self.came[kind, seq].astype(jnp.float32)

    def step(self, number, seq):
        _, _, _, y = place()
        if number == 0:
            self.start(4, seq, 3)
            self.start(3, seq, 1 + 2 * y)
            self.start(2, seq, 1)
        elif number == 1:
            self.add(4, seq, 4)
            self.start(1, seq, 4)
            self.add(3, seq, 2)
        elif number == 2:
            self.add(1, seq, 2)
            self.start(0, seq, 2)
        else:
            self.add(0, seq, 0)
            self.add(2, seq, 0)

    def drain(self, seq):
        for kind in range(Windows.KINDS):
            pl.when(self.windows.gets(kind))(lambda: self.copy(kind, seq).wait_send())


def back_kernel(scale, kept, last_chunks, *refs):
    (
        q_ref,
        pairs_ref,
        low_ref,
        lse_ref,
        o_ref,
        do_ref,
        cos_ref,
        sin_ref,
        x_ref,
        ht_ref,
        gains_ref,
        dgain_ref,
        w_ref,
        dx_ref,
        dout_ref,
        dff_ref,
    ) = refs[:16]
    dxo_ref, refs = refs[16], refs[17:]
    total = kept + 1 + len(last_chunks)
    shares, refs = refs[:8], refs[8:]
    grads, out, came, dall, dx, dgains, dw, load_sems, dx_sems, grad_sems = refs[:10]
    mines, refs = refs[10 : 11 + kept], refs[11 + kept :]
    count = Scatter.BUFFERS
    buffers = [refs[count * k : count * (k + 1)] for k in range(total)]
    sems = refs[count * total]
    seqs, heads, block, head_dim = q_ref.shape
    width = heads * head_dim

    grads[...] = jnp.zeros_like(grads)
    dgains[...] = jnp.zeros_like(dgains)
    dgains[1:2] = dgain_ref[0:1]
    greet(neighbours())
    sources = [dff_ref.at[k] for k in range(kept)] + [dout_ref]
    step = dff_ref.shape[-1] // 3
    plans = [
        (source, mines[i], load_sems.at[i], put_parts(shares[:3], i, step))
        for i, source in enumerate(sources[:kept])
    ]
    plans.append((dout_ref, mines[kept], load_sems.at[kept], put_columns(shares[3], 0)))

    def put_last(result):
        shares[5][...] = result[:, :head_dim]
        shares[6][...] = result[:, head_dim : 2 * head_dim]
        shares[7][...] = result[:, 2 * head_dim :]

    for start, end in last_chunks:
        source = dw.at[:, :, :, :, :, pl.ds(start, end - start)]
        put = put_columns(shares[4], start) if end <= width else put_last
        plans.append((source, None, None, put))
    scatter = Scatter(plans, buffers, sems)
    windows = Windows(None, None, block)
    back = WindowGrads(windows, grads, out, came, grad_sems, block)
    halves = block // HALF

    def load(seq):
        return pltpu.make_async_copy(
            dx_ref.at[pl.ds(seq * block, block)], dx.at[seq % 2], dx_sems.at[seq % 2]
        )

    load(0).start()
    load(1).start()

    def finish_one(seq):
        part = pl.ds(seq * block, block)
        own = grads[seq, 4 * block :]
        key, value = own[:, :head_dim], own[:, head_dim:]
        turned = pltpu.roll(key, head_dim // 2, 1)
        key = key * cos_ref[part] - turned * sin_ref[part]
        dall[part, width : width + head_dim] = key.astype(jnp.bfloat16)
        dall[part, width + head_dim :] = value.astype(jnp.bfloat16)
        load(seq).wait()
        dxo_ref[part], terms = finish_rows(
            x_ref[part], dx[seq % 2], dall[part], w_ref, gains_ref[0:1]
        )
        dgains[0:1] += terms
        if seq + 2 < seqs:
            load(seq + 2).start()

    def weight_grads(start, end):
        @pl.loop(0, 2)
        def _(tile):
            part = pl.ds(pl.multiple_of(tile * (width // 2), width // 2), width // 2)
            value = matmul(ht_ref[part], dall[:, start:end]).astype(jnp.bfloat16)
            dw[tile, :, :, :, :, start:end] = value.reshape(
                (2,) + dw.shape[2:5] + (end - start,)
            )

    def weight_tail():
        weight_grads(width, width + 2 * head_dim)
        gains = dgains[...].T.astype(jnp.bfloat16)
        dw[:, :, :, :, :, width + 2 * head_dim :] = gains.reshape(
            dw.shape[:5] + (gains.shape[1],)
        )

    def run(place):
        for kind, number, index in BACK_ORDER[place]:
            if kind == 0:
                scatter.step(number, index)
            elif kind == 1:
                back.step(number, index)
            elif kind == 2:
                weight_grads(0, width)
            elif kind == 3:
                finish_one(number)
            else:
                weight_tail()

    run(0)

    @pl.loop(0, seqs)
    def _(seq):
        part = pl.ds(pl.multiple_of(seq * block, block), block)

        def put_dq(base, first, dq):
            there = pl.ds(pl.multiple_of(seq * block + first, HALF), HALF)
            for h in range(GROUP):
                dall[there, (base + h) * head_dim : (base + h + 1) * head_dim] = dq[h]

        for half in range(halves):
            attend_back_half(
                scale,
                half,
                q_ref.at[seq],
                pairs_ref.at[seq],
                low_ref.at[seq],
                lse_ref.at[seq],
                o_ref.at[seq],
                do_ref.at[seq],
                cos_ref.at[part],
                sin_ref.at[part],
                put_dq,
                grads.at[seq],
            )
            for index in range(seqs):
                number = 1 + index * halves + half
                if BACK_ORDER[number] and number < seqs * halves:
                    pl.when(seq == index)(lambda: run(number))

    run(seqs * halves)

    @pl.loop(0, seqs)
    def _(seq):
        back.drain(seq)


def back(
    query, pairs, low, lse, mixed, grad, cosine, sine, x, normed_t, gains, dgain, weights, dx, dout, dff, scale
):
    seqs, heads, block, head_dim = query.shape
    rows, width = x.shape
    columns = weights.shape[1]
    kept = dff.shape[0]
    shard_rows = dff.shape[-2]
    low_type = jnp.bfloat16
    span = pairs.shape[1]
    last_chunks = ((0, width // 2), (width // 2, width), (width, columns))
    widths = [dff.shape[-1]] * kept + [width] + [end - start for start, end in last_chunks]
    lanes = 2 * head_dim
    results = [kept * dff.shape[-1] // 3] * 3 + [width, width, head_dim, head_dim]
    results.append(columns - width - lanes)
    return pl.pallas_call(
        functools.partial(back_kernel, scale, kept, last_chunks),
        in_specs=[vmem()] * 13 + [hbm()] * 3,
        out_specs=[vmem()] * 9,
        out_shape=[jax.ShapeDtypeStruct((rows, width), low_type)]
        + [jax.ShapeDtypeStruct((shard_rows, n), jnp.float32) for n in results],
        scratch_shapes=[
            pltpu.VMEM((seqs, span, lanes), jnp.float32),
            pltpu.VMEM((Windows.KINDS, seqs, block, lanes), low_type),
            pltpu.VMEM((Windows.KINDS, seqs, block, lanes), low_type),
            pltpu.VMEM((rows, width + lanes), low_type),
            pltpu.VMEM((2, block, width), jnp.float32),
            pltpu.VMEM((128, width), jnp.float32),
            pltpu.VMEM((2, 2, 4, 2, shard_rows, columns), low_type),
            pltpu.SemaphoreType.DMA((kept + 1,)),
            pltpu.SemaphoreType.DMA((2,)),
            pltpu.SemaphoreType.DMA((2, Windows.KINDS, seqs)),
        ]
        + [pltpu.VMEM((2, 4, 2, shard_rows, n), low_type) for n in widths[: kept + 1]]
        + Scatter.scratch(widths, shard_rows, 2 / 3),
        compiler_params=params(collective_id=4, has_side_effects=True),
        name="back",
    )(
        query,
        pairs,
        low,
        lse,
        mixed,
        grad,
        cosine,
        sine,
        x,
        normed_t,
        gains,
        dgain,
        weights,
        dx,
        dout,
        dff,
    )


def stack_ff(gate, up_part, down_t, chunks):
    step = gate.shape[1] // FF_CHUNKS
    return [
        part[:, chunk * step : (chunk + 1) * step]
        for chunk in chunks
        for part in (gate, up_part, down_t)
    ]


def unstack_ff(stacked):
    rows, hidden = stacked.shape[0], stacked.shape[1] // 3
    parts = stacked.reshape(rows, FF_CHUNKS, 3, hidden // FF_CHUNKS)
    return [parts[:, :, i].reshape(rows, hidden) for i in range(3)]


def shifted(value, axis, steps):
    count = lax.axis_size(axis)
    initial, last = (max(0, -steps), min(count, count - steps))
    return lax.ppermute(value, axis, [(source, source + steps) for source in range(initial, last)])


def on_device(
    own_links,
    tokens,
    segments,
    cotangent,
    first_gain,
    query_weight,
    key_weight,
    value_weight,
    out_weight,
    second_gain,
    gate_weight,
    up_weight,
    down_weight,
):
    seqs, block_len, width = tokens.shape
    head_dim = key_weight.shape[1]
    heads = query_weight.shape[1] // head_dim
    hidden = gate_weight.shape[1]
    shard_rows = first_gain.shape[0]
    reach = (WINDOW - 1 + block_len - 1) // block_len
    scale = head_dim ** (-0.5)
    rows = seqs * block_len
    keys_from = width + 2 * head_dim
    inputs = tokens.reshape(rows, width)
    grad_rows = cotangent.reshape(rows, width)

    gains = jnp.zeros((shard_rows, 128), first_gain.dtype)
    gains = gains.at[:, 0].set(first_gain).at[:, 1].set(second_gain)
    shard = jnp.concatenate([query_weight, key_weight, value_weight, gains], axis=1)
    out_t, down_t = out_weight.T, down_weight.T

    pieces = (out_t, gate_weight, up_weight, down_t)

    if own_links:
        near_count = FF_CHUNKS - FAR
        half = 3 * hidden // FF_CHUNKS // 2
        ranges = [(0, 0, 256, 512), (0, 512, 768, width), (0, width, width + 256, keys_from + 128)]
        ranges += [(1, start, start + 384, start + 512) for start in range(0, width, 512)]
        for start in range(width, width + near_count * 2 * half, half):
            ranges.append((1, start, start + 2 * half // 3, start + half))
        normed_t, query, pairs, gains, mixed, lse, cosine, sine, low, full, weights = front(
            inputs, segments, shard, pieces, scale, ranges, near_count, heads, head_dim
        )
        weights = weights.reshape(width, -1)
        scattered, far = SCATTERED, FAR
    else:
        weights = lax.all_gather(shard, ("batch", "seq"), axis=0, tiled=True)
        parts = stack_ff(gate_weight, up_weight, down_t, range(FF_CHUNKS))
        rest = jnp.concatenate([out_t] + parts, axis=1)
        full = lax.all_gather(rest, ("batch", "seq"), axis=0, tiled=True)
        earlier = lax.all_gather(segments, "seq", axis=1, tiled=True)
        starts = jnp.sum(earlier[:, None, :] < segments[:, :, None], axis=-1, dtype=jnp.int32)
        query_place = jnp.arange(block_len, dtype=jnp.int32) + lax.axis_index("seq") * block_len
        low = jnp.maximum(starts, query_place[None, :] - (WINDOW - 1))
        low = low - (query_place[0] - reach * block_len)
        cosine, sine = tables((query_place[None, :] - starts).reshape(-1), head_dim)
        normed_t, query, own_pairs, gains = project(
            inputs, cosine, sine, weights, seqs, heads, head_dim
        )
        passed = [shifted(own_pairs, "seq", distance) for distance in range(reach, 0, -1)]
        pairs = jnp.concatenate(passed + [own_pairs], axis=1)
        mixed, lse = attend(query, pairs, low, scale)
        scattered, far = 0, 0
        full = full.reshape(2, 2, 4, 2, width // 32, -1)
    output, grad_mixed, grad_heads, dgain_two, grad_out_t, grad_ff, _, *shares = feed(
        own_links, scattered, far, inputs, mixed, grad_rows, gains, full, pieces
    )
    if own_links:
        grad_input, *more, share_out, share_query, share_key, share_value, share_gains = back(
            query,
            pairs,
            low,
            lse,
            mixed,
            grad_heads,
            cosine,
            sine,
            inputs,
            normed_t,
            gains,
            dgain_two,
            weights,
            grad_mixed,
            grad_out_t,
            grad_ff,
            scale,
        )
        share_gate, share_up, share_down_t = [
            jnp.concatenate(pair, axis=1) for pair in zip(shares, more)
        ]
    else:
        grad_query, grad_pairs = attend_back(
            query, pairs, low, lse, mixed, grad_heads, cosine, sine, scale
        )
        own_grad = grad_pairs[:, reach * block_len :]
        for distance in range(1, reach + 1):
            start = (reach - distance) * block_len
            piece = grad_pairs[:, start : start + block_len].astype(jnp.bfloat16)
            own_grad = own_grad + shifted(piece, "seq", -distance).astype(own_grad.dtype)
        grad_key = own_grad[..., :head_dim].reshape(rows, head_dim)
        grad_key = grad_key * cosine - jnp.roll(grad_key, head_dim // 2, axis=1) * sine
        grad_kv = jnp.concatenate(
            [grad_key.reshape(seqs, block_len, head_dim), own_grad[..., head_dim:]], axis=-1
        ).astype(jnp.bfloat16)
        grad_qkv_w, grad_input, dgain_one = finish(
            inputs, normed_t, grad_query, grad_kv, gains, grad_mixed, weights
        )
        grad_gains = jnp.zeros((width, 128), jnp.bfloat16)
        grad_gains = grad_gains.at[:, 0].set(dgain_one[0].astype(jnp.bfloat16))
        grad_gains = grad_gains.at[:, 1].set(dgain_two[0].astype(jnp.bfloat16))
        grad_ff = grad_ff.reshape(FF_CHUNKS, width, -1)
        grad_out_t = grad_out_t.reshape(width, -1)
        grads = jnp.concatenate([grad_qkv_w, grad_gains, grad_out_t] + list(grad_ff), axis=1)
        share = lax.psum_scatter(grads, ("batch", "seq"), scatter_dimension=0, tiled=True)
        share = share.astype(jnp.float32)
        share_query, share_key = share[:, :width], share[:, width : width + head_dim]
        share_value = share[:, width + head_dim : keys_from]
        share_gains = share[:, keys_from : keys_from + 128]
        share_out = share[:, keys_from + 128 : keys_from + 128 + width]
        share_gate, share_up, share_down_t = unstack_ff(share[:, keys_from + 128 + width :])
    return (
        output.reshape(tokens.shape),
        grad_input.reshape(tokens.shape),
        share_gains[:, 0],
        share_query,
        share_key,
        share_value,
        share_out.T,
        share_gains[:, 1],
        share_gate,
        share_up,
        share_down_t.T,
    )


def solution(mesh):
    both = ("batch", "seq")
    rows_split, columns_split = P(both, None), P(None, both)
    tokens_split, gain_split = P("batch", "seq", None), P(both)
    weights = (
        gain_split,
        rows_split,
        rows_split,
        rows_split,
        columns_split,
        gain_split,
        rows_split,
        rows_split,
        columns_split,
    )
    in_specs = (tokens_split, P("batch", "seq"), tokens_split) + weights
    out_specs = (tokens_split, tokens_split) + weights
    own_links = (mesh.shape["batch"], mesh.shape["seq"]) == (4, 8)
    return jax.shard_map(
        functools.partial(on_device, own_links),
        mesh=mesh,
        in_specs=in_specs,
        out_specs=out_specs,
        check_vma=False,
    )
```

```python
import functools

import jax
import jax.numpy as jnp
from jax import lax
from jax.experimental import pallas as pl
from jax.experimental.pallas import tpu as pltpu
from jax.sharding import PartitionSpec as P

WINDOW = 1024
FF_CHUNKS = 6
SCATTERED = 4
FAR = 2
FEED_TILE = 512
MESH_ID = pl.DeviceIdType.MESH
MIB = 1 << 20


def tables(positions, head_dim):
    inverse = 10000.0 ** (-2.0 * jnp.arange(head_dim // 2, dtype=jnp.float32) / head_dim)
    angle = positions.astype(jnp.float32)[:, None] * inverse[None, :]
    cosine, sine = jnp.cos(angle), jnp.sin(angle)
    return (
        jnp.concatenate([cosine, cosine], axis=-1),
        jnp.concatenate([-sine, sine], axis=-1),
    )


def matmul(left, right):
    return jnp.dot(left, right, preferred_element_type=jnp.float32)


def right_times(left, right):
    return lax.dot_general(
        left, right, (((1,), (1,)), ((), ())), preferred_element_type=jnp.float32
    )


def place():
    batch, seq = lax.axis_index("batch"), lax.axis_index("seq")
    return batch // 2, lax.rem(batch, 2), seq // 2, lax.rem(seq, 2)


def device(x, c, z, y):
    return (x * 2 + c, z * 2 + y)


def greet(partners):
    barrier = pltpu.get_barrier_semaphore()
    for partner in partners:
        pl.semaphore_signal(barrier, inc=1, device_id=partner, device_id_type=MESH_ID)
    pl.semaphore_wait(barrier, len(partners))


def neighbours():
    x, c, z, y = place()
    return [
        device(x, c, lax.rem(z + 1, 4), y),
        device(x, c, lax.rem(z + 2, 4), y),
        device(x, c, lax.rem(z + 3, 4), y),
        device(1 - x, c, z, y),
        device(x, c, z, 1 - y),
        device(x, 1 - c, z, y),
    ]


def remote(source, target, send_sem, recv_sem, partner):
    return pltpu.make_async_remote_copy(
        src_ref=source,
        dst_ref=target,
        send_sem=send_sem,
        recv_sem=recv_sem,
        device_id=partner,
        device_id_type=MESH_ID,
    )


FRONT_ORDER = (
    ((0, 0, 0), (0, 0, 1), (0, 0, 2), (0, 0, 3), (0, 1, 0), (0, 1, 1), (0, 2, 0), (0, 0, 4), (0, 1, 2), (0, 2, 1), (0, 0, 5), (0, 1, 3), (0, 3, 0), (0, 2, 2), (0, 0, 6), (0, 1, 4), (0, 4, 0), (0, 3, 1), (0, 2, 3), (0, 0, 7), (0, 1, 5), (0, 4, 1), (0, 3, 2), (0, 2, 4), (0, 0, 8), (0, 4, 2), (0, 1, 6),),
    ((0, 3, 3),),
    ((0, 2, 5), (0, 1, 7), (0, 4, 3), (0, 0, 9),),
    ((0, 3, 4), (0, 2, 6), (0, 1, 8), (0, 0, 10),),
    ((1, 0, 0), (0, 4, 4), (1, 0, 1), (0, 3, 5), (0, 2, 7), (0, 0, 11), (0, 4, 5), (0, 1, 9), (1, 0, 2), (0, 3, 6), (0, 2, 8), (0, 0, 12), (0, 4, 6), (0, 1, 10), (1, 1, 0), (1, 0, 3), (1, 1, 1), (0, 3, 7), (0, 2, 9), (0, 4, 7), (0, 1, 11), (1, 1, 2), (0, 3, 8), (0, 1, 12), (0, 2, 10), (0, 4, 8), (1, 2, 0),),
    ((1, 1, 3),),
    ((1, 2, 1),),
    (),
    ((0, 3, 9), (0, 2, 11), (1, 2, 2),),
    ((0, 4, 9),),
    ((0, 2, 12), (0, 3, 10), (1, 2, 3),),
    ((0, 4, 10),),
    ((0, 3, 11), (0, 3, 12), (0, 4, 11), (0, 4, 12),),
)

FEED_ORDER = (
    ((0, 0, 0), (0, 0, 1),),
    (),
    (),
    (),
    ((0, 1, 0),),
    (),
    ((0, 2, 0), (0, 1, 1),),
    (),
    ((1, 0, 0),),
    (),
    ((0, 3, 0), (1, 1, 0),),
    ((0, 2, 1),),
    ((1, 0, 1), (0, 4, 0),),
    (),
    ((1, 2, 0), (1, 1, 1),),
    (),
    ((0, 3, 1), (1, 0, 2),),
    ((1, 3, 0),),
    ((0, 4, 1),),
    ((1, 1, 2),),
    ((1, 2, 1), (1, 4, 0), (1, 0, 3),),
    (),
    ((1, 2, 2), (1, 1, 3),),
    ((1, 3, 1),),
    (),
    ((1, 3, 2),),
    ((1, 4, 1), (1, 2, 3),),
    (),
    (),
    ((1, 4, 2), (1, 3, 3),),
    ((1, 4, 3),),
)

BACK_ORDER = (
    ((0, 0, 0), (0, 0, 1), (0, 0, 2),),
    (),
    ((0, 1, 0), (1, 0, 0),),
    ((0, 1, 1),),
    ((0, 1, 2), (1, 0, 1),),
    ((1, 1, 0),),
    ((0, 2, 0), (1, 0, 2),),
    ((1, 2, 0),),
    ((1, 0, 3), (2, 0, 0), (0, 2, 1), (1, 3, 0), (1, 1, 1), (0, 0, 3), (0, 0, 4), (3, 0, 0), (0, 1, 3), (1, 2, 1), (0, 1, 4), (0, 2, 2), (0, 3, 0), (1, 3, 1), (3, 1, 0), (1, 1, 2), (1, 1, 3), (0, 4, 0), (1, 2, 2), (1, 2, 3), (0, 3, 1), (0, 2, 3), (1, 3, 2), (3, 2, 0), (0, 2, 4), (1, 3, 3), (3, 3, 0), (0, 3, 2), (4, 0, 0), (0, 0, 5), (0, 3, 3), (0, 3, 4), (0, 1, 5), (0, 4, 1), (0, 2, 5), (0, 4, 2), (0, 3, 5), (0, 4, 3), (0, 4, 4), (0, 4, 5),),
)


class Gather:
    STEPS = 5
    SEMS = 8

    def __init__(self, sems, local_sems, chunks):
        self.sems, self.local_sems, self.chunks = sems, local_sems, chunks

    @staticmethod
    def scratch(count):
        return [
            pltpu.SemaphoreType.DMA((2, count, Gather.SEMS)),
            pltpu.SemaphoreType.DMA((count,)),
        ]

    def keep(self, chunk):
        x, c, z, y = place()
        shard, full, start, _, end = self.chunks[chunk]
        whole = pl.ds(start, end - start)
        return pltpu.make_async_copy(
            shard.at[:, whole], full.at[x, c, z, y, :, whole], self.local_sems.at[chunk]
        )

    def copy(self, chunk, slot):
        x, c, z, y = place()
        shard, full, start, middle, end = self.chunks[chunk]
        whole = pl.ds(start, end - start)
        first, second = pl.ds(start, middle - start), pl.ds(middle, end - middle)
        if slot < 3:
            source, target = shard.at[:, whole], full.at[x, c, z, y, :, whole]
            partner = device(x, c, lax.rem(z + slot + 1, 4), y)
        else:
            source, partner = {
                3: (full.at[x, c, :, y, :, first], device(x, c, z, 1 - y)),
                4: (full.at[x, c, :, y, :, second], device(1 - x, c, z, y)),
                5: (full.at[x, c, :, :, :, first], device(1 - x, c, z, y)),
                6: (full.at[:, c, :, y, :, second], device(x, c, z, 1 - y)),
                7: (full.at[:, c, :, :, :, whole], device(x, 1 - c, z, y)),
            }[slot]
            target = source
        return remote(
            source, target, self.sems.at[0, chunk, slot], self.sems.at[1, chunk, slot], partner
        )

    def step(self, number, chunk):
        if number == 0:
            self.keep(chunk).start()
            for slot in (0, 1, 2):
                self.copy(chunk, slot).start()
        elif number == 1:
            self.keep(chunk).wait()
            for slot in (0, 1, 2):
                self.copy(chunk, slot).wait_recv()
            self.copy(chunk, 3).start()
            self.copy(chunk, 4).start()
        elif number == 2:
            self.copy(chunk, 3).wait_recv()
            self.copy(chunk, 5).start()
            self.copy(chunk, 4).wait_recv()
            self.copy(chunk, 6).start()
        elif number == 3:
            self.copy(chunk, 5).wait_recv()
            self.copy(chunk, 6).wait_recv()
            self.copy(chunk, 7).start()
        else:
            self.copy(chunk, 7).wait_recv()
            for slot in range(self.SEMS):
                self.copy(chunk, slot).wait_send()


class Windows:
    KINDS = 5

    def __init__(self, window, sems, block):
        self.window, self.sems, self.block = window, sems, block

    def rows(self, seq, distance):
        start = (4 - distance) * self.block
        return self.window.at[seq, pl.ds(start, self.block)]

    def copy(self, kind, seq):
        x, c, z, y = place()
        down, over = device(x, c, lax.rem(z + 1, 4), y), device(x, c, z, 1 - y)
        source, target, partner = {
            0: (0, 2, down),
            1: (2, 4, down),
            2: (0, 1, over),
            3: (2, 3 - 2 * y, over),
            4: (4, 3, over),
        }[kind]
        return remote(
            self.rows(seq, source),
            self.rows(seq, target),
            self.sems.at[0, kind, seq],
            self.sems.at[1, kind, seq],
            partner,
        )

    def sends(self, kind):
        _, _, z, y = place()
        return {0: z < 3, 1: (z > 0) & (z < 3), 2: y == 0, 3: z > 0, 4: (z > 1) & (y == 1)}[kind]

    def gets(self, kind):
        _, _, z, y = place()
        return {0: z > 0, 1: z > 1, 2: y == 1, 3: z > 0, 4: (z > 1) & (y == 0)}[kind]

    def start(self, kind, seq):
        pl.when(self.sends(kind))(lambda: self.copy(kind, seq).start())

    def wait(self, kind, seq):
        pl.when(self.gets(kind))(lambda: self.copy(kind, seq).wait_recv())

    def own(self, seq):
        self.start(0, seq)
        self.start(2, seq)

    def once(self, seq):
        self.wait(0, seq)
        self.start(1, seq)
        self.start(3, seq)

    def twice(self, seq):
        self.wait(1, seq)
        self.start(4, seq)

    def all(self, seq):
        for kind in (2, 3, 4):
            self.wait(kind, seq)

    def drain(self, seq):
        for kind in range(self.KINDS):
            pl.when(self.sends(kind))(lambda: self.copy(kind, seq).wait_send())


class Scatter:
    SEMS = 8

    def __init__(self, plans, buffers, sems):
        self.plans, self.buffers, self.sems = plans, buffers, sems

    @staticmethod
    def scratch(widths, rows, share=0.5):
        out = []
        for n in widths:
            h = round(n * share / 128) * 128
            low = jnp.bfloat16
            out += [
                pltpu.VMEM((2, 4, 2, rows, n), low),
                pltpu.VMEM((4, 2, rows, h), low),
                pltpu.VMEM((2, 4, rows, n - h), low),
                pltpu.VMEM((4, rows, h), low),
                pltpu.VMEM((4, rows, n - h), low),
                pltpu.VMEM((3, rows, n), low),
            ]
        return out + [pltpu.SemaphoreType.DMA((2, max(1, len(widths)), Scatter.SEMS))]

    BUFFERS = 6

    def copy(self, chunk, slot):
        x, c, z, y = place()
        source = self.plans[chunk][0]
        one, two_a, two_b, three_a, three_b, last = self.buffers[chunk]
        half = two_a.shape[-1]
        first, second = slice(0, half), slice(half, one.shape[-1])
        if slot >= 5:
            hop = slot - 4
            source, target = one.at[0, lax.rem(z + hop, 4), 0], last.at[hop - 1]
            partner = device(x, c, lax.rem(z + hop, 4), y)
        else:
            over_x, over_y = device(1 - x, c, z, y), device(x, c, z, 1 - y)
            source, target, partner = {
                0: lambda: (source.at[:, 1 - c], one, device(x, 1 - c, z, y)),
                1: lambda: (one.at[1 - x, :, :, :, first], two_a, over_x),
                2: lambda: (one.at[:, :, 1 - y, :, second], two_b, over_y),
                3: lambda: (two_a.at[:, 1 - y], three_a, over_y),
                4: lambda: (two_b.at[1 - x], three_b, over_x),
            }[slot]()
        return remote(
            source, target, self.sems.at[0, chunk, slot], self.sems.at[1, chunk, slot], partner
        )

    def load(self, chunk):
        _, c, _, _ = place()
        source, mine, sem, _ = self.plans[chunk]
        return pltpu.make_async_copy(source.at[:, c], mine, sem)

    def step(self, number, chunk):
        x, c, z, y = place()
        source, mine, _, result = self.plans[chunk]
        one, two_a, two_b, three_a, three_b, last = self.buffers[chunk]
        half = two_a.shape[-1]
        first, second = slice(0, half), slice(half, one.shape[-1])
        if number == 0:
            self.copy(chunk, 0).start()
            if mine is not None:
                self.load(chunk).start()
        elif number == 1:
            if mine is not None:
                self.load(chunk).wait()
            else:
                mine = source.at[:, c]
            self.copy(chunk, 0).wait_recv()
            for i in range(2):

                @pl.loop(0, 4)
                def _(j):
                    for k in range(2):
                        add_rows(one.at[i, j, k], mine.at[i, j, k])

            self.copy(chunk, 1).start()
            self.copy(chunk, 2).start()
            self.copy(chunk, 0).wait_send()
        elif number == 2:
            self.copy(chunk, 1).wait_recv()

            @pl.loop(0, 4)
            def _(j):
                for k in range(2):
                    add_rows(two_a.at[j, k], one.at[x, j, k, :, first])

            self.copy(chunk, 3).start()
            self.copy(chunk, 2).wait_recv()

            @pl.loop(0, 4)
            def _(j):
                for i in range(2):
                    add_rows(two_b.at[i, j], one.at[i, j, y, :, second])

            self.copy(chunk, 4).start()
        elif number == 3:
            self.copy(chunk, 1).wait_send()
            self.copy(chunk, 2).wait_send()
            self.copy(chunk, 3).wait_recv()
            self.copy(chunk, 4).wait_recv()

            @pl.loop(0, 4)
            def _(k):
                left = three_a[k].astype(jnp.float32) + two_a[k, y].astype(jnp.float32)
                right = three_b[k].astype(jnp.float32) + two_b[x, k].astype(jnp.float32)
                one[0, k, 0, :, first] = left.astype(one.dtype)
                one[0, k, 0, :, second] = right.astype(one.dtype)

            for slot in (5, 6, 7):
                self.copy(chunk, slot).start()
        else:
            total = one[0, z, 0].astype(jnp.float32)
            for slot in (5, 6, 7):
                self.copy(chunk, slot).wait_recv()
                total += last[slot - 5].astype(jnp.float32)
            result(total)
            for slot in (3, 4, 5, 6, 7):
                self.copy(chunk, slot).wait_send()


def add_rows(target, other):
    target[...] = (target[...].astype(jnp.float32) + other[...].astype(jnp.float32)).astype(
        target.dtype
    )


ROW_TILE = 256
LOG2E = 1.4426950408889634
NEG = -1e30


def row(block, index):
    return pl.BlockSpec(block, index)


def vmem():
    return pl.BlockSpec(memory_space=pltpu.VMEM)


def hbm():
    return pl.BlockSpec(memory_space=pl.ANY)


def params(**more):
    return pltpu.CompilerParams(vmem_limit_bytes=62 * MIB, **more)


def inverse_rms(values):
    return lax.rsqrt(jnp.mean(values * values, axis=-1, keepdims=True) + 1e-06)


def rms_back(values, scale, gain, grad):
    inner = jnp.mean(values * gain * grad, axis=-1, keepdims=True)
    return scale * gain * grad - values * (scale * scale * scale * inner)


def project_block(x_ref, cos_ref, sin_ref, columns, gain, ht_ref, q_ref, kv_ref):
    heads, _, head_dim = q_ref.shape
    width = heads * head_dim
    x = x_ref[...].astype(jnp.float32)
    normed = (x * inverse_rms(x) * gain).astype(jnp.bfloat16)
    ht_ref[...] = normed.T
    cosine, sine = cos_ref[...], sin_ref[...]

    def turn(u):
        return (u * cosine + pltpu.roll(u, head_dim // 2, 1) * sine).astype(jnp.bfloat16)

    for pair in range(heads // 2):
        both = matmul(normed, columns(2 * pair * head_dim, (2 * pair + 2) * head_dim))
        q_ref[2 * pair] = turn(both[:, :head_dim])
        q_ref[2 * pair + 1] = turn(both[:, head_dim:])
    both = matmul(normed, columns(width, width + 2 * head_dim))
    kv_ref[:, :head_dim] = turn(both[:, :head_dim])
    kv_ref[:, head_dim:] = both[:, head_dim:].astype(jnp.bfloat16)


def gain_rows(columns, start):
    return columns(start, start + 128).astype(jnp.float32).T[:8]


def project_kernel(x_ref, cos_ref, sin_ref, w_ref, ht_ref, q_ref, kv_ref, gains_ref):
    width = x_ref.shape[1]

    def columns(start, end):
        return w_ref[:, start:end]

    gains_ref[...] = gain_rows(columns, width + kv_ref.shape[2])
    project_block(
        x_ref, cos_ref, sin_ref, columns, gains_ref[0:1], ht_ref, q_ref.at[0], kv_ref.at[0]
    )


def project(x, cosine, sine, weights, seqs, heads, head_dim):
    rows, width = x.shape
    block = rows // seqs
    return pl.pallas_call(
        project_kernel,
        grid=(seqs,),
        in_specs=[
            row((block, width), lambda b: (b, 0)),
            row((block, head_dim), lambda b: (b, 0)),
            row((block, head_dim), lambda b: (b, 0)),
            row(weights.shape, lambda b: (0, 0)),
        ],
        out_specs=[
            row((width, block), lambda b: (0, b)),
            row((1, heads, block, head_dim), lambda b: (b, 0, 0, 0)),
            row((1, block, 2 * head_dim), lambda b: (b, 0, 0)),
            row((8, width), lambda b: (0, 0)),
        ],
        out_shape=[
            jax.ShapeDtypeStruct((width, rows), jnp.bfloat16),
            jax.ShapeDtypeStruct((seqs, heads, block, head_dim), jnp.bfloat16),
            jax.ShapeDtypeStruct((seqs, block, 2 * head_dim), jnp.bfloat16),
            jax.ShapeDtypeStruct((8, width), jnp.float32),
        ],
        compiler_params=params(),
        name="project",
    )(x, cosine, sine, weights)


HALF = 128
GROUP = 8


def window_bias(low_ref, first, span):
    place = lax.broadcasted_iota(jnp.int32, (span, HALF), 0)
    local = lax.broadcasted_iota(jnp.int32, (span, HALF), 1)
    low = low_ref[:, first : first + HALF] - first
    allowed = (place >= low) & (place <= local + (span - HALF))
    bias = jnp.where(allowed, 0.0, NEG)
    return jnp.concatenate([bias] * GROUP, axis=1)


def attend_half(scale, half, q_ref, kv_ref, low_ref, o_ref, lse_ref):
    heads, block, head_dim = q_ref.shape
    span = kv_ref.shape[0] - (block - HALF)
    factor = scale * LOG2E
    first = half * HALF
    keys = kv_ref[first : first + span, :head_dim]
    values_t = kv_ref[first : first + span, head_dim:].T
    values_t = jnp.concatenate([values_t, jnp.ones((16, span), values_t.dtype)], axis=0)
    bias = window_bias(low_ref, first, span)

    for base in range(0, heads, GROUP):
        query = q_ref[base : base + GROUP, first : first + HALF].reshape(GROUP * HALF, head_dim)
        score = right_times(keys, query) * factor + bias
        peak = jnp.max(score, axis=0, keepdims=True)
        weights = jnp.exp2(score - peak).astype(jnp.bfloat16)
        both = matmul(values_t, weights)
        total = both[head_dim : head_dim + 8]
        result = (both[:head_dim] / total[0:1]).T.astype(jnp.bfloat16)
        o_ref[base : base + GROUP, first : first + HALF] = result.reshape(GROUP, HALF, head_dim)
        lse_ref[half, base // GROUP] = jnp.log2(total) + peak


def attend_kernel(scale, q_ref, kv_ref, low_ref, o_ref, lse_ref):
    for half in range(q_ref.shape[2] // HALF):
        attend_half(
            scale, half, q_ref.at[0], kv_ref.at[0], low_ref.at[0], o_ref.at[0], lse_ref.at[0]
        )


def attend(query, pairs, low, scale):
    seqs, heads, block, head_dim = query.shape
    span = pairs.shape[1]
    return pl.pallas_call(
        functools.partial(attend_kernel, scale),
        grid=(seqs,),
        in_specs=[
            row((1, heads, block, head_dim), lambda b: (b, 0, 0, 0)),
            row((1, span, 2 * head_dim), lambda b: (b, 0, 0)),
            row((1, 1, block), lambda b: (b, 0, 0)),
        ],
        out_specs=[
            row((1, heads, block, head_dim), lambda b: (b, 0, 0, 0)),
            row(
                (1, block // HALF, heads // GROUP, 8, GROUP * HALF), lambda b: (b, 0, 0, 0, 0)
            ),
        ],
        out_shape=[
            jax.ShapeDtypeStruct(query.shape, jnp.bfloat16),
            jax.ShapeDtypeStruct(
                (seqs, block // HALF, heads // GROUP, 8, GROUP * HALF), jnp.float32
            ),
        ],
        compiler_params=params(),
        name="attend",
    )(query, pairs, low[:, None, :])


def attend_back_half(
    scale, half, q_ref, kv_ref, low_ref, lse_ref, o_ref, do_ref, cos_ref, sin_ref, put_dq, dkv_ref
):
    heads, block, head_dim = q_ref.shape
    span = kv_ref.shape[0] - (block - HALF)
    factor = scale * LOG2E
    lanes = GROUP * HALF
    first = half * HALF
    window = slice(first, first + span)
    keys, values = kv_ref[window, :head_dim], kv_ref[window, head_dim:]
    keys_t = keys.T
    bias = window_bias(low_ref, first, span)
    cosine = cos_ref[first : first + HALF][None]
    sine = sin_ref[first : first + HALF][None]

    for base in range(0, heads, GROUP):
        here = (slice(base, base + GROUP), slice(first, first + HALF))
        query = q_ref[here].reshape(lanes, head_dim)
        grad = do_ref[here].reshape(lanes, head_dim)
        mixed = o_ref[here].reshape(lanes, head_dim)
        product = grad.astype(jnp.float32) * mixed.astype(jnp.float32)
        delta = jnp.sum(product.T, axis=0, keepdims=True)
        lse = lse_ref[half, base // GROUP, 0:1]
        score = right_times(keys, query)
        weights = jnp.exp2((score * factor - lse) + bias)
        low_weights = weights.astype(jnp.bfloat16)
        dkv_ref[window, head_dim:] += matmul(low_weights, grad)
        slope = right_times(values, grad)
        slope = (weights * (slope - delta)).astype(jnp.bfloat16)
        dkv_ref[window, :head_dim] += matmul(slope, query) * scale
        dq = (matmul(keys_t, slope).T * scale).reshape(GROUP, HALF, head_dim)
        turned = pltpu.roll(dq.reshape(lanes, head_dim), head_dim // 2, 1)
        dq = dq * cosine - turned.reshape(GROUP, HALF, head_dim) * sine
        put_dq(base, first, dq.astype(jnp.bfloat16))


def attend_back_kernel(
    scale, q_ref, kv_ref, low_ref, lse_ref, o_ref, do_ref, cos_ref, sin_ref, dq_ref, dkv_ref
):
    dkv_ref[...] = jnp.zeros_like(dkv_ref)

    def put_dq(base, first, dq):
        dq_ref[0, base : base + GROUP, first : first + HALF] = dq

    for half in range(q_ref.shape[2] // HALF):
        attend_back_half(
            scale,
            half,
            q_ref.at[0],
            kv_ref.at[0],
            low_ref.at[0],
            lse_ref.at[0],
            o_ref.at[0],
            do_ref.at[0],
            cos_ref,
            sin_ref,
            put_dq,
            dkv_ref.at[0],
        )


def attend_back(query, pairs, low, lse, mixed, grad, cosine, sine, scale):
    seqs, heads, block, head_dim = query.shape
    span = pairs.shape[1]
    per_head = row((1, heads, block, head_dim), lambda b: (b, 0, 0, 0))
    table = row((block, head_dim), lambda b: (b, 0))
    return pl.pallas_call(
        functools.partial(attend_back_kernel, scale),
        grid=(seqs,),
        in_specs=[
            per_head,
            row((1, span, 2 * head_dim), lambda b: (b, 0, 0)),
            row((1, 1, block), lambda b: (b, 0, 0)),
            row((1,) + lse.shape[1:], lambda b: (b, 0, 0, 0, 0)),
            per_head,
            per_head,
            table,
            table,
        ],
        out_specs=[per_head, row((1, span, 2 * head_dim), lambda b: (b, 0, 0))],
        out_shape=[
            jax.ShapeDtypeStruct(query.shape, jnp.bfloat16),
            jax.ShapeDtypeStruct(pairs.shape, jnp.float32),
        ],
        compiler_params=params(),
        name="attend_back",
    )(query, pairs, low[:, None, :], lse, mixed, grad, cosine, sine)


def gelu_parts(gate):
    cube = 0.044715 * gate * gate
    bend = jnp.tanh(0.7978845608028654 * gate * (1.0 + cube))
    half = 0.5 * (1.0 + bend)
    value = gate * half
    slope = half + gate * (half * (1.0 - bend)) * (0.7978845608028654 * (1.0 + 3.0 * cube))
    return value, slope


def put_parts(refs, chunk, step):
    def put(total):
        for i, ref in enumerate(refs):
            ref[:, chunk * step : (chunk + 1) * step] = total[:, i * step : (i + 1) * step]

    return put


def put_columns(ref, start):
    def put(total):
        ref[:, start : start + total.shape[1]] = total

    return put


def feed_kernel(own, scattered, far, x_ref, o_ref, g_ref, gains_ref, full_ref, *refs):
    pieces, refs = refs[:4], refs[4:]
    y_ref, dx_ref, do_ref, dgain_ref, dout_ref, dff_ref = refs[:6]
    far_ref, refs = refs[6], refs[7:]
    shares, refs = refs[:3], refs[3:]
    outw, ff, mixed, normed, normed_t, g_t, y_acc, dh_acc, m_all, dgate_all, dup_all, grads = refs[
        :12
    ]
    in_sem, out_sem = refs[12:14]
    rows, width = g_ref.shape
    seqs, heads, block, head_dim = o_ref.shape
    step = ff.shape[-1] // 3
    tiles = rows // ROW_TILE
    shard_rows = width // 32
    near = FF_CHUNKS - far
    gain = gains_ref[1:2]
    if far:
        stacked = stack_columns(pieces, refs[-2], refs[-1], range(near, FF_CHUNKS), 0)
        for copy in stacked:
            copy.start()
    if own:
        greet(neighbours())
        count = Scatter.BUFFERS
        buffers = [refs[14 + count * k : 14 + count * (k + 1)] for k in range(scattered)]
        plans = [
            (grads.at[k % 2], None, None, put_parts(shares, k, step)) for k in range(scattered)
        ]
        refs = refs[14 + count * scattered :]
        scatter = Scatter(plans, buffers, refs[0])
        if far:
            wide = 3 * step
            ranges = [
                (refs[3], far_ref, k * wide, k * wide + wide // 2, (k + 1) * wide)
                for k in range(far)
            ]
            gather = Gather(refs[1], refs[2], ranges)
            for copy in stacked:
                copy.wait()

    def run(place):
        if own:
            for kind, number, chunk in FEED_ORDER[place]:
                (gather, scatter)[kind].step(number, chunk)

    def load(chunk):
        source, start = full_ref, width + chunk * 3 * step
        if chunk >= near:
            source, start = far_ref, (chunk - near) * 3 * step
        return pltpu.make_async_copy(
            source.at[:, :, :, :, :, pl.ds(start, 3 * step)], ff.at[chunk % 2], in_sem.at[chunk % 2]
        )

    def weights(slot, index):
        return ff[slot, :, :, :, :, :, index * step : (index + 1) * step].reshape(width, step)

    def store(chunk):
        return pltpu.make_async_copy(
            grads.at[chunk % 2], dff_ref.at[chunk - scattered], out_sem.at[chunk % 2]
        )

    run(0)
    out_load = pltpu.make_async_copy(
        full_ref.at[:, :, :, :, :, pl.ds(0, width)], outw, in_sem.at[2]
    )
    out_load.start()
    load(0).start()
    x_load = pltpu.make_async_copy(x_ref, normed, in_sem.at[3])
    x_load.start()
    x_load.wait()
    out_load.wait()

    def here(tile):
        return pl.ds(pl.multiple_of(tile * ROW_TILE, ROW_TILE), ROW_TILE)

    def prologue(tile):
        part = here(tile)
        attended = jnp.concatenate([o_ref[tile, h] for h in range(heads)], axis=1)
        x1 = normed[part].astype(jnp.float32) + right_times(attended, outw[...].reshape(width, width))
        mixed[part] = x1
        y_acc[part] = x1
        low = (x1 * inverse_rms(x1) * gain).astype(jnp.bfloat16)
        normed[part] = low
        normed_t[:, part] = low.T
        g_t[:, part] = g_ref[part].T
        dh_acc[part] = jnp.zeros((ROW_TILE, width), jnp.float32)

    for tile in range(tiles):
        prologue(tile)
        run(1 + tile)
    at = 1 + tiles
    for chunk in range(FF_CHUNKS):
        slot = chunk % 2
        if chunk >= near:
            load(chunk).start()
        load(chunk).wait()
        if chunk + 1 < near:
            load(chunk + 1).start()

        def forth(tile):
            part = pl.ds(tile * FEED_TILE, FEED_TILE)
            low, grad = normed[part], g_ref[part]
            gate = matmul(low, weights(slot, 0))
            up_part = matmul(low, weights(slot, 1))
            dm = matmul(grad, weights(slot, 2))
            value, slope = gelu_parts(gate)
            m = (value * up_part).astype(jnp.bfloat16)
            dgate = (dm * up_part * slope).astype(jnp.bfloat16)
            dup = (dm * value).astype(jnp.bfloat16)
            m_all[part], dgate_all[part], dup_all[part] = m, dgate, dup
            y_acc[part] += right_times(m, weights(slot, 2))
            dh_acc[part] += right_times(dgate, weights(slot, 0)) + right_times(
                dup, weights(slot, 1)
            )

        def grads_of(tile):
            part = pl.ds(tile * (width // 2), width // 2)
            for i, (left, right) in enumerate(
                ((normed_t, dgate_all), (normed_t, dup_all), (g_t, m_all))
            ):
                value = matmul(left[part], right[...]).astype(jnp.bfloat16)
                grads[slot, tile, :, :, :, :, i * step : (i + 1) * step] = value.reshape(
                    2, 4, 2, shard_rows, step
                )

        for tile in range(2):
            forth(tile)
            run(at + tile)
        if chunk - 2 >= scattered:
            store(chunk - 2).wait()
        for tile in range(2):
            grads_of(tile)
            run(at + 2 + tile)
        at += 4
        if chunk >= scattered:
            store(chunk).start()

    dgain_ref[...] = jnp.zeros_like(dgain_ref)

    @pl.loop(0, tiles)
    def _(tile):
        part = here(tile)
        normed[part] = y_acc[part].astype(jnp.bfloat16)
        x1, dh = mixed[part], dh_acc[part]
        scale = inverse_rms(x1)
        dgain_ref[0:1] += jnp.sum(dh * x1 * scale, axis=0, keepdims=True)
        dx = g_ref[part].astype(jnp.float32) + rms_back(x1, scale, gain, dh)
        mixed[part] = dx
        low = dx.astype(jnp.bfloat16)
        g_t[:, part] = low.T
        back = matmul(low, outw[...].reshape(width, width)).astype(jnp.bfloat16)
        for h in range(heads):
            do_ref[tile, h] = back[:, h * head_dim : (h + 1) * head_dim]

    outs = [
        pltpu.make_async_copy(normed, y_ref, in_sem.at[0]),
        pltpu.make_async_copy(mixed, dx_ref, in_sem.at[1]),
    ]
    for out in outs:
        out.start()
    run(at)

    @pl.loop(0, width // ROW_TILE)
    def _(tile):
        part = here(tile)
        for h in range(0, heads, 2):
            for s in range(seqs):
                pair = jnp.concatenate([o_ref[s, h], o_ref[s, h + 1]], axis=1)
                term = matmul(g_t[part, s * block : (s + 1) * block], pair)
                total = term if s == 0 else total + term
            lanes = slice(h * head_dim, (h + 2) * head_dim)
            ff[0, tile // 2, lax.rem(tile, 2), :, :, :, lanes] = total.astype(
                jnp.bfloat16
            ).reshape(4, 2, shard_rows, 2 * head_dim)

    outs.append(
        pltpu.make_async_copy(
            ff.at[0, :, :, :, :, :, pl.ds(0, width)], dout_ref, in_sem.at[2]
        )
    )
    outs[-1].start()
    run(at + 1)
    for chunk in range(max(scattered, FF_CHUNKS - 2), FF_CHUNKS):
        store(chunk).wait()
    for out in outs:
        out.wait()


def feed(own, scattered, far, x, mixed_heads, grad, gains, full, pieces):
    rows, width = x.shape
    step = pieces[1].shape[1] // FF_CHUNKS
    low = jnp.bfloat16
    chunk = (2, 2, 4, 2, width // 32, 3 * step)
    kept = FF_CHUNKS - scattered
    options = {"collective_id": 3, "has_side_effects": True} if own else {}
    return pl.pallas_call(
        functools.partial(feed_kernel, own, scattered, far),
        in_specs=[hbm(), vmem(), vmem(), vmem()] + [hbm()] * 5,
        out_specs=[hbm(), hbm(), vmem(), vmem(), hbm(), hbm(), hbm()] + [vmem()] * 3,
        out_shape=[
            jax.ShapeDtypeStruct((rows, width), low),
            jax.ShapeDtypeStruct((rows, width), jnp.float32),
            jax.ShapeDtypeStruct(mixed_heads.shape, low),
            jax.ShapeDtypeStruct((8, width), jnp.float32),
            jax.ShapeDtypeStruct(chunk[:-1] + (width,), low),
            jax.ShapeDtypeStruct((kept,) + chunk, low),
            jax.ShapeDtypeStruct(chunk[:-1] + (max(1, far) * 3 * step,), low),
        ]
        + [jax.ShapeDtypeStruct((width // 32, max(1, scattered) * step), jnp.float32)] * 3,
        scratch_shapes=[
            pltpu.VMEM(chunk[:-1] + (width,), low),
            pltpu.VMEM((2,) + chunk, low),
            pltpu.VMEM((rows, width), jnp.float32),
            pltpu.VMEM((rows, width), low),
            pltpu.VMEM((width, rows), low),
            pltpu.VMEM((width, rows), low),
            pltpu.VMEM((rows, width), jnp.float32),
            pltpu.VMEM((rows, width), jnp.float32),
            pltpu.VMEM((rows, step), low),
            pltpu.VMEM((rows, step), low),
            pltpu.VMEM((rows, step), low),
            pltpu.VMEM((2,) + chunk, low),
            pltpu.SemaphoreType.DMA((4,)),
            pltpu.SemaphoreType.DMA((2,)),
        ]
        + (Scatter.scratch([3 * step] * scattered, width // 32) if own else [])
        + (Gather.scratch(far) if far else [])
        + (
            [
                pltpu.VMEM((width // 32, far * 3 * step), low),
                pltpu.SemaphoreType.DMA((3 * far,)),
            ]
            if far
            else []
        ),
        compiler_params=params(**options),
        name="feed",
    )(x, mixed_heads, grad, gains, full, *pieces)


def finish_rows(x, dx, grad, w_ref, gain):
    dh = right_times(grad, w_ref[:, : grad.shape[1]])
    x = x.astype(jnp.float32)
    scale = inverse_rms(x)
    total = (dx + rms_back(x, scale, gain, dh)).astype(jnp.bfloat16)
    return total, jnp.sum(dh * x * scale, axis=0, keepdims=True)


def finish_kernel(
    x_ref, ht_ref, dq_ref, dkv_ref, gains_ref, dx_ref, w_ref, dw_ref, dxo_ref, dgain_ref, dall
):
    width = x_ref.shape[1]
    seqs, heads, block, _ = dq_ref.shape
    dgain_ref[...] = jnp.zeros_like(dgain_ref)

    @pl.loop(0, seqs)
    def _(tile):
        part = pl.ds(pl.multiple_of(tile * block, block), block)
        grad = jnp.concatenate([dq_ref[tile, h] for h in range(heads)] + [dkv_ref[tile]], axis=1)
        dall[part] = grad
        dxo_ref[part], terms = finish_rows(
            x_ref[part], dx_ref[part], grad, w_ref, gains_ref[0:1]
        )
        dgain_ref[0:1] += terms

    @pl.loop(0, width // ROW_TILE)
    def _(tile):
        part = pl.ds(pl.multiple_of(tile * ROW_TILE, ROW_TILE), ROW_TILE)
        dw_ref[part] = matmul(ht_ref[part], dall[...]).astype(jnp.bfloat16)


def finish(x, normed_t, dq, dkv, gains, dx, weights):
    rows, width = x.shape
    columns = width + dkv.shape[2]
    return pl.pallas_call(
        finish_kernel,
        in_specs=[vmem()] * 7,
        out_specs=[vmem()] * 3,
        out_shape=[
            jax.ShapeDtypeStruct((width, columns), jnp.bfloat16),
            jax.ShapeDtypeStruct((rows, width), jnp.bfloat16),
            jax.ShapeDtypeStruct((8, width), jnp.float32),
        ],
        scratch_shapes=[pltpu.VMEM((rows, columns), jnp.bfloat16)],
        compiler_params=params(),
        name="finish",
    )(x, normed_t, dq, dkv, gains, dx, weights)


def segment_partners():
    x, c, z, y = place()
    partners = [device(x, c, z, 1 - y)]
    for hop in (1, 2, 3):
        partners += [device(x, c, lax.rem(z + hop, 4), there) for there in (y, 1 - y)]
    return partners


def place_rows(all_ref, frequencies, cos_ref, sin_ref, low_ref):
    _, _, z, y = place()
    _, seqs, block = all_ref.shape
    offset = (z * 2 + y) * block
    place_of = lax.broadcasted_iota(jnp.int32, (block, 1), 0) + offset
    lanes = lax.broadcasted_iota(jnp.int32, (block, cos_ref.shape[1]), 1)
    for seq in range(seqs):
        mine = all_ref[z * 2 + y, seq : seq + 1].astype(jnp.float32)
        mine = jnp.broadcast_to(mine, (128, block)).T[:, 0:1].astype(jnp.int32)
        smaller = jnp.zeros((block, block), jnp.float32)
        for other in range(all_ref.shape[0]):
            smaller += jnp.where(all_ref[other, seq : seq + 1] < mine, 1.0, 0.0)
        starts = jnp.sum(smaller, axis=1, keepdims=True).astype(jnp.int32)
        angle = (place_of - starts).astype(jnp.float32) * frequencies
        rows = slice(seq * block, (seq + 1) * block)
        cos_ref[rows] = jnp.cos(angle)
        sine = jnp.sin(angle)
        sin_ref[rows] = jnp.where(lanes < cos_ref.shape[1] // 2, -sine, sine)
        low = jnp.maximum(starts, place_of - (WINDOW - 1)) - (offset - 4 * block)
        low = jnp.broadcast_to(low.astype(jnp.float32), lanes.shape)
        low_ref[seq] = low.T[0:1].astype(jnp.int32)


def stack_columns(pieces, target, sems, chunks, start):
    out, *parts = pieces
    copies = []
    if start:
        copies.append(pltpu.make_async_copy(out, target.at[:, pl.ds(0, start)], sems.at[0]))
    step = parts[0].shape[1] // FF_CHUNKS
    for chunk in chunks:
        for part in parts:
            source = part.at[:, pl.ds(chunk * step, step)]
            there = target.at[:, pl.ds(start, step)]
            copies.append(pltpu.make_async_copy(source, there, sems.at[len(copies)]))
            start += step
    return copies


def front_kernel(
    scale,
    ranges,
    ranges_ff,
    x_ref,
    frequency_ref,
    segments_ref,
    first_ref,
    *refs,
):
    pieces, refs = refs[:4], refs[4:]
    (
        ht_ref,
        q_ref,
        pairs_ref,
        gains_ref,
        o_ref,
        lse_ref,
        cos_ref,
        sin_ref,
        low_ref,
        full_ref,
        w_ref,
        window,
        w_all,
        all_segments,
        sems,
        local_sems,
        window_sems,
        out_sems,
        segment_sems,
        stack,
        stack_sems,
    ) = refs
    seqs, heads, block, head_dim = q_ref.shape
    width = heads * head_dim
    reach = window.shape[1] - block
    window[:, :reach] = jnp.zeros((seqs, reach, 2 * head_dim), window.dtype)
    stacked = stack_columns(pieces, stack, stack_sems, ranges_ff, width)
    for copy in stacked:
        copy.start()
    partners = segment_partners()
    x, c, z, y = place()
    greet(partners + [device(1 - x, c, z, y), device(x, 1 - c, z, y)])
    mine = all_segments.at[z * 2 + y]
    keep = pltpu.make_async_copy(segments_ref, mine, segment_sems.at[2, 0])
    keep.start()
    copies = [
        remote(segments_ref, mine, segment_sems.at[0, i], segment_sems.at[1, i], partner)
        for i, partner in enumerate(partners)
    ]
    for copy in copies:
        copy.start()
    refs = ((first_ref, w_all), (stack, full_ref))
    gather = Gather(sems, local_sems, [refs[i] + tuple(rest) for i, *rest in ranges])
    windows = Windows(window, window_sems, block)

    def run(place, first=0, last=None):
        for kind, number, index in FRONT_ORDER[place][first:last]:
            if kind == 0:
                gather.step(number, index)
            else:
                (windows.once, windows.twice, windows.all)[number](index)

    def columns(start, end):
        return w_all[:, :, :, :, :, start:end].reshape(width, end - start)

    ahead = [item[1] for item in FRONT_ORDER[0]].index(1)
    for copy in stacked:
        copy.wait()
    run(0, 0, ahead)
    keep.wait()
    for copy in copies:
        copy.wait()
    place_rows(all_segments, frequency_ref[0:1], cos_ref, sin_ref, low_ref)
    run(0, ahead)
    gains_ref[...] = gain_rows(columns, width + 2 * head_dim)

    @pl.loop(0, seqs)
    def _(seq):
        part = pl.ds(pl.multiple_of(seq * block, block), block)
        project_block(
            x_ref.at[part],
            cos_ref.at[part],
            sin_ref.at[part],
            columns,
            gains_ref[0:1],
            ht_ref.at[:, part],
            q_ref.at[seq],
            window.at[seq, pl.ds(reach, block)],
        )
        windows.own(seq)
        for index in range(seqs - 1):
            if FRONT_ORDER[1 + index]:
                pl.when(seq == index)(lambda: run(1 + index))

    run(seqs)
    halves = block // HALF

    @pl.loop(0, seqs)
    def _(seq):
        for half in range(halves):
            attend_half(
                scale,
                half,
                q_ref.at[seq],
                window.at[seq],
                low_ref.at[seq],
                o_ref.at[seq],
                lse_ref.at[seq],
            )
            for index in range(seqs):
                number = seqs + 1 + index * halves + half
                if FRONT_ORDER[number] and number < seqs * (1 + halves):
                    pl.when(seq == index)(lambda: run(number))

    outs = [
        pltpu.make_async_copy(window, pairs_ref, out_sems.at[0]),
        pltpu.make_async_copy(w_all, w_ref, out_sems.at[1]),
    ]
    for out in outs:
        out.start()
    run(seqs * (1 + halves))

    @pl.loop(0, seqs)
    def _(seq):
        windows.drain(seq)

    for out in outs:
        out.wait()


def front(x, segments, first, pieces, scale, ranges, near, heads, head_dim):
    rows, width = x.shape
    seqs, block = segments.shape
    shard_rows, hidden = pieces[1].shape
    columns = width + near * 3 * hidden // FF_CHUNKS
    half = head_dim // 2
    inverse = 10000.0 ** (-2.0 * jnp.arange(half, dtype=jnp.float32) / head_dim)
    frequencies = jnp.broadcast_to(jnp.concatenate([inverse, inverse]), (8, head_dim))
    low_type = jnp.bfloat16
    span = 5 * block
    lse = (seqs, block // HALF, heads // GROUP, 8, GROUP * HALF)
    stacked = (2, 2, 4, 2, shard_rows)
    return pl.pallas_call(
        functools.partial(front_kernel, scale, ranges, range(near)),
        in_specs=[vmem()] * 2 + [hbm()] * 6,
        out_specs=[vmem(), vmem(), hbm()] + [vmem()] * 6 + [hbm(), hbm()],
        out_shape=[
            jax.ShapeDtypeStruct((width, rows), low_type),
            jax.ShapeDtypeStruct((seqs, heads, block, head_dim), low_type),
            jax.ShapeDtypeStruct((seqs, span, 2 * head_dim), low_type),
            jax.ShapeDtypeStruct((8, width), jnp.float32),
            jax.ShapeDtypeStruct((seqs, heads, block, head_dim), low_type),
            jax.ShapeDtypeStruct(lse, jnp.float32),
            jax.ShapeDtypeStruct((rows, head_dim), jnp.float32),
            jax.ShapeDtypeStruct((rows, head_dim), jnp.float32),
            jax.ShapeDtypeStruct((seqs, 1, block), jnp.int32),
            jax.ShapeDtypeStruct(stacked + (columns,), low_type),
            jax.ShapeDtypeStruct(stacked + (first.shape[1],), low_type),
        ],
        scratch_shapes=[
            pltpu.VMEM((seqs, span, 2 * head_dim), low_type),
            pltpu.VMEM(stacked + (first.shape[1],), low_type),
            pltpu.VMEM((8, seqs, block), jnp.int32),
        ]
        + Gather.scratch(len(ranges))
        + [
            pltpu.SemaphoreType.DMA((2, Windows.KINDS, seqs)),
            pltpu.SemaphoreType.DMA((2,)),
            pltpu.SemaphoreType.DMA((3, 7)),
            pltpu.VMEM((shard_rows, columns), low_type),
            pltpu.SemaphoreType.DMA((1 + 3 * near,)),
        ],
        compiler_params=params(collective_id=2, has_side_effects=True),
        name="front",
    )(x, frequencies, segments, first, *pieces)


class WindowGrads:
    def __init__(self, windows, grads, out, came, sems, block):
        self.windows, self.grads, self.out, self.came = windows, grads, out, came
        self.sems, self.block = sems, block

    def rows(self, seq, distance):
        start = (4 - distance) * self.block
        if not isinstance(distance, int):
            start = pl.multiple_of(start, self.block)
        return self.grads.at[seq, pl.ds(start, self.block)]

    def copy(self, kind, seq):
        x, c, z, y = place()
        over = device(x, c, z, 1 - y)
        partner = device(x, c, lax.rem(z + 3, 4), y) if kind < 2 else over
        return remote(
            self.out.at[kind, seq],
            self.came.at[kind, seq],
            self.sems.at[0, kind, seq],
            self.sems.at[1, kind, seq],
            partner,
        )

    def start(self, kind, seq, distance):
        @pl.when(self.windows.gets(kind))
        def _():
            self.out[kind, seq] = self.rows(seq, distance)[...].astype(jnp.bfloat16)
            self.copy(kind, seq).start()

    def add(self, kind, seq, distance):
        @pl.when(self.windows.sends(kind))
        def _():
            self.copy(kind, seq).wait_recv()
            target = self.rows(seq, distance)
            target[...] += self.came[kind, seq].astype(jnp.float32)

    def step(self, number, seq):
        _, _, _, y = place()
        if number == 0:
            self.start(4, seq, 3)
            self.start(3, seq, 1 + 2 * y)
            self.start(2, seq, 1)
        elif number == 1:
            self.add(4, seq, 4)
            self.start(1, seq, 4)
            self.add(3, seq, 2)
        elif number == 2:
            self.add(1, seq, 2)
            self.start(0, seq, 2)
        else:
            self.add(0, seq, 0)
            self.add(2, seq, 0)

    def drain(self, seq):
        for kind in range(Windows.KINDS):
            pl.when(self.windows.gets(kind))(lambda: self.copy(kind, seq).wait_send())


def back_kernel(scale, kept, last_chunks, *refs):
    (
        q_ref,
        pairs_ref,
        low_ref,
        lse_ref,
        o_ref,
        do_ref,
        cos_ref,
        sin_ref,
        x_ref,
        ht_ref,
        gains_ref,
        dgain_ref,
        w_ref,
        dx_ref,
        dout_ref,
        dff_ref,
    ) = refs[:16]
    dxo_ref, refs = refs[16], refs[17:]
    total = kept + 1 + len(last_chunks)
    shares, refs = refs[:8], refs[8:]
    grads, out, came, dall, dx, dgains, dw, load_sems, dx_sems, grad_sems = refs[:10]
    mines, refs = refs[10 : 11 + kept], refs[11 + kept :]
    count = Scatter.BUFFERS
    buffers = [refs[count * k : count * (k + 1)] for k in range(total)]
    sems = refs[count * total]
    seqs, heads, block, head_dim = q_ref.shape
    width = heads * head_dim

    grads[...] = jnp.zeros_like(grads)
    dgains[...] = jnp.zeros_like(dgains)
    dgains[1:2] = dgain_ref[0:1]
    greet(neighbours())
    sources = [dff_ref.at[k] for k in range(kept)] + [dout_ref]
    step = dff_ref.shape[-1] // 3
    plans = [
        (source, mines[i], load_sems.at[i], put_parts(shares[:3], i, step))
        for i, source in enumerate(sources[:kept])
    ]
    plans.append((dout_ref, mines[kept], load_sems.at[kept], put_columns(shares[3], 0)))

    def put_last(result):
        shares[5][...] = result[:, :head_dim]
        shares[6][...] = result[:, head_dim : 2 * head_dim]
        shares[7][...] = result[:, 2 * head_dim :]

    for start, end in last_chunks:
        source = dw.at[:, :, :, :, :, pl.ds(start, end - start)]
        put = put_columns(shares[4], start) if end <= width else put_last
        plans.append((source, None, None, put))
    scatter = Scatter(plans, buffers, sems)
    windows = Windows(None, None, block)
    back = WindowGrads(windows, grads, out, came, grad_sems, block)
    halves = block // HALF

    def load(seq):
        return pltpu.make_async_copy(
            dx_ref.at[pl.ds(seq * block, block)], dx.at[seq % 2], dx_sems.at[seq % 2]
        )

    load(0).start()
    load(1).start()

    def finish_one(seq):
        part = pl.ds(seq * block, block)
        own = grads[seq, 4 * block :]
        key, value = own[:, :head_dim], own[:, head_dim:]
        turned = pltpu.roll(key, head_dim // 2, 1)
        key = key * cos_ref[part] - turned * sin_ref[part]
        dall[part, width : width + head_dim] = key.astype(jnp.bfloat16)
        dall[part, width + head_dim :] = value.astype(jnp.bfloat16)
        load(seq).wait()
        dxo_ref[part], terms = finish_rows(
            x_ref[part], dx[seq % 2], dall[part], w_ref, gains_ref[0:1]
        )
        dgains[0:1] += terms
        if seq + 2 < seqs:
            load(seq + 2).start()

    def weight_grads(start, end):
        @pl.loop(0, 2)
        def _(tile):
            part = pl.ds(pl.multiple_of(tile * (width // 2), width // 2), width // 2)
            value = matmul(ht_ref[part], dall[:, start:end]).astype(jnp.bfloat16)
            dw[tile, :, :, :, :, start:end] = value.reshape(
                (2,) + dw.shape[2:5] + (end - start,)
            )

    def weight_tail():
        weight_grads(width, width + 2 * head_dim)
        gains = dgains[...].T.astype(jnp.bfloat16)
        dw[:, :, :, :, :, width + 2 * head_dim :] = gains.reshape(
            dw.shape[:5] + (gains.shape[1],)
        )

    def run(place):
        for kind, number, index in BACK_ORDER[place]:
            if kind == 0:
                scatter.step(number, index)
            elif kind == 1:
                back.step(number, index)
            elif kind == 2:
                weight_grads(0, width)
            elif kind == 3:
                finish_one(number)
            else:
                weight_tail()

    run(0)

    @pl.loop(0, seqs)
    def _(seq):
        part = pl.ds(pl.multiple_of(seq * block, block), block)

        def put_dq(base, first, dq):
            there = pl.ds(pl.multiple_of(seq * block + first, HALF), HALF)
            for h in range(GROUP):
                dall[there, (base + h) * head_dim : (base + h + 1) * head_dim] = dq[h]

        for half in range(halves):
            attend_back_half(
                scale,
                half,
                q_ref.at[seq],
                pairs_ref.at[seq],
                low_ref.at[seq],
                lse_ref.at[seq],
                o_ref.at[seq],
                do_ref.at[seq],
                cos_ref.at[part],
                sin_ref.at[part],
                put_dq,
                grads.at[seq],
            )
            for index in range(seqs):
                number = 1 + index * halves + half
                if BACK_ORDER[number] and number < seqs * halves:
                    pl.when(seq == index)(lambda: run(number))

    run(seqs * halves)

    @pl.loop(0, seqs)
    def _(seq):
        back.drain(seq)


def back(
    query, pairs, low, lse, mixed, grad, cosine, sine, x, normed_t, gains, dgain, weights, dx, dout, dff, scale
):
    seqs, heads, block, head_dim = query.shape
    rows, width = x.shape
    columns = weights.shape[1]
    kept = dff.shape[0]
    shard_rows = dff.shape[-2]
    low_type = jnp.bfloat16
    span = pairs.shape[1]
    last_chunks = ((0, width // 2), (width // 2, width), (width, columns))
    widths = [dff.shape[-1]] * kept + [width] + [end - start for start, end in last_chunks]
    lanes = 2 * head_dim
    results = [kept * dff.shape[-1] // 3] * 3 + [width, width, head_dim, head_dim]
    results.append(columns - width - lanes)
    return pl.pallas_call(
        functools.partial(back_kernel, scale, kept, last_chunks),
        in_specs=[vmem()] * 13 + [hbm()] * 3,
        out_specs=[vmem()] * 9,
        out_shape=[jax.ShapeDtypeStruct((rows, width), low_type)]
        + [jax.ShapeDtypeStruct((shard_rows, n), jnp.float32) for n in results],
        scratch_shapes=[
            pltpu.VMEM((seqs, span, lanes), jnp.float32),
            pltpu.VMEM((Windows.KINDS, seqs, block, lanes), low_type),
            pltpu.VMEM((Windows.KINDS, seqs, block, lanes), low_type),
            pltpu.VMEM((rows, width + lanes), low_type),
            pltpu.VMEM((2, block, width), jnp.float32),
            pltpu.VMEM((128, width), jnp.float32),
            pltpu.VMEM((2, 2, 4, 2, shard_rows, columns), low_type),
            pltpu.SemaphoreType.DMA((kept + 1,)),
            pltpu.SemaphoreType.DMA((2,)),
            pltpu.SemaphoreType.DMA((2, Windows.KINDS, seqs)),
        ]
        + [pltpu.VMEM((2, 4, 2, shard_rows, n), low_type) for n in widths[: kept + 1]]
        + Scatter.scratch(widths, shard_rows, 2 / 3),
        compiler_params=params(collective_id=4, has_side_effects=True),
        name="back",
    )(
        query,
        pairs,
        low,
        lse,
        mixed,
        grad,
        cosine,
        sine,
        x,
        normed_t,
        gains,
        dgain,
        weights,
        dx,
        dout,
        dff,
    )


def stack_ff(gate, up_part, down_t, chunks):
    step = gate.shape[1] // FF_CHUNKS
    return [
        part[:, chunk * step : (chunk + 1) * step]
        for chunk in chunks
        for part in (gate, up_part, down_t)
    ]


def unstack_ff(stacked):
    rows, hidden = stacked.shape[0], stacked.shape[1] // 3
    parts = stacked.reshape(rows, FF_CHUNKS, 3, hidden // FF_CHUNKS)
    return [parts[:, :, i].reshape(rows, hidden) for i in range(3)]


def shifted(value, axis, steps):
    count = lax.axis_size(axis)
    initial, last = (max(0, -steps), min(count, count - steps))
    return lax.ppermute(value, axis, [(source, source + steps) for source in range(initial, last)])


def on_device(
    own_links,
    tokens,
    segments,
    cotangent,
    first_gain,
    query_weight,
    key_weight,
    value_weight,
    out_weight,
    second_gain,
    gate_weight,
    up_weight,
    down_weight,
):
    seqs, block_len, width = tokens.shape
    head_dim = key_weight.shape[1]
    heads = query_weight.shape[1] // head_dim
    hidden = gate_weight.shape[1]
    shard_rows = first_gain.shape[0]
    reach = (WINDOW - 1 + block_len - 1) // block_len
    scale = head_dim ** (-0.5)
    rows = seqs * block_len
    keys_from = width + 2 * head_dim
    inputs = tokens.reshape(rows, width)
    grad_rows = cotangent.reshape(rows, width)

    gains = jnp.zeros((shard_rows, 128), first_gain.dtype)
    gains = gains.at[:, 0].set(first_gain).at[:, 1].set(second_gain)
    shard = jnp.concatenate([query_weight, key_weight, value_weight, gains], axis=1)
    out_t, down_t = out_weight.T, down_weight.T

    pieces = (out_t, gate_weight, up_weight, down_t)

    if own_links:
        near_count = FF_CHUNKS - FAR
        half = 3 * hidden // FF_CHUNKS // 2
        ranges = [(0, 0, 256, 512), (0, 512, 768, width), (0, width, width + 256, keys_from + 128)]
        ranges += [(1, start, start + 384, start + 512) for start in range(0, width, 512)]
        for start in range(width, width + near_count * 2 * half, half):
            ranges.append((1, start, start + 2 * half // 3, start + half))
        normed_t, query, pairs, gains, mixed, lse, cosine, sine, low, full, weights = front(
            inputs, segments, shard, pieces, scale, ranges, near_count, heads, head_dim
        )
        weights = weights.reshape(width, -1)
        scattered, far = SCATTERED, FAR
    else:
        weights = lax.all_gather(shard, ("batch", "seq"), axis=0, tiled=True)
        parts = stack_ff(gate_weight, up_weight, down_t, range(FF_CHUNKS))
        rest = jnp.concatenate([out_t] + parts, axis=1)
        full = lax.all_gather(rest, ("batch", "seq"), axis=0, tiled=True)
        earlier = lax.all_gather(segments, "seq", axis=1, tiled=True)
        starts = jnp.sum(earlier[:, None, :] < segments[:, :, None], axis=-1, dtype=jnp.int32)
        query_place = jnp.arange(block_len, dtype=jnp.int32) + lax.axis_index("seq") * block_len
        low = jnp.maximum(starts, query_place[None, :] - (WINDOW - 1))
        low = low - (query_place[0] - reach * block_len)
        cosine, sine = tables((query_place[None, :] - starts).reshape(-1), head_dim)
        normed_t, query, own_pairs, gains = project(
            inputs, cosine, sine, weights, seqs, heads, head_dim
        )
        passed = [shifted(own_pairs, "seq", distance) for distance in range(reach, 0, -1)]
        pairs = jnp.concatenate(passed + [own_pairs], axis=1)
        mixed, lse = attend(query, pairs, low, scale)
        scattered, far = 0, 0
        full = full.reshape(2, 2, 4, 2, width // 32, -1)
    output, grad_mixed, grad_heads, dgain_two, grad_out_t, grad_ff, _, *shares = feed(
        own_links, scattered, far, inputs, mixed, grad_rows, gains, full, pieces
    )
    if own_links:
        grad_input, *more, share_out, share_query, share_key, share_value, share_gains = back(
            query,
            pairs,
            low,
            lse,
            mixed,
            grad_heads,
            cosine,
            sine,
            inputs,
            normed_t,
            gains,
            dgain_two,
            weights,
            grad_mixed,
            grad_out_t,
            grad_ff,
            scale,
        )
        share_gate, share_up, share_down_t = [
            jnp.concatenate(pair, axis=1) for pair in zip(shares, more)
        ]
    else:
        grad_query, grad_pairs = attend_back(
            query, pairs, low, lse, mixed, grad_heads, cosine, sine, scale
        )
        own_grad = grad_pairs[:, reach * block_len :]
        for distance in range(1, reach + 1):
            start = (reach - distance) * block_len
            piece = grad_pairs[:, start : start + block_len].astype(jnp.bfloat16)
            own_grad = own_grad + shifted(piece, "seq", -distance).astype(own_grad.dtype)
        grad_key = own_grad[..., :head_dim].reshape(rows, head_dim)
        grad_key = grad_key * cosine - jnp.roll(grad_key, head_dim // 2, axis=1) * sine
        grad_kv = jnp.concatenate(
            [grad_key.reshape(seqs, block_len, head_dim), own_grad[..., head_dim:]], axis=-1
        ).astype(jnp.bfloat16)
        grad_qkv_w, grad_input, dgain_one = finish(
            inputs, normed_t, grad_query, grad_kv, gains, grad_mixed, weights
        )
        grad_gains = jnp.zeros((width, 128), jnp.bfloat16)
        grad_gains = grad_gains.at[:, 0].set(dgain_one[0].astype(jnp.bfloat16))
        grad_gains = grad_gains.at[:, 1].set(dgain_two[0].astype(jnp.bfloat16))
        grad_ff = grad_ff.reshape(FF_CHUNKS, width, -1)
        grad_out_t = grad_out_t.reshape(width, -1)
        grads = jnp.concatenate([grad_qkv_w, grad_gains, grad_out_t] + list(grad_ff), axis=1)
        grads = grads.astype(jnp.float32)
        share = lax.psum_scatter(grads, ("batch", "seq"), scatter_dimension=0, tiled=True)
        share_query, share_key = share[:, :width], share[:, width : width + head_dim]
        share_value = share[:, width + head_dim : keys_from]
        share_gains = share[:, keys_from : keys_from + 128]
        share_out = share[:, keys_from + 128 : keys_from + 128 + width]
        share_gate, share_up, share_down_t = unstack_ff(share[:, keys_from + 128 + width :])
    return (
        output.reshape(tokens.shape),
        grad_input.reshape(tokens.shape),
        share_gains[:, 0],
        share_query,
        share_key,
        share_value,
        share_out.T,
        share_gains[:, 1],
        share_gate,
        share_up,
        share_down_t.T,
    )


def solution(mesh):
    both = ("batch", "seq")
    rows_split, columns_split = P(both, None), P(None, both)
    tokens_split, gain_split = P("batch", "seq", None), P(both)
    weights = (
        gain_split,
        rows_split,
        rows_split,
        rows_split,
        columns_split,
        gain_split,
        rows_split,
        rows_split,
        columns_split,
    )
    in_specs = (tokens_split, P("batch", "seq"), tokens_split) + weights
    out_specs = (tokens_split, tokens_split) + weights
    own_links = (mesh.shape["batch"], mesh.shape["seq"]) == (4, 8)
    return jax.shard_map(
        functools.partial(on_device, own_links),
        mesh=mesh,
        in_specs=in_specs,
        out_specs=out_specs,
        check_vma=False,
    )
```
